32 devices in a mesh: dp: 16 (over z, x, core), tensor: 2 (over y).
Axes of the slice: x: 2, y: 2, z: 4, core: 2. Of those that a mesh axis runs over, the one named last changes fastest.
Arguments:
- tokens: bfloat16 [32768, 768], P('dp'), may hold values from -6 to 6
- cotangent: bfloat16 [32768, 768], P('dp'), may hold values from -6 to 6
- buckets: int32 [64], P('dp'), may hold values from 0 to 1, as said below
- lengths: int32 [64, 4], P('dp'), may hold values from 0 to 512, as said below
- qkv_weight: bfloat16 [2, 3, 768, 768], P(None, None, 'dp', 'tensor'), may hold values from -0.3125 to 0.3125
- qv_bias: float32 [2, 2, 768], P(None, None, 'tensor'), may hold values from -1.5 to 1.5
- out_weight: bfloat16 [2, 768, 768], P(None, 'dp', 'tensor'), may hold values from -0.875 to 0.875
- ffn_in_weight: bfloat16 [2, 768, 3072], P(None, 'dp', 'tensor'), may hold values from -0.21875 to 0.21875
- ffn_in_bias: float32 [2, 3072], P(None, 'tensor'), may hold values from -1.5 to 1.5
- ffn_out_weight: bfloat16 [2, 768, 3072], P(None, 'dp', 'tensor'), may hold values from -0.109375 to 0.109375
- out_bias: float32 [2, 2, 768], replicated, may hold values from -1.5 to 1.5
- norm_gain: float32 [2, 2, 768], replicated, may hold values from 0.5 to 1.5
- norm_bias: float32 [2, 2, 768], replicated, may hold values from -1.5 to 1.5
Outputs:
- layer_one: bfloat16 [32768, 768], P('dp')
- layer_two: bfloat16 [32768, 768], P('dp')
- token_grad: float32 [32768, 768], P('dp')
- qkv_grad: float32 [2, 3, 768, 768], P(None, None, 'dp', 'tensor')
- qv_bias_grad: float32 [2, 2, 768], P(None, None, 'tensor')
- out_weight_grad: float32 [2, 768, 768], P(None, 'dp', 'tensor')
- ffn_in_weight_grad: float32 [2, 768, 3072], P(None, 'dp', 'tensor')
- ffn_in_bias_grad: float32 [2, 3072], P(None, 'tensor')
- ffn_out_weight_grad: float32 [2, 768, 3072], P(None, 'dp', 'tensor')
- out_bias_grad: float32 [2, 2, 768], replicated
- norm_gain_grad: float32 [2, 2, 768], replicated
- norm_bias_grad: float32 [2, 2, 768], replicated
The draws below stay inside these ranges and needn't reach their ends.
Inputs may be any that keep to these rules, and one draw needn't show every extreme that they name: `buckets`: 0 marks a slab of four sequences of 128 slots, 1 a slab of one sequence of 512 slots; some slab of every draw has bucket 1. `lengths`: for a slab of bucket 0, each of the four entries is its sequence's live length, from 32 to 128. For bucket 1, the first entry is the live length, from 128 to 512, and the other three are 0. Some slab of bucket 1 has length 512.
All inputs are finite; a program needn't handle non-finite values.
Results may differ from the reference program's by a relative error of at most 0.038.
Values may be sent and summed in bfloat16 or wider, within the bound.
No kernel may reach another device: no remote copies, remote signals or barrier semaphores. Data moves between devices by JAX's collectives and lax.ppermute only.
A program may use at most 256 MiB of HBM per device.

```python
import math
import jax
import jax.numpy as jnp
from jax import lax

D = 768
HEADS = 12
HEAD_DIM = 64
FF = 3072
LAYERS = 2
SHORT = 128
SLAB = 512
SLABS_MB = 2
MB = 2
TOKENS = 32768
N_DP = 16


def slab_layout(key):
    slab_count = MB * SLABS_MB * N_DP
    keys_list = jax.random.split(key, 4)
    positions = jnp.arange(slab_count, dtype=jnp.int32)
    chosen = jax.random.randint(keys_list[0], (), 0, slab_count)
    buckets = jax.random.randint(keys_list[1], (slab_count,), 0, 2)
    buckets = jnp.where(positions == chosen, 1, buckets)
    short_lengths = jax.random.randint(keys_list[2], (slab_count, 4), SHORT // 4, SHORT + 1)
    long_lengths = jax.random.randint(keys_list[3], (slab_count,), SLAB // 4, SLAB + 1)
    long_lengths = jnp.where(positions == chosen, SLAB, long_lengths)
    long_rows = jnp.where(jnp.arange(4, dtype=jnp.int32)[None, :] == 0, long_lengths[:, None], 0)
    lengths = jnp.where(buckets[:, None] == 0, short_lengths, long_rows)
    return (buckets.astype(jnp.int32), lengths.astype(jnp.int32))


def draw_buckets(key, part):
    return slab_layout(key)[0]


def draw_lengths(key, part):
    return slab_layout(key)[1]


def spiked(result, stream_key, source, target, parts, factor):
    def block_of(axis_at):
        return (jnp.arange(result.shape[axis_at]) // (result.shape[axis_at] // parts)).reshape((-1,) + (1,) * (result.ndim - 1 - axis_at))

    near = jax.random.permutation(stream_key, parts)[block_of(target)]
    other_side = (block_of(target) + parts // 2) % parts
    return jnp.where((block_of(source) == near) | (block_of(source) == other_side), factor * result, result)


def steps_of(stream_key, dims, cuts, least, top_value):
    level, own = 1.0, jax.random.fold_in(stream_key, 6)
    for position, blocks in cuts:
        heights = jnp.exp(jax.random.uniform(jax.random.fold_in(own, position), (blocks,), jnp.float32, least / len(cuts), top_value / len(cuts)))
        level = level * jnp.repeat(heights, dims[position] // blocks).reshape([-1 if axis == position else 1 for axis in range(len(dims))])
    return level


def normal_values(stream_key, shape, spread, bound, cuts=(), held_as=jnp.bfloat16):
    array = jax.random.normal(stream_key, shape, jnp.float32) * spread
    if len(cuts) > 0:
        array = steps_of(stream_key, shape, cuts, -0.22, 0.18) * array
    return jnp.clip(array, min=-bound, max=bound).astype(held_as)


def bell_draw_with(stream_key, dims, scale, most, cuts, heavy, kind=jnp.bfloat16):
    values = scale * jax.random.normal(stream_key, dims, jnp.float32)
    if cuts:
        values = values * steps_of(stream_key, dims, cuts, -0.22, 0.18)
    return jnp.clip(spiked(values, jax.random.fold_in(stream_key, 3), *heavy), -most, most).astype(kind)


def setup_inputs(seed: int = 0) -> dict:
    splits = jax.random.split(jax.random.key(seed), 14)
    return {
        "tokens": bell_draw_with(splits[0], (TOKENS, D), 1.0, 6.0, ((0, 16),), (0, 1, 16, 2.0)),
        "cotangent": normal_values(splits[1], (TOKENS, D), 1.0, 6.0, ((0, 16),)),
        "buckets": draw_buckets(jax.random.fold_in(splits[13], 71), 0),
        "lengths": draw_lengths(jax.random.fold_in(splits[13], 71), 0),
        "qkv_weight": normal_values(splits[4], (LAYERS, 3, D, D), (D // 2) ** -0.5, 0.3125, ((2, 16), (3, 2))),
        "qv_bias": normal_values(splits[5], (LAYERS, 2, D), 0.3, 1.5, ((2, 2),), jnp.float32),
        "out_weight": normal_values(splits[6], (LAYERS, D, D), (D // 16) ** -0.5, 0.875, ((1, 16), (2, 2))),
        "ffn_in_weight": normal_values(splits[7], (LAYERS, D, FF), D ** -0.5, 0.21875, ((1, 16), (2, 2))),
        "ffn_in_bias": normal_values(splits[8], (LAYERS, FF), 0.3, 1.5, ((1, 2),), jnp.float32),
        "ffn_out_weight": normal_values(splits[9], (LAYERS, D, FF), FF ** -0.5, 0.109375, ((1, 16), (2, 2))),
        "out_bias": normal_values(splits[10], (LAYERS, 2, D), 0.3, 1.5, (), jnp.float32),
        "norm_gain": jnp.clip(1.0 + 0.1 * jax.random.normal(splits[11], (LAYERS, 2, D), jnp.float32), 0.5, 1.5),
        "norm_bias": normal_values(splits[12], (LAYERS, 2, D), 0.3, 1.5, (), jnp.float32),
    }


@jax.custom_vjp
def low(v):
    return lax.optimization_barrier(v.astype(jnp.bfloat16)).astype(jnp.float32)

@jax.custom_vjp
def low_back(v):
    return v

def low_keep(v):
    return (low(v), None)

def low_pass(kept, grad):
    return (grad,)

def back_keep(v):
    return (v, None)

def back_low(kept, grad):
    return (low(grad),)
low.defvjp(low_keep, low_pass)
low_back.defvjp(back_keep, back_low)
norm_eps = 1e-06
big_negative = -1e+30
root_half = 0.7071067811865476

def matmul(left, right):
    return jnp.dot(left, right, precision=lax.Precision.HIGHEST, preferred_element_type=jnp.float32)

def layer_norm(residual, norm_gain, norm_shift):
    centered = residual - lax.optimization_barrier(jnp.mean(residual, axis=-1, keepdims=True))
    inv_spread = lax.rsqrt(lax.optimization_barrier(jnp.mean(centered * centered, axis=-1, keepdims=True)) + norm_eps)
    return centered * inv_spread * norm_gain + norm_shift

def gelu_value(inputs):
    return 0.5 * inputs * (1.0 + lax.erf(inputs * root_half))

def slab_mask(bucket, slab_lengths):
    segment_width = jnp.where(bucket == 0, SHORT, SLAB).astype(jnp.int32)
    positions = jnp.arange(SLAB, dtype=jnp.int32)
    segment = positions // segment_width
    offset = positions - segment * segment_width
    segment_length = slab_lengths[segment]
    return (segment[:, None] == segment[None, :]) & (offset[None, :] < segment_length[None, :])

def slab_attention(query_rows, key_rows, value_rows, bucket, slab_lengths):
    visible = slab_mask(bucket, slab_lengths)
    raw_scores = low_back(jnp.einsum('qhe,khe->hqk', query_rows, key_rows, precision=lax.Precision.HIGHEST))
    scores = jnp.where(visible[None], raw_scores * HEAD_DIM ** (-0.5), big_negative)
    shifted = jnp.exp(scores - lax.optimization_barrier(jnp.max(scores, axis=-1, keepdims=True)))
    probs = low(shifted / lax.optimization_barrier(jnp.sum(shifted, axis=-1, keepdims=True)))
    return jnp.einsum('hqk,khe->qhe', probs, value_rows, precision=lax.Precision.HIGHEST)

def slab_entry(packed):
    return jax.checkpoint(slab_attention)(packed[0], packed[1], packed[2], packed[3], packed[4])

def one_layer(current, weights, buckets, lengths):
    qkv_weight, qv_bias, out_weight, ffn_in_weight, ffn_in_bias, ffn_out_weight, out_bias, norm_gain, norm_bias = weights
    row_count = current.shape[0]
    slab_count = row_count // SLAB
    query_rows = low_back(low(matmul(current, qkv_weight[0]) + qv_bias[0]))
    key_rows = low_back(low(matmul(current, qkv_weight[1])))
    value_rows = low_back(low(matmul(current, qkv_weight[2]) + qv_bias[1]))
    shape_slabs = (slab_count, SLAB, HEADS, HEAD_DIM)
    mixed = lax.map(slab_entry, (query_rows.reshape(shape_slabs), key_rows.reshape(shape_slabs), value_rows.reshape(shape_slabs), buckets, lengths))
    mixed = low_back(low(mixed.reshape(row_count, D)))
    attention_out = low_back(matmul(mixed, out_weight.T) + out_bias[0])
    hidden = low(layer_norm(current + attention_out, norm_gain[0], norm_bias[0]))
    pre_gelu = low_back(matmul(hidden, ffn_in_weight) + ffn_in_bias)
    activated = low(gelu_value(pre_gelu))
    ffn_out = low_back(matmul(activated, ffn_out_weight.T) + out_bias[1])
    return low(layer_norm(hidden + ffn_out, norm_gain[1], norm_bias[1]))

def encoder(weights, rows, buckets, lengths):
    current = rows
    outputs = []
    for layer_index in range(LAYERS):
        layer_weights = tuple((member[layer_index] for member in weights))
        current = one_layer(current, layer_weights, buckets, lengths)
        outputs.append(current)
    return (outputs[0], outputs[LAYERS - 1])

def reference(tokens, cotangent, buckets, lengths, qkv_weight, qv_bias, out_weight, ffn_in_weight, ffn_in_bias, ffn_out_weight, out_bias, norm_gain, norm_bias):
    params = tuple((member.astype(jnp.float32) for member in (qkv_weight, qv_bias, out_weight, ffn_in_weight, ffn_in_bias, ffn_out_weight, out_bias, norm_gain, norm_bias)))
    slab_count = buckets.shape[0]
    group_slabs = math.gcd(slab_count, 8)
    group_count = slab_count // group_slabs
    input_groups = tokens.astype(jnp.float32).reshape(group_count, group_slabs * SLAB, D)
    cotangent_groups = cotangent.astype(jnp.float32).reshape(group_count, group_slabs * SLAB, D)
    bucket_groups = buckets.reshape(group_count, group_slabs)
    length_groups = lengths.reshape(group_count, group_slabs, 4)

    def step(totals, packed):
        inputs, cotangent_rows, bucket_rows, length_rows = packed

        def forward(weights, rows):
            return encoder(weights, rows, bucket_rows, length_rows)
        outputs, pullback = jax.vjp(forward, params, inputs)
        weight_grads, input_grads = pullback((jnp.zeros_like(outputs[0]), cotangent_rows))
        totals = jax.tree.map(jnp.add, totals, weight_grads)
        return (totals, (outputs[0], outputs[1], input_grads))
    initial = jax.tree.map(jnp.zeros_like, params)
    totals, (first_out, second_out, input_grads) = lax.scan(step, initial, (input_groups, cotangent_groups, bucket_groups, length_groups))
    return (first_out.reshape(TOKENS, D).astype(jnp.bfloat16), second_out.reshape(TOKENS, D).astype(jnp.bfloat16), input_grads.reshape(TOKENS, D), totals[0], totals[1], totals[2], totals[3], totals[4], totals[5], totals[6], totals[7], totals[8])
```

```python
import jax
import jax.numpy as jnp
from jax import lax
from jax.sharding import PartitionSpec as P

HEAD_DIM = 64


norm_eps = 1e-06
big_negative = -1e30
root_half = 0.7071067811865476
inv_root_tau = 0.3989422804014327


def layer_norm(residual, norm_gain, norm_shift):
    centered = residual - jnp.mean(residual, axis=-1, keepdims=True)
    inv_spread = lax.rsqrt(jnp.mean(centered * centered, axis=-1, keepdims=True) + norm_eps)
    normed = centered * inv_spread
    return (normed * norm_gain + norm_shift, normed, inv_spread)


def norm_back(gradient, normed, inv_spread, norm_gain):
    scaled = gradient * norm_gain
    inner = jnp.mean(scaled * normed, axis=-1, keepdims=True)
    return inv_spread * (scaled - jnp.mean(scaled, axis=-1, keepdims=True) - normed * inner)


def gelu_value(inputs):
    return 0.5 * inputs * (1.0 + lax.erf(inputs * root_half))


def gelu_slope(inputs):
    return 0.5 * (1.0 + lax.erf(inputs * root_half)) + inputs * inv_root_tau * jnp.exp(
        -0.5 * inputs * inputs
    )


def slab_mask(bucket, slab_lengths, row_count):
    segment_width = jnp.where(bucket == 0, row_count // 4, row_count).astype(jnp.int32)
    positions = jnp.arange(row_count, dtype=jnp.int32)
    segment = positions // segment_width
    offset = positions - segment * segment_width
    choices_four = jnp.arange(4, dtype=jnp.int32)
    segment_length = jnp.sum(
        jnp.where(segment[:, None] == choices_four[None, :], slab_lengths[None, :], 0), axis=1
    )
    return (segment[:, None] == segment[None, :]) & (offset[None, :] < segment_length[None, :])


def attend(query_rows, key_rows, value_rows, visible):
    score_scale = query_rows.shape[-1] ** (-0.5)
    raw_scores = jnp.einsum(
        "gqhe,gkhe->ghqk", query_rows, key_rows, preferred_element_type=jnp.float32
    )
    scores = jnp.where(visible[:, None], raw_scores * score_scale, big_negative)
    row_max = jnp.max(scores, axis=-1, keepdims=True)
    row_total = jnp.sum(jnp.exp(scores - row_max), axis=-1, keepdims=True)
    logsum = row_max + jnp.log(row_total)
    probs_low = jnp.exp(scores - logsum).astype(jnp.bfloat16)
    mixed = jnp.einsum("ghqk,gkhe->gqhe", probs_low, value_rows, preferred_element_type=jnp.float32)
    return (mixed.astype(jnp.bfloat16), logsum[..., 0])


def attend_back(query_rows, key_rows, value_rows, visible, logsum, mixed_grad):
    score_scale = query_rows.shape[-1] ** (-0.5)
    raw_scores = jnp.einsum(
        "gqhe,gkhe->ghqk", query_rows, key_rows, preferred_element_type=jnp.float32
    )
    scores = jnp.where(visible[:, None], raw_scores * score_scale, big_negative)
    probs = jnp.exp(scores - logsum[..., None])
    probs_grad = jnp.einsum(
        "gqhe,gkhe->ghqk", mixed_grad, value_rows, preferred_element_type=jnp.float32
    )
    row_delta = jnp.sum(probs * probs_grad, axis=-1, keepdims=True)
    raw_grad = (probs * (probs_grad - row_delta) * score_scale).astype(jnp.bfloat16)
    query_grad = jnp.einsum(
        "ghqk,gkhe->gqhe", raw_grad, key_rows, preferred_element_type=jnp.float32
    )
    key_grad = jnp.einsum(
        "ghqk,gqhe->gkhe", raw_grad, query_rows, preferred_element_type=jnp.float32
    )
    value_grad = jnp.einsum(
        "ghqk,gqhe->gkhe",
        probs.astype(jnp.bfloat16),
        mixed_grad,
        preferred_element_type=jnp.float32,
    )
    return (
        query_grad.astype(jnp.bfloat16),
        key_grad.astype(jnp.bfloat16),
        value_grad.astype(jnp.bfloat16),
    )


def to_groups(tensor, group_count):
    row_count, head_count, head_size = tensor.shape
    return tensor.reshape(group_count, row_count // group_count, head_count, head_size)


def from_groups(tensor):
    return tensor.reshape(-1, tensor.shape[2], tensor.shape[3])


def grouped_forward(query_rows, key_rows, value_rows, visible):
    group_count = visible.shape[0]
    mixed, logsum = attend(
        to_groups(query_rows, group_count),
        to_groups(key_rows, group_count),
        to_groups(value_rows, group_count),
        visible,
    )
    return (from_groups(mixed), jnp.transpose(logsum, (1, 0, 2)).reshape(logsum.shape[1], -1))


def grouped_backward(query_rows, key_rows, value_rows, visible, logsum, mixed_grad):
    group_count = visible.shape[0]
    head_count, row_count = logsum.shape
    grouped_lse = jnp.transpose(
        logsum.reshape(head_count, group_count, row_count // group_count), (1, 0, 2)
    )
    gradients = attend_back(
        to_groups(query_rows, group_count),
        to_groups(key_rows, group_count),
        to_groups(value_rows, group_count),
        visible,
        grouped_lse,
        to_groups(mixed_grad, group_count),
    )
    return tuple((from_groups(member) for member in gradients))


def slab_forward(query_rows, key_rows, value_rows, bucket, slab_lengths):
    row_count = query_rows.shape[0]
    visible = slab_mask(bucket, slab_lengths, row_count)[None]
    return grouped_forward(query_rows, key_rows, value_rows, visible)


def slab_backward(query_rows, key_rows, value_rows, bucket, slab_lengths, logsum, mixed_grad):
    row_count = query_rows.shape[0]
    visible = slab_mask(bucket, slab_lengths, row_count)[None]
    return grouped_backward(query_rows, key_rows, value_rows, visible, logsum, mixed_grad)


def micro_forward(query_rows, key_rows, value_rows, bucket_rows, length_rows):
    slab_count = bucket_rows.shape[0]
    slab_rows = query_rows.shape[0] // slab_count
    mixed_parts = []
    logsum_parts = []
    for slab_index in range(slab_count):
        start = slab_index * slab_rows
        finish = start + slab_rows
        mixed, logsum = slab_forward(
            query_rows[start:finish],
            key_rows[start:finish],
            value_rows[start:finish],
            bucket_rows[slab_index],
            length_rows[slab_index],
        )
        mixed_parts.append(mixed)
        logsum_parts.append(logsum)
    return (jnp.concatenate(mixed_parts, axis=0), jnp.concatenate(logsum_parts, axis=1))


def micro_backward(query_rows, key_rows, value_rows, bucket_rows, length_rows, logsum, mixed_grad):
    slab_count = bucket_rows.shape[0]
    slab_rows = query_rows.shape[0] // slab_count
    query_parts = []
    key_parts = []
    value_parts = []
    for slab_index in range(slab_count):
        start = slab_index * slab_rows
        finish = start + slab_rows
        query_grad, key_grad, value_grad = slab_backward(
            query_rows[start:finish],
            key_rows[start:finish],
            value_rows[start:finish],
            bucket_rows[slab_index],
            length_rows[slab_index],
            logsum[:, start:finish],
            mixed_grad[start:finish],
        )
        query_parts.append(query_grad)
        key_parts.append(key_grad)
        value_parts.append(value_grad)
    return (
        jnp.concatenate(query_parts, axis=0),
        jnp.concatenate(key_parts, axis=0),
        jnp.concatenate(value_parts, axis=0),
    )


AXES = ("tensor", "dp")


def pack_shard(qkv_weight, out_weight, ffn_in_weight, ffn_out_weight):
    rows = out_weight.shape[0]
    qkv_flat = jnp.transpose(qkv_weight, (1, 0, 2)).reshape(rows, -1)
    return jnp.concatenate([qkv_flat, out_weight], axis=1), jnp.concatenate(
        [ffn_in_weight, ffn_out_weight], axis=1
    )


def whole_weights(shards, split):
    attention_shard, ffn_shard = shards
    attention_all = lax.all_gather(attention_shard, AXES, tiled=True)
    ffn_all = lax.all_gather(ffn_shard, AXES, tiled=True)
    model_width = attention_all.shape[0] // split
    attention_all = attention_all.reshape(split, model_width, 4, -1)
    ffn_all = ffn_all.reshape(split, model_width, 2, -1)
    attention_all = jnp.transpose(attention_all, (2, 1, 0, 3)).reshape(4, model_width, -1)
    ffn_all = jnp.transpose(ffn_all, (2, 1, 0, 3)).reshape(2, model_width, -1)
    return attention_all[:3], attention_all[3], ffn_all[0], ffn_all[1]


def scatter_gradient(terms, split):
    count, model_width, columns = terms.shape
    packed = jnp.transpose(
        terms.astype(jnp.bfloat16).reshape(count, model_width, split, -1), (2, 1, 0, 3)
    ).reshape(split * model_width, -1)
    mine = lax.psum_scatter(packed, AXES, scatter_dimension=0, tiled=True)
    return jnp.transpose(mine.astype(jnp.float32).reshape(-1, count, columns // split), (1, 0, 2))


def layer_forward(inputs, whole, smalls, bucket_rows, length_rows):
    qkv_whole, out_whole, in_whole, down_whole = whole
    query_bias, ffn_bias, branch_bias, norm_gain, norm_shift = smalls
    row_count = inputs.shape[0]
    head_count = qkv_whole.shape[2] // HEAD_DIM
    projected = jnp.einsum("sd,cde->cse", inputs, qkv_whole, preferred_element_type=jnp.float32)
    query_rows = (
        (projected[0] + query_bias[0]).astype(jnp.bfloat16).reshape(row_count, head_count, HEAD_DIM)
    )
    key_rows = projected[1].astype(jnp.bfloat16).reshape(row_count, head_count, HEAD_DIM)
    value_rows = (
        (projected[2] + query_bias[1]).astype(jnp.bfloat16).reshape(row_count, head_count, HEAD_DIM)
    )
    mixed, logsum = micro_forward(query_rows, key_rows, value_rows, bucket_rows, length_rows)
    mixed = mixed.reshape(row_count, -1)
    attention_out = (
        jnp.einsum("se,de->sd", mixed, out_whole, preferred_element_type=jnp.float32)
        + branch_bias[0]
    )
    hidden, normed_one, spread_one = layer_norm(
        inputs.astype(jnp.float32) + attention_out, norm_gain[0], norm_shift[0]
    )
    hidden_low = hidden.astype(jnp.bfloat16)
    pre_gelu = jnp.dot(hidden_low, in_whole, preferred_element_type=jnp.float32) + ffn_bias
    activated = gelu_value(pre_gelu).astype(jnp.bfloat16)
    ffn_out = (
        jnp.einsum("sf,df->sd", activated, down_whole, preferred_element_type=jnp.float32)
        + branch_bias[1]
    )
    result, normed_two, spread_two = layer_norm(
        hidden_low.astype(jnp.float32) + ffn_out, norm_gain[1], norm_shift[1]
    )
    kept = (
        inputs,
        query_rows,
        key_rows,
        value_rows,
        logsum,
        mixed,
        normed_one,
        spread_one,
        hidden_low,
        pre_gelu,
        normed_two,
        spread_two,
    )
    return (result.astype(jnp.bfloat16), kept)


def layer_backward(gradient, kept, whole, smalls, bucket_rows, length_rows):
    qkv_whole, out_whole, in_whole, down_whole = whole
    query_bias, ffn_bias, branch_bias, norm_gain, norm_shift = smalls
    (
        inputs,
        query_rows,
        key_rows,
        value_rows,
        logsum,
        mixed,
        normed_one,
        spread_one,
        hidden_low,
        pre_gelu,
        normed_two,
        spread_two,
    ) = kept
    row_count = inputs.shape[0]
    head_count = query_rows.shape[1]
    gain_two = jnp.sum(gradient * normed_two, axis=0)
    shift_two = jnp.sum(gradient, axis=0)
    resid_two_grad = norm_back(gradient, normed_two, spread_two, norm_gain[1])
    branch_grad = resid_two_grad.astype(jnp.bfloat16)
    bias_two = jnp.sum(branch_grad.astype(jnp.float32), axis=0)
    activated = gelu_value(pre_gelu).astype(jnp.bfloat16)
    down_term = jnp.einsum("sd,sf->df", branch_grad, activated, preferred_element_type=jnp.float32)
    activated_grad = jnp.dot(branch_grad, down_whole, preferred_element_type=jnp.float32)
    pre_grad = (activated_grad * gelu_slope(pre_gelu)).astype(jnp.bfloat16)
    ffn_bias_term = jnp.sum(pre_grad.astype(jnp.float32), axis=0)
    in_term = jnp.einsum("sd,sf->df", hidden_low, pre_grad, preferred_element_type=jnp.float32)
    hidden_part = jnp.einsum("sf,df->sd", pre_grad, in_whole, preferred_element_type=jnp.float32)
    hidden_grad = hidden_part + resid_two_grad
    gain_one = jnp.sum(hidden_grad * normed_one, axis=0)
    shift_one = jnp.sum(hidden_grad, axis=0)
    resid_one_grad = norm_back(hidden_grad, normed_one, spread_one, norm_gain[0])
    attention_grad = resid_one_grad.astype(jnp.bfloat16)
    bias_one = jnp.sum(attention_grad.astype(jnp.float32), axis=0)
    out_term = jnp.einsum("sd,se->de", attention_grad, mixed, preferred_element_type=jnp.float32)
    mixed_grad = (
        jnp.dot(attention_grad, out_whole, preferred_element_type=jnp.float32)
        .astype(jnp.bfloat16)
        .reshape(row_count, head_count, HEAD_DIM)
    )
    query_grad, key_grad, value_grad = micro_backward(
        query_rows, key_rows, value_rows, bucket_rows, length_rows, logsum, mixed_grad
    )
    stacked = jnp.stack([query_grad, key_grad, value_grad]).reshape(3, row_count, -1)
    qkv_term = jnp.einsum("sd,cse->cde", inputs, stacked, preferred_element_type=jnp.float32)
    query_bias_term = jnp.stack(
        [
            jnp.sum(stacked[0].astype(jnp.float32), axis=0),
            jnp.sum(stacked[2].astype(jnp.float32), axis=0),
        ]
    )
    input_part = jnp.einsum("cse,cde->sd", stacked, qkv_whole, preferred_element_type=jnp.float32)
    input_grad = input_part + resid_one_grad
    matrix_terms = (qkv_term, out_term, in_term, down_term)
    small_terms = (
        query_bias_term,
        ffn_bias_term,
        jnp.stack([bias_one, bias_two]),
        jnp.stack([gain_one, gain_two]),
        jnp.stack([shift_one, shift_two]),
    )
    return (input_grad, matrix_terms, small_terms)


def on_device(
    tokens,
    cotangent,
    buckets,
    lengths,
    qkv_weight,
    qv_bias,
    out_weight,
    ffn_in_weight,
    ffn_in_bias,
    ffn_out_weight,
    out_bias,
    norm_gain,
    norm_bias,
):
    split = lax.axis_size("tensor")
    place = lax.axis_index("tensor")
    rows = tokens.shape[0] // split
    slabs = buckets.shape[0] // split
    layer_count = qkv_weight.shape[0]
    current = lax.dynamic_slice_in_dim(tokens, place * rows, rows)
    gradient = lax.dynamic_slice_in_dim(cotangent, place * rows, rows).astype(jnp.float32)
    bucket_rows = lax.dynamic_slice_in_dim(buckets, place * slabs, slabs)
    length_rows = lax.dynamic_slice_in_dim(lengths, place * slabs, slabs)
    qv_whole = lax.all_gather(qv_bias, "tensor", axis=2, tiled=True)
    ffn_bias_whole = lax.all_gather(ffn_in_bias, "tensor", axis=1, tiled=True)
    smalls_all = (qv_whole, ffn_bias_whole, out_bias, norm_gain, norm_bias)
    whole_layers = [
        whole_weights(
            pack_shard(qkv_weight[index], out_weight[index], ffn_in_weight[index], ffn_out_weight[index]),
            split,
        )
        for index in range(layer_count)
    ]
    kept_layers = []
    results = []
    for layer_index in range(layer_count):
        smalls = tuple((member[layer_index] for member in smalls_all))
        current, kept = layer_forward(
            current, whole_layers[layer_index], smalls, bucket_rows, length_rows
        )
        kept_layers.append(kept)
        results.append(lax.all_gather(current, "tensor", axis=0, tiled=True))
    matrix_sums = [None] * layer_count
    small_sums = [None] * layer_count
    for layer_index in reversed(range(layer_count)):
        smalls = tuple((member[layer_index] for member in smalls_all))
        gradient, (qkv_term, out_term, in_term, down_term), small_sums[layer_index] = layer_backward(
            gradient, kept_layers[layer_index], whole_layers[layer_index], smalls, bucket_rows, length_rows
        )
        ffn_mine = scatter_gradient(jnp.stack([in_term, down_term]), split)
        attention_mine = scatter_gradient(
            jnp.concatenate([qkv_term, out_term[None]], axis=0), split
        )
        matrix_sums[layer_index] = (attention_mine[:3], attention_mine[3], ffn_mine[0], ffn_mine[1])
    input_grads = lax.all_gather(gradient.astype(jnp.bfloat16), "tensor", axis=0, tiled=True)
    query_total, ffn_total, branch_total, gain_total, shift_total = lax.psum(
        tuple((jnp.stack(group) for group in zip(*small_sums))), AXES
    )
    qv_columns = qv_bias.shape[2]
    ffn_columns = ffn_in_bias.shape[1]
    return (
        results[0],
        results[layer_count - 1],
        input_grads.astype(jnp.float32),
        jnp.stack([member[0] for member in matrix_sums]),
        lax.dynamic_slice_in_dim(query_total, place * qv_columns, qv_columns, axis=2),
        jnp.stack([member[1] for member in matrix_sums]),
        jnp.stack([member[2] for member in matrix_sums]),
        lax.dynamic_slice_in_dim(ffn_total, place * ffn_columns, ffn_columns, axis=1),
        jnp.stack([member[3] for member in matrix_sums]),
        branch_total,
        gain_total,
        shift_total,
    )


def solution(mesh):
    placed = (
        P("dp", None),
        P("dp", None),
        P("dp"),
        P("dp", None),
        P(None, None, "dp", "tensor"),
        P(None, None, "tensor"),
        P(None, "dp", "tensor"),
        P(None, "dp", "tensor"),
        P(None, "tensor"),
        P(None, "dp", "tensor"),
        P(),
        P(),
        P(),
    )
    return jax.shard_map(
        on_device,
        mesh=mesh,
        in_specs=placed,
        out_specs=(
            P("dp", None),
            P("dp", None),
            P("dp", None),
            P(None, None, "dp", "tensor"),
            P(None, None, "tensor"),
            P(None, "dp", "tensor"),
            P(None, "dp", "tensor"),
            P(None, "tensor"),
            P(None, "dp", "tensor"),
            P(),
            P(),
            P(),
        ),
        check_vma=False,
    )
```

```python
import functools

import jax
import jax.numpy as jnp
from jax import lax
from jax.experimental import pallas as pl
from jax.experimental.pallas import tpu as pltpu
from jax.sharding import PartitionSpec as P

HEAD_DIM = 64
PAIR = 2 * HEAD_DIM
AXES = ("tensor", "dp")
CORE = ("dp", 1)
FFN_PARTS = 3
ROW_TILE = 256
TILE_ROWS = 16
PLANNED_BLOCKS = 16
VMEM_LIMIT = 58 * 1024 * 1024

norm_eps = 1e-06
big_negative = -1e30
inv_root_tau = 0.3989422804014327
log2_e = 1.4426950408889634
score_scale = HEAD_DIM ** (-0.5)
exponent_scale = score_scale * log2_e
erf_slope = 0.3275911 * 0.7071067811865476
erf_terms = (1.061405429, -1.453152027, 1.421413741, -0.284496736, 0.254829592)


def dot_nn(left, right):
    return lax.dot_general(
        left, right, (((1,), (0,)), ((), ())), preferred_element_type=jnp.float32
    )


def dot_nt(left, right):
    return lax.dot_general(
        left, right, (((1,), (1,)), ((), ())), preferred_element_type=jnp.float32
    )


def flipped(member):
    return member.astype(jnp.float32).T


def hop_orders(block_count):
    bits = []
    bit = block_count // 2
    while bit > 1:
        bits.append(("dp", bit))
        bit //= 2
    return (bits + [("tensor", 1)], bits[:-1] + [("tensor", 1), bits[-1]])


def slot_table(order):
    table = []
    for slot in range(2 ** len(order)):
        dp_part, tensor_part = 0, 0
        for position, (axis, bit) in enumerate(order):
            if slot >> position & 1:
                if axis == "dp":
                    dp_part ^= bit
                else:
                    tensor_part ^= bit
        table.append((dp_part, tensor_part))
    return table


def hop(member, dim):
    axis, bit = dim
    pairs = [(place, place ^ bit) for place in range(lax.axis_size(axis))]
    return lax.ppermute(member, axis, pairs)


def gather_piece(shard, order):
    current = shard[None]
    for dim in order[:-1]:
        current = jnp.concatenate([current, hop(current, dim)], axis=0)
    later = hop(current, order[-1])
    return (current, later, hop(current, CORE), hop(later, CORE))


def scatter_piece(keep, send, order):
    parts = [keep, hop(send, CORE)]
    for dim in reversed(order):
        half = parts[0].shape[0] // 2
        upper = sum(part[half:].astype(jnp.float32) for part in parts).astype(jnp.bfloat16)
        parts = [part[:half] for part in parts] + [hop(upper, dim)]
    return sum(part[0].astype(jnp.float32) for part in parts)


def gather_whole(shard, order):
    whole = lax.all_gather(shard, AXES, tiled=True)
    columns = shard.shape[1]
    split = lax.axis_size("tensor")
    blocks = whole.reshape(split, PLANNED_BLOCKS, -1, columns)
    half = 2 ** (len(order) - 1)
    table = slot_table(order)
    return tuple(
        jnp.stack(
            [blocks[tensor_part, dp_part ^ core] for dp_part, tensor_part in table[part * half :][:half]]
        )
        for core in range(2)
        for part in range(2)
    )


def scatter_whole(keep, send, order):
    split = lax.axis_size("tensor")
    placed = {}
    for slot, (dp_part, tensor_part) in enumerate(slot_table(order)):
        placed[tensor_part, dp_part] = keep[slot]
        placed[tensor_part, dp_part ^ 1] = send[slot]
    whole = jnp.stack(
        [placed[half, block] for half in range(split) for block in range(PLANNED_BLOCKS)]
    )
    whole = whole.reshape(-1, keep.shape[2])
    return lax.psum_scatter(whole, AXES, scatter_dimension=0, tiled=True).astype(jnp.float32)


def load_blocks(meta, sources, order, target, columns, source_columns, sems):
    table = slot_table(order)
    half = len(table) // 2
    block_rows = sources[0].shape[1]
    for slot, (dp_part, tensor_part) in enumerate(table):
        for core in range(2):
            source = sources[2 * core + slot // half]
            place = meta[0] ^ (dp_part ^ core)
            half_at = meta[1] ^ tensor_part
            rows = pl.ds(pl.multiple_of(place * block_rows, TILE_ROWS), block_rows)
            pltpu.make_async_copy(
                source.at[slot % half, :, source_columns],
                target.at[half_at, rows, columns],
                sems.at[half_at],
            ).start()


def await_blocks(target, half_at, columns, sems):
    view = target.at[half_at, :, columns]
    pltpu.make_async_copy(view, view, sems.at[half_at]).wait()


def store_blocks(meta, source, targets, order, relative_half, columns, sem):
    block_rows = targets[0].shape[1]
    tensor_weight = 2 ** order.index(("tensor", 1))
    for slot, (dp_part, tensor_part) in enumerate(slot_table(order)):
        if tensor_part:
            continue
        for core in range(2):
            place = meta[0] ^ (dp_part ^ core)
            rows = pl.ds(pl.multiple_of(place * block_rows, TILE_ROWS), block_rows)
            pltpu.make_async_copy(
                source.at[rows, :],
                targets[core].at[slot + tensor_weight * relative_half, :, columns],
                sem,
            ).start()


def await_stored(source, sem):
    pltpu.make_async_copy(source, source, sem).wait()


def norm_stats(residual):
    centered = residual - jnp.mean(residual, axis=-1, keepdims=True)
    inv_spread = lax.rsqrt(jnp.mean(centered * centered, axis=-1, keepdims=True) + norm_eps)
    return centered * inv_spread, inv_spread


def norm_back(gradient, normed, inv_spread, gain):
    scaled = gradient * gain
    inner = jnp.mean(scaled * normed, axis=-1, keepdims=True)
    return inv_spread * (scaled - jnp.mean(scaled, axis=-1, keepdims=True) - normed * inner)


def row_tiles(row_count):
    tile = min(ROW_TILE, row_count)
    return [slice(start, start + tile) for start in range(0, row_count, tile)]


def column_sum(member):
    return jnp.sum(member, axis=0, keepdims=True)


def gelu_parts(inputs):
    bell = jnp.exp(-0.5 * inputs * inputs)
    ratio = 1.0 / (1.0 + erf_slope * jnp.abs(inputs))
    series = 0.5 * erf_terms[0]
    for term in erf_terms[1:]:
        series = series * ratio + 0.5 * term
    tail = series * ratio * bell
    below = jnp.where(inputs < 0, tail, 1.0 - tail)
    return inputs * below, below + inputs * (bell * inv_root_tau)


def qkv_forward_kernel(orders, meta, inputs, bias, *refs):
    qk_sources, vo_sources, out, weights, qk_sems, v_sems = (
        refs[0:4], refs[4:8], refs[8], refs[9], refs[10], refs[11],
    )
    step = pl.program_id(0)
    columns = out.shape[2]

    @pl.when(step == 0)
    def _():
        load_blocks(
            meta, qk_sources, orders[0], weights, slice(0, 2 * columns), slice(None), qk_sems
        )
        load_blocks(
            meta, vo_sources, orders[1], weights, slice(2 * columns, 3 * columns),
            slice(0, columns), v_sems,
        )

    half_at = meta[1] ^ (step // 3)

    @pl.when(step % 3 == 0)
    def _():
        await_blocks(weights, half_at, slice(0, 2 * columns), qk_sems)
        await_blocks(weights, half_at, slice(2 * columns, 3 * columns), v_sems)

    which = pl.ds(pl.multiple_of((step % 3) * columns, 128), columns)
    for rows in row_tiles(inputs.shape[0]):
        out[0, rows, :] = (dot_nn(inputs[rows, :], weights[half_at, :, which]) + bias[0]).astype(
            jnp.bfloat16
        )


def slab_features(meta, slab, slab_rows, k_side, q_side):
    segment_rows = slab_rows // 4
    row = lax.broadcasted_iota(jnp.int32, (slab_rows, PAIR), 0)
    lane = lax.broadcasted_iota(jnp.int32, (slab_rows, PAIR), 1) & (HEAD_DIM - 1)
    short = meta[2 + slab] == 0
    segment = jnp.where(short, row // segment_rows, 0)
    offset = row - segment * segment_rows
    base = 2 + meta_slabs(meta) + 4 * slab
    length = jnp.where(
        segment == 0,
        meta[base],
        jnp.where(segment == 1, meta[base + 1], jnp.where(segment == 2, meta[base + 2], meta[base + 3])),
    )
    same = segment == lane
    k_value = jnp.where(lane < 4, jnp.where(same, 1.0, 0.0), jnp.where(offset >= length, 1.0, 0.0))
    q_value = jnp.where(lane < 4, jnp.where(same, 0.0, big_negative), big_negative)
    k_side[slab] = jnp.where(lane < 5, k_value, 0.0).astype(jnp.bfloat16)
    q_side[slab] = jnp.where(lane < 5, q_value, 0.0).astype(jnp.bfloat16)


def meta_slabs(meta):
    return (meta.shape[0] - 2) // 5


def lane_low(row_count):
    return lax.broadcasted_iota(jnp.int32, (row_count, PAIR), 1) < HEAD_DIM


def attention_forward_kernel(meta, qkv, mixed, logsum, k_side, q_side):
    slab, pair = pl.program_id(1), pl.program_id(0)
    slab_rows = qkv.shape[1]

    @pl.when(pair == 0)
    def _():
        slab_features(meta, slab, slab_rows, k_side, q_side)

    low = lane_low(slab_rows)
    query, key = qkv[0].astype(jnp.float32), qkv[1].astype(jnp.float32)
    k_extra, q_extra = k_side[slab].astype(jnp.float32), q_side[slab].astype(jnp.float32)
    value_flip = flipped(qkv[2])
    sub = lax.broadcasted_iota(jnp.int32, (PAIR, slab_rows), 0)
    outcomes = []
    for head in range(2):
        mine = low if head == 0 else jnp.logical_not(low)
        q_head = jnp.where(mine, query, q_extra).astype(jnp.bfloat16)
        k_head = jnp.where(mine, key, k_extra).astype(jnp.bfloat16)
        scores = dot_nt(k_head, q_head)
        top = jnp.max(scores, axis=0, keepdims=True)
        weight = jnp.exp2((scores - top) * exponent_scale).astype(jnp.bfloat16)
        sum_row = HEAD_DIM if head == 0 else 0
        kept = sub < HEAD_DIM if head == 0 else sub >= HEAD_DIM
        v_head = jnp.where(kept, value_flip, jnp.where(sub == sum_row, 1.0, 0.0))
        blend = dot_nn(v_head.astype(jnp.bfloat16), weight)
        total = blend[sum_row : sum_row + 1, :]
        logsum[0, 0, head : head + 1, :] = top * exponent_scale + jnp.log(total) * log2_e
        outcomes.append(blend / total)
    mixed[...] = jnp.where(sub < HEAD_DIM, outcomes[0], outcomes[1]).T.astype(jnp.bfloat16)


def ffn_forward_kernel(orders, meta, mixed, inputs, vectors, ffn_bias, *refs):
    vo_sources, in_sources, down_sources = refs[0:4], refs[4:8], refs[8:12]
    hidden, normed_one, spread_one, activated, slope, result, normed_two, spread_two = refs[12:20]
    out_whole, in_whole, down_whole, total, out_sems, in_sems, down_sems = refs[20:]
    step = pl.program_id(0)
    steps = pl.num_programs(0)
    everything = slice(None)
    out_columns = out_whole.shape[2]
    tiles = row_tiles(inputs.shape[0])
    lanes = spread_one.shape[1]

    @pl.when(step == 0)
    def _():
        load_blocks(
            meta, vo_sources, orders[1], out_whole, everything,
            slice(out_columns, 2 * out_columns), out_sems,
        )
        load_blocks(meta, in_sources, orders[0], in_whole, everything, everything, in_sems)
        load_blocks(meta, down_sources, orders[1], down_whole, everything, everything, down_sems)
        for half_at in range(2):
            await_blocks(out_whole, half_at, everything, out_sems)
        for rows in tiles:
            attention_out = vectors[0:1, :]
            for half_at in range(2):
                columns = slice(half_at * out_columns, (half_at + 1) * out_columns)
                attention_out = attention_out + dot_nt(mixed[rows, columns], out_whole[half_at])
            normed, spread = norm_stats(inputs[rows, :].astype(jnp.float32) + attention_out)
            low = (normed * vectors[2:3, :] + vectors[4:5, :]).astype(jnp.bfloat16)
            hidden[rows, :] = low
            normed_one[rows, :] = normed.astype(jnp.bfloat16)
            spread_one[rows, :] = jnp.broadcast_to(spread, (spread.shape[0], lanes))
            total[rows, :] = low.astype(jnp.float32) + vectors[1:2, :]

    half_at = meta[1] ^ (step // FFN_PARTS)
    width = activated.shape[1]
    part = pl.ds(pl.multiple_of((step % FFN_PARTS) * width, 128), width)

    @pl.when(step % FFN_PARTS == 0)
    def _():
        await_blocks(in_whole, half_at, everything, in_sems)
        await_blocks(down_whole, half_at, everything, down_sems)

    for rows in tiles:
        pre_gelu = dot_nn(hidden[rows, :], in_whole[half_at, :, part]) + ffn_bias[0]
        value, steep = gelu_parts(pre_gelu)
        low = value.astype(jnp.bfloat16)
        activated[rows, :] = low
        slope[rows, :] = steep.astype(jnp.bfloat16)
        total[rows, :] += dot_nt(low, down_whole[half_at, :, part])

    @pl.when(step == steps - 1)
    def _():
        for rows in tiles:
            normed, spread = norm_stats(total[rows, :])
            result[rows, :] = (normed * vectors[3:4, :] + vectors[5:6, :]).astype(jnp.bfloat16)
            normed_two[rows, :] = normed.astype(jnp.bfloat16)
            spread_two[rows, :] = jnp.broadcast_to(spread, (spread.shape[0], lanes))


def ffn_backward_kernel(
    orders, meta, gradient, normed_two, spread_two, hidden, normed_one, spread_one, activated,
    slope, vectors, *refs
):
    in_sources, down_sources = refs[0:4], refs[4:8]
    attention_grad, resid_grad, sums, bias_sums = refs[8:12]
    in_targets, down_targets = refs[12:14], refs[14:16]
    (
        in_whole, down_whole, total, branch, branch_flip, hidden_flip, pre_part, grad_parts,
        in_sems, down_sems, out_sems,
    ) = refs[16:]
    step = pl.program_id(0)
    steps = pl.num_programs(0)
    everything = slice(None)
    tiles = row_tiles(hidden.shape[0])
    slot = step % 2

    @pl.when(step == 0)
    def _():
        load_blocks(meta, in_sources, orders[0], in_whole, everything, everything, in_sems)
        load_blocks(meta, down_sources, orders[1], down_whole, everything, everything, down_sems)
        gain_sum, shift_sum, branch_sum = 0.0, 0.0, 0.0
        for rows in tiles:
            grad = gradient[rows, :].astype(jnp.float32)
            normed = normed_two[rows, :].astype(jnp.float32)
            resid = norm_back(grad, normed, spread_two[rows, 0:1], vectors[3:4, :])
            low = resid.astype(jnp.bfloat16)
            total[rows, :] = resid
            branch[rows, :] = low
            branch_flip[:, rows] = flipped(low).astype(jnp.bfloat16)
            hidden_flip[:, rows] = flipped(hidden[rows, :]).astype(jnp.bfloat16)
            gain_sum += column_sum(grad * normed)
            shift_sum += column_sum(grad)
            branch_sum += column_sum(low.astype(jnp.float32))
        sums[...] = jnp.zeros(sums.shape, jnp.float32)
        sums[1:2, :] = branch_sum
        sums[3:4, :] = gain_sum
        sums[5:6, :] = shift_sum

    half_at = meta[1] ^ (step // FFN_PARTS)
    width = activated.shape[1]
    part = pl.ds(pl.multiple_of((step % FFN_PARTS) * width, 128), width)

    @pl.when(step % FFN_PARTS == 0)
    def _():
        await_blocks(in_whole, half_at, everything, in_sems)
        await_blocks(down_whole, half_at, everything, down_sems)

    @pl.when(step >= 2)
    def _():
        await_stored(grad_parts.at[slot, 0], out_sems.at[slot, 0])
        await_stored(grad_parts.at[slot, 1], out_sems.at[slot, 1])

    grad_parts[slot, 1] = dot_nn(branch_flip[...], activated[...]).astype(jnp.bfloat16)
    store_blocks(
        meta, grad_parts.at[slot, 1], down_targets, orders[1], step // FFN_PARTS, part,
        out_sems.at[slot, 1],
    )
    bias_sum = 0.0
    for rows in tiles:
        active_grad = dot_nn(branch[rows, :], down_whole[half_at, :, part])
        low = (active_grad * slope[rows, :].astype(jnp.float32)).astype(jnp.bfloat16)
        pre_part[rows, :] = low
        bias_sum += column_sum(low.astype(jnp.float32))
        total[rows, :] += dot_nt(low, in_whole[half_at, :, part])
    bias_sums[0] = bias_sum
    grad_parts[slot, 0] = dot_nn(hidden_flip[...], pre_part[...]).astype(jnp.bfloat16)
    store_blocks(
        meta, grad_parts.at[slot, 0], in_targets, orders[0], step // FFN_PARTS, part,
        out_sems.at[slot, 0],
    )

    @pl.when(step == steps - 1)
    def _():
        gain_sum, shift_sum, branch_sum = 0.0, 0.0, 0.0
        for rows in tiles:
            grad = total[rows, :]
            normed = normed_one[rows, :].astype(jnp.float32)
            resid = norm_back(grad, normed, spread_one[rows, 0:1], vectors[2:3, :])
            low = resid.astype(jnp.bfloat16)
            resid_grad[rows, :] = resid
            attention_grad[rows, :] = low
            gain_sum += column_sum(grad * normed)
            shift_sum += column_sum(grad)
            branch_sum += column_sum(low.astype(jnp.float32))
        sums[0:1, :] = branch_sum
        sums[2:3, :] = gain_sum
        sums[4:5, :] = shift_sum
        for late in range(2):
            await_stored(grad_parts.at[late, 0], out_sems.at[late, 0])
            await_stored(grad_parts.at[late, 1], out_sems.at[late, 1])


def out_backward_kernel(orders, meta, attention_grad, mixed, *refs):
    vo_sources, mixed_grad, out_targets = refs[0:4], refs[4], refs[5:7]
    out_whole, grad_flip, grad_parts, load_sems, out_sems = refs[7:]
    step = pl.program_id(0)
    columns = mixed.shape[1]
    everything = slice(None)
    tiles = row_tiles(mixed.shape[0])

    @pl.when(step == 0)
    def _():
        load_blocks(
            meta, vo_sources, orders[1], out_whole, everything, slice(columns, 2 * columns), load_sems
        )
        for rows in tiles:
            grad_flip[:, rows] = flipped(attention_grad[rows, :]).astype(jnp.bfloat16)

    half_at = meta[1] ^ step
    grad_parts[step] = dot_nn(grad_flip[...], mixed[...]).astype(jnp.bfloat16)
    store_blocks(
        meta, grad_parts.at[step], out_targets, orders[0], step, everything, out_sems.at[step]
    )
    await_blocks(out_whole, half_at, everything, load_sems)
    for rows in tiles:
        mixed_grad[rows, :] = dot_nn(attention_grad[rows, :], out_whole[half_at]).astype(
            jnp.bfloat16
        )

    @pl.when(step == 1)
    def _():
        for late in range(2):
            await_stored(grad_parts.at[late], out_sems.at[late])


def attention_backward_kernel(meta, qkv, mixed, mixed_grad, logsum, grads, sums, k_side, q_side):
    slab, pair = pl.program_id(1), pl.program_id(0)
    slab_rows = qkv.shape[1]

    @pl.when(pair == 0)
    def _():
        slab_features(meta, slab, slab_rows, k_side, q_side)

    low = lane_low(slab_rows)
    query, key, value = (qkv[place].astype(jnp.float32) for place in range(3))
    k_extra, q_extra = k_side[slab].astype(jnp.float32), q_side[slab].astype(jnp.float32)
    grad_low = mixed_grad[...]
    grad = grad_low.astype(jnp.float32)
    product = (grad * mixed[...].astype(jnp.float32)).T
    key_flip = key.T
    sub = lax.broadcasted_iota(jnp.int32, (PAIR, slab_rows), 0)
    query_flip, key_grad, value_grad = 0.0, 0.0, 0.0
    for head in range(2):
        mine = low if head == 0 else jnp.logical_not(low)
        kept = sub < HEAD_DIM if head == 0 else sub >= HEAD_DIM
        span = slice(head * HEAD_DIM, (head + 1) * HEAD_DIM)
        q_head = jnp.where(mine, query, q_extra).astype(jnp.bfloat16)
        k_head = jnp.where(mine, key, k_extra).astype(jnp.bfloat16)
        v_head = jnp.where(mine, value, 0.0).astype(jnp.bfloat16)
        probs = jnp.exp2(
            dot_nt(k_head, q_head) * exponent_scale - logsum[0, 0, head : head + 1, :]
        )
        delta = column_sum(product[span, :])
        raw_grad = (probs * (dot_nt(v_head, grad_low) - delta)).astype(jnp.bfloat16)
        g_head = jnp.where(mine, grad, 0.0).astype(jnp.bfloat16)
        value_grad += dot_nn(probs.astype(jnp.bfloat16), g_head)
        key_grad += dot_nn(raw_grad, jnp.where(mine, query, 0.0).astype(jnp.bfloat16))
        query_flip += dot_nn(jnp.where(kept, key_flip, 0.0).astype(jnp.bfloat16), raw_grad)
    query_low = (query_flip * score_scale).T.astype(jnp.bfloat16)
    value_low = value_grad.astype(jnp.bfloat16)
    grads[0] = query_low
    grads[1] = (key_grad * score_scale).astype(jnp.bfloat16)
    grads[2] = value_low

    @pl.when(slab == 0)
    def _():
        sums[...] = jnp.zeros(sums.shape, jnp.float32)

    sums[0:1, :] += column_sum(query_low.astype(jnp.float32))
    sums[1:2, :] += column_sum(value_low.astype(jnp.float32))


def qkv_backward_kernel(orders, meta, inputs, grads, resid_grad, *refs):
    qk_sources, vo_sources, input_grad = refs[0:4], refs[4:8], refs[8]
    q_targets, kv_targets = refs[9:11], refs[11:13]
    weights, inputs_flip, grad_parts, qk_sems, v_sems, out_sems = refs[13:]
    step = pl.program_id(0)
    steps = pl.num_programs(0)
    columns = grads.shape[2]
    tiles = row_tiles(inputs.shape[0])
    slot = step % 2
    which = step % 3

    @pl.when(step == 0)
    def _():
        load_blocks(
            meta, qk_sources, orders[0], weights, slice(0, 2 * columns), slice(None), qk_sems
        )
        load_blocks(
            meta, vo_sources, orders[1], weights, slice(2 * columns, 3 * columns),
            slice(0, columns), v_sems,
        )
        for rows in tiles:
            inputs_flip[:, rows] = flipped(inputs[rows, :]).astype(jnp.bfloat16)
            input_grad[rows, :] = resid_grad[rows, :]

    @pl.when(step >= 2)
    def _():
        await_stored(grad_parts.at[slot], out_sems.at[slot])

    grad_parts[slot] = dot_nn(inputs_flip[...], grads[0]).astype(jnp.bfloat16)

    @pl.when(which == 0)
    def _():
        store_blocks(
            meta, grad_parts.at[slot], q_targets, orders[0], step // 3, slice(None), out_sems.at[slot]
        )

    @pl.when(which > 0)
    def _():
        store_blocks(
            meta, grad_parts.at[slot], kv_targets, orders[1], step // 3,
            pl.ds(pl.multiple_of((which - 1) * columns, 128), columns), out_sems.at[slot],
        )

    half_at = meta[1] ^ (step // 3)

    @pl.when(which == 0)
    def _():
        await_blocks(weights, half_at, slice(0, 2 * columns), qk_sems)
        await_blocks(weights, half_at, slice(2 * columns, 3 * columns), v_sems)

    span = pl.ds(pl.multiple_of(which * columns, 128), columns)
    for rows in tiles:
        input_grad[rows, :] += dot_nt(grads[0, rows, :], weights[half_at, :, span])

    @pl.when(step == steps - 1)
    def _():
        for late in range(2):
            await_stored(grad_parts.at[late], out_sems.at[late])


def fixed(shape):
    return pl.BlockSpec(
        shape, lambda *_: (0,) * len(shape), pipeline_mode=pl.Buffered(1)
    )


def fixed_out(shape):
    return pl.BlockSpec(shape, lambda *_: (0,) * len(shape))


ANYWHERE = pl.BlockSpec(memory_space=pl.ANY)


def run_kernel(kernel, meta, grid, ins, outs, scratch, flops, moved, name):
    in_specs, operands = zip(*ins)
    out_specs, out_shapes = zip(*outs)
    return pl.pallas_call(
        kernel,
        grid_spec=pltpu.PrefetchScalarGridSpec(
            num_scalar_prefetch=1,
            grid=grid,
            in_specs=list(in_specs),
            out_specs=list(out_specs),
            scratch_shapes=scratch,
        ),
        out_shape=list(out_shapes),
        compiler_params=pltpu.CompilerParams(vmem_limit_bytes=VMEM_LIMIT),
        cost_estimate=pl.CostEstimate(flops=flops, bytes_accessed=moved, transcendentals=0),
        name=name,
    )(meta, *operands)


def low_shape(*shape):
    return jax.ShapeDtypeStruct(shape, jnp.bfloat16)


def full_shape(*shape):
    return jax.ShapeDtypeStruct(shape, jnp.float32)


def pair_sems():
    return pltpu.SemaphoreType.DMA((2,))


def half_of(step, meta, count):
    return meta[1] ^ (step // count)


def qkv_forward(orders, meta, inputs, bias, qk_blocks, vo_blocks):
    rows, width = inputs.shape
    columns = width // 2
    (qkv,) = run_kernel(
        functools.partial(qkv_forward_kernel, orders),
        meta,
        (6,),
        [
            (fixed((rows, width)), inputs),
            (
                pl.BlockSpec((1, 1, columns), lambda i, m: ((i % 3) * 2 + half_of(i, m, 3), 0, 0)),
                bias,
            ),
        ]
        + [(ANYWHERE, member) for member in qk_blocks + vo_blocks],
        [
            (
                pl.BlockSpec((1, rows, columns), lambda i, m: (i % 3, 0, half_of(i, m, 3))),
                low_shape(3, rows, width),
            )
        ],
        [pltpu.VMEM((2, width, 3 * columns), jnp.bfloat16), pair_sems(), pair_sems()],
        6 * rows * width * width,
        8 * rows * width + 6 * width * width,
        "qkv_forward",
    )
    return qkv


def attention_forward(meta, qkv, slab_count):
    _, rows, width = qkv.shape
    slab_rows = rows // slab_count
    pairs = width // PAIR
    return run_kernel(
        attention_forward_kernel,
        meta,
        (pairs, slab_count),
        [(pl.BlockSpec((3, slab_rows, PAIR), lambda p, s, m: (0, s, p)), qkv)],
        [
            (pl.BlockSpec((slab_rows, PAIR), lambda p, s, m: (s, p)), low_shape(rows, width)),
            (
                pl.BlockSpec((1, 1, 8, slab_rows), lambda p, s, m: (s, p, 0, 0)),
                full_shape(slab_count, pairs, 8, slab_rows),
            ),
        ],
        [pltpu.VMEM((slab_count, slab_rows, PAIR), jnp.bfloat16)] * 2,
        16 * rows * slab_rows * width,
        8 * rows * width,
        "attention_forward",
    )


def ffn_forward(orders, meta, mixed, inputs, vectors, ffn_bias, vo_blocks, in_blocks, down_blocks):
    rows, width = inputs.shape
    half_width = in_blocks[0].shape[2]
    part = half_width // FFN_PARTS

    def part_at(i, m):
        return half_of(i, m, FFN_PARTS) * FFN_PARTS + i % FFN_PARTS

    whole_rows = (fixed_out((rows, width)), low_shape(rows, width))
    spread = (fixed_out((rows, 128)), full_shape(rows, 128))
    inner = (
        pl.BlockSpec((rows, part), lambda i, m: (0, part_at(i, m))),
        low_shape(rows, 2 * half_width),
    )
    return run_kernel(
        functools.partial(ffn_forward_kernel, orders),
        meta,
        (2 * FFN_PARTS,),
        [
            (fixed((rows, width)), mixed),
            (fixed((rows, width)), inputs),
            (fixed((8, width)), vectors),
            (pl.BlockSpec((1, 1, part), lambda i, m: (part_at(i, m), 0, 0)), ffn_bias),
        ]
        + [(ANYWHERE, member) for member in vo_blocks + in_blocks + down_blocks],
        [whole_rows, whole_rows, spread, inner, inner, whole_rows, whole_rows, spread],
        [
            pltpu.VMEM((2, width, width // 2), jnp.bfloat16),
            pltpu.VMEM((2, width, half_width), jnp.bfloat16),
            pltpu.VMEM((2, width, half_width), jnp.bfloat16),
            pltpu.VMEM((rows, width), jnp.float32),
            pair_sems(),
            pair_sems(),
            pair_sems(),
        ],
        8 * rows * width * half_width,
        24 * rows * width + 8 * width * half_width,
        "ffn_forward",
    )


def ffn_backward(orders, meta, gradient, kept, vectors, in_blocks, down_blocks):
    hidden, normed_one, spread_one, activated, slope, normed_two, spread_two = kept
    rows, width = hidden.shape
    half_width = in_blocks[0].shape[2]
    part = half_width // FFN_PARTS
    slots, block_rows = 2 * in_blocks[0].shape[0], in_blocks[0].shape[1]

    def part_at(i, m):
        return half_of(i, m, FFN_PARTS) * FFN_PARTS + i % FFN_PARTS

    low_rows = fixed((rows, width))
    spread = fixed((rows, 128))
    inner = pl.BlockSpec((rows, part), lambda i, m: (0, part_at(i, m)))
    target = (ANYWHERE, low_shape(slots, block_rows, half_width))
    return run_kernel(
        functools.partial(ffn_backward_kernel, orders),
        meta,
        (2 * FFN_PARTS,),
        [
            (low_rows, gradient),
            (low_rows, normed_two),
            (spread, spread_two),
            (low_rows, hidden),
            (low_rows, normed_one),
            (spread, spread_one),
            (inner, activated),
            (inner, slope),
            (fixed((8, width)), vectors),
        ]
        + [(ANYWHERE, member) for member in in_blocks + down_blocks],
        [
            (fixed_out((rows, width)), low_shape(rows, width)),
            (fixed_out((rows, width)), full_shape(rows, width)),
            (fixed_out((8, width)), full_shape(8, width)),
            (
                pl.BlockSpec((1, 1, part), lambda i, m: (part_at(i, m), 0, 0)),
                full_shape(2 * FFN_PARTS, 1, part),
            ),
            target,
            target,
            target,
            target,
        ],
        [
            pltpu.VMEM((2, width, half_width), jnp.bfloat16),
            pltpu.VMEM((2, width, half_width), jnp.bfloat16),
            pltpu.VMEM((rows, width), jnp.float32),
            pltpu.VMEM((rows, width), jnp.bfloat16),
            pltpu.VMEM((width, rows), jnp.bfloat16),
            pltpu.VMEM((width, rows), jnp.bfloat16),
            pltpu.VMEM((rows, part), jnp.bfloat16),
            pltpu.VMEM((2, 2, width, part), jnp.bfloat16),
            pair_sems(),
            pair_sems(),
            pltpu.SemaphoreType.DMA((2, 2)),
        ],
        16 * rows * width * half_width,
        40 * rows * width + 16 * width * half_width,
        "ffn_backward",
    )


def out_backward(orders, meta, attention_grad, mixed, vo_blocks):
    rows, width = mixed.shape
    columns = width // 2
    slots, block_rows = 2 * vo_blocks[0].shape[0], vo_blocks[0].shape[1]
    half = pl.BlockSpec((rows, columns), lambda i, m: (0, half_of(i, m, 1)))
    target = (ANYWHERE, low_shape(slots, block_rows, columns))
    return run_kernel(
        functools.partial(out_backward_kernel, orders),
        meta,
        (2,),
        [(fixed((rows, width)), attention_grad), (half, mixed)]
        + [(ANYWHERE, member) for member in vo_blocks],
        [(half, low_shape(rows, width)), target, target],
        [
            pltpu.VMEM((2, width, columns), jnp.bfloat16),
            pltpu.VMEM((width, rows), jnp.bfloat16),
            pltpu.VMEM((2, width, columns), jnp.bfloat16),
            pair_sems(),
            pair_sems(),
        ],
        4 * rows * width * width,
        6 * rows * width + 4 * width * width,
        "out_backward",
    )


def attention_backward(meta, qkv, mixed, mixed_grad, logsum, slab_count):
    _, rows, width = qkv.shape
    slab_rows = rows // slab_count
    pairs = width // PAIR
    three = pl.BlockSpec((3, slab_rows, PAIR), lambda p, s, m: (0, s, p))
    one = pl.BlockSpec((slab_rows, PAIR), lambda p, s, m: (s, p))
    return run_kernel(
        attention_backward_kernel,
        meta,
        (pairs, slab_count),
        [
            (three, qkv),
            (one, mixed),
            (one, mixed_grad),
            (pl.BlockSpec((1, 1, 8, slab_rows), lambda p, s, m: (s, p, 0, 0)), logsum),
        ],
        [
            (three, low_shape(3, rows, width)),
            (pl.BlockSpec((8, PAIR), lambda p, s, m: (0, p)), full_shape(8, width)),
        ],
        [pltpu.VMEM((slab_count, slab_rows, PAIR), jnp.bfloat16)] * 2,
        40 * rows * slab_rows * width,
        16 * rows * width,
        "attention_backward",
    )


def qkv_backward(orders, meta, inputs, grads, resid_grad, qk_blocks, vo_blocks):
    rows, width = inputs.shape
    columns = width // 2
    slots, block_rows = 2 * qk_blocks[0].shape[0], qk_blocks[0].shape[1]
    q_target = (ANYWHERE, low_shape(slots, block_rows, columns))
    kv_target = (ANYWHERE, low_shape(slots, block_rows, 2 * columns))
    return run_kernel(
        functools.partial(qkv_backward_kernel, orders),
        meta,
        (6,),
        [
            (fixed((rows, width)), inputs),
            (pl.BlockSpec((1, rows, columns), lambda i, m: (i % 3, 0, half_of(i, m, 3))), grads),
            (fixed((rows, width)), resid_grad),
        ]
        + [(ANYWHERE, member) for member in qk_blocks + vo_blocks],
        [
            (fixed_out((rows, width)), full_shape(rows, width)),
            q_target,
            q_target,
            kv_target,
            kv_target,
        ],
        [
            pltpu.VMEM((2, width, 3 * columns), jnp.bfloat16),
            pltpu.VMEM((width, rows), jnp.bfloat16),
            pltpu.VMEM((2, width, columns), jnp.bfloat16),
            pair_sems(),
            pair_sems(),
            pair_sems(),
        ],
        12 * rows * width * width,
        14 * rows * width + 12 * width * width,
        "qkv_backward",
    )


def both_halves(mine, theirs, place):
    first = jnp.concatenate([mine, theirs], axis=0)
    second = jnp.concatenate([theirs, mine], axis=0)
    return jnp.where(place == 0, first, second)


def on_device(
    tokens,
    cotangent,
    buckets,
    lengths,
    qkv_weight,
    qv_bias,
    out_weight,
    ffn_in_weight,
    ffn_in_bias,
    ffn_out_weight,
    out_bias,
    norm_gain,
    norm_bias,
):
    split = lax.axis_size("tensor")
    dp_size = lax.axis_size("dp")
    place = lax.axis_index("tensor")
    width = tokens.shape[1]
    rows = tokens.shape[0] // split
    slabs = buckets.shape[0] // split
    layer_count = qkv_weight.shape[0]
    block_rows = width // dp_size
    routed = block_rows % TILE_ROWS == 0 and dp_size & (dp_size - 1) == 0
    orders = hop_orders(dp_size if routed else PLANNED_BLOCKS)
    gather = gather_piece if routed else gather_whole
    scatter = scatter_piece if routed else scatter_whole

    own_tokens = lax.dynamic_slice_in_dim(tokens, place * rows, rows)
    own_cotangent = lax.dynamic_slice_in_dim(cotangent, place * rows, rows)
    own_buckets = lax.dynamic_slice_in_dim(buckets, place * slabs, slabs)
    own_lengths = lax.dynamic_slice_in_dim(lengths, place * slabs, slabs)
    if routed:
        position = jnp.stack([lax.axis_index("dp"), place]).astype(jnp.int32)
    else:
        position = jnp.zeros((2,), jnp.int32)
    meta = jnp.concatenate([position, own_buckets, own_lengths.reshape(-1)])

    pieces = []
    for index in range(layer_count):
        qk_shard = jnp.concatenate([qkv_weight[index, 0], qkv_weight[index, 1]], axis=1)
        vo_shard = jnp.concatenate([qkv_weight[index, 2], out_weight[index]], axis=1)
        pieces.append(
            (
                gather(qk_shard, orders[0]),
                gather(vo_shard, orders[1]),
                gather(ffn_in_weight[index], orders[0]),
                gather(ffn_out_weight[index], orders[1]),
            )
        )
    qv_whole = lax.all_gather(qv_bias, "tensor", axis=2, tiled=True)
    ffn_bias_whole = lax.all_gather(ffn_in_bias, "tensor", axis=1, tiled=True)

    current = own_tokens
    kept_layers = []
    results = []
    for index in range(layer_count):
        qk_blocks, vo_blocks, in_blocks, down_blocks = pieces[index]
        zero = jnp.zeros((width,), jnp.float32)
        bias = jnp.stack([qv_whole[index, 0], zero, qv_whole[index, 1]]).reshape(6, 1, -1)
        vectors = jnp.concatenate(
            [out_bias[index], norm_gain[index], norm_bias[index], jnp.zeros((2, width), jnp.float32)]
        )
        qkv = qkv_forward(orders, meta, current, bias, qk_blocks, vo_blocks)
        mixed, logsum = attention_forward(meta, qkv, slabs)
        hidden, normed_one, spread_one, activated, slope, result, normed_two, spread_two = ffn_forward(
            orders, meta, mixed, current, vectors,
            ffn_bias_whole[index].reshape(2 * FFN_PARTS, 1, -1), vo_blocks, in_blocks, down_blocks,
        )
        kept_layers.append(
            (
                current, qkv, mixed, logsum, vectors,
                (hidden, normed_one, spread_one, activated, slope, normed_two, spread_two),
            )
        )
        current = result
        results.append(both_halves(result, hop(result, ("tensor", 1)), place))

    gradient = own_cotangent
    matrix_grads = [None] * layer_count
    small_grads = [None] * layer_count
    for index in reversed(range(layer_count)):
        qk_blocks, vo_blocks, in_blocks, down_blocks = pieces[index]
        inputs, qkv, mixed, logsum, vectors, kept = kept_layers[index]
        attention_grad, resid_grad, sums, ffn_sums, in_keep, in_send, down_keep, down_send = (
            ffn_backward(orders, meta, gradient, kept, vectors, in_blocks, down_blocks)
        )
        in_grad = scatter(in_keep, in_send, orders[0])
        down_grad = scatter(down_keep, down_send, orders[1])
        mixed_grad, out_keep, out_send = out_backward(orders, meta, attention_grad, mixed, vo_blocks)
        out_grad = scatter(out_keep, out_send, orders[0])
        grads, qkv_sums = attention_backward(meta, qkv, mixed, mixed_grad, logsum, slabs)
        gradient, q_keep, q_send, kv_keep, kv_send = qkv_backward(
            orders, meta, inputs, grads, resid_grad, qk_blocks, vo_blocks
        )
        q_grad = scatter(q_keep, q_send, orders[0])
        kv_grad = scatter(kv_keep, kv_send, orders[1])
        columns = q_grad.shape[1]
        matrix_grads[index] = (
            jnp.stack([q_grad, kv_grad[:, :columns], kv_grad[:, columns:]]),
            out_grad,
            in_grad,
            down_grad,
        )
        small_grads[index] = lax.psum(
            jnp.concatenate([sums[:6].reshape(-1), qkv_sums[:2].reshape(-1), ffn_sums.reshape(-1)]),
            AXES,
        )
    low_gradient = gradient.astype(jnp.bfloat16)
    token_grad = both_halves(
        gradient, hop(low_gradient, ("tensor", 1)).astype(jnp.float32), place
    )

    smalls = jnp.stack(small_grads)
    eight = smalls[:, : 8 * width].reshape(layer_count, 4, 2, width)
    ffn_total = smalls[:, 8 * width :]
    qv_columns = qv_bias.shape[2]
    ffn_columns = ffn_in_bias.shape[1]
    return (
        results[0],
        results[layer_count - 1],
        token_grad,
        jnp.stack([member[0] for member in matrix_grads]),
        lax.dynamic_slice_in_dim(eight[:, 3], place * qv_columns, qv_columns, axis=2),
        jnp.stack([member[1] for member in matrix_grads]),
        jnp.stack([member[2] for member in matrix_grads]),
        lax.dynamic_slice_in_dim(ffn_total, place * ffn_columns, ffn_columns, axis=1),
        jnp.stack([member[3] for member in matrix_grads]),
        eight[:, 0],
        eight[:, 1],
        eight[:, 2],
    )


def solution(mesh):
    placed = (
        P("dp", None),
        P("dp", None),
        P("dp"),
        P("dp", None),
        P(None, None, "dp", "tensor"),
        P(None, None, "tensor"),
        P(None, "dp", "tensor"),
        P(None, "dp", "tensor"),
        P(None, "tensor"),
        P(None, "dp", "tensor"),
        P(),
        P(),
        P(),
    )
    return jax.shard_map(
        on_device,
        mesh=mesh,
        in_specs=placed,
        out_specs=(
            P("dp", None),
            P("dp", None),
            P("dp", None),
            P(None, None, "dp", "tensor"),
            P(None, None, "tensor"),
            P(None, "dp", "tensor"),
            P(None, "dp", "tensor"),
            P(None, "tensor"),
            P(None, "dp", "tensor"),
            P(),
            P(),
            P(),
        ),
        check_vma=False,
    )
```

```python
import functools

import jax
import jax.numpy as jnp
from jax import lax
from jax.experimental import pallas as pl
from jax.experimental.pallas import tpu as pltpu
from jax.sharding import PartitionSpec as P

HEAD_DIM = 64
PAIR = 2 * HEAD_DIM
AXES = ("tensor", "dp")
CORE = ("dp", 1)
FFN_PARTS = 3
ROW_TILE = 256
TILE_ROWS = 16
PLANNED_BLOCKS = 16
HOPS = ((True, False), (True, False))
HOPS_BACK = ((True, True), (True, False))
COST_WEIGHT = 8
LATE_WEIGHTS = True
HOLD_TOKENS = False
VMEM_LIMIT = 58 * 1024 * 1024

norm_eps = 1e-06
big_negative = -1e30
inv_root_tau = 0.3989422804014327
log2_e = 1.4426950408889634
score_scale = HEAD_DIM ** (-0.5)
exponent_scale = score_scale * log2_e
erf_slope = 0.3275911 * 0.7071067811865476
erf_terms = (1.061405429, -1.453152027, 1.421413741, -0.284496736, 0.254829592)


def dot_nn(left, right):
    return lax.dot_general(
        left, right, (((1,), (0,)), ((), ())), preferred_element_type=jnp.float32
    )


def dot_nt(left, right):
    return lax.dot_general(
        left, right, (((1,), (1,)), ((), ())), preferred_element_type=jnp.float32
    )


def flipped(member):
    return member.astype(jnp.float32).T


def hop_orders(block_count):
    far = []
    bit = 4
    while bit < block_count:
        far.append(("dp", bit))
        bit *= 2
    across, along = ("dp", 2), ("tensor", 1)
    return (far + [across, along], far + [along, across])


def slot_table(order):
    table = []
    for slot in range(2 ** len(order)):
        dp_part, tensor_part = 0, 0
        for position, (axis, bit) in enumerate(order):
            if slot >> position & 1:
                if axis == "dp":
                    dp_part ^= bit
                else:
                    tensor_part ^= bit
        table.append((dp_part, tensor_part))
    return table


def hop(member, dim):
    axis, bit = dim
    pairs = [(place, place ^ bit) for place in range(lax.axis_size(axis))]
    return lax.ppermute(member, axis, pairs)


def tied(member, others):
    return lax.optimization_barrier((member, *others))[0] if others else member


class Piece:
    def __init__(self, arrays, order, first, count):
        self.arrays, self.order, self.columns = tuple(arrays), order, slice(first, first + count)
        self.count = count

    def narrow(self, first, count):
        return Piece(self.arrays, self.order, self.columns.start + first, count)


class Gathering:
    def __init__(self, shard, orders):
        self.shard, self.orders, self.width = shard[None], orders, shard.shape[1] // 2

    def halves(self, member):
        return [member[..., : self.width], member[..., self.width :]]

    def far(self, *others):
        shard = tied(self.shard, others)
        count = 2 ** (len(self.orders[0]) - 2)
        parts = [shard] + [hop(shard, ("dp", 4 * step)) for step in range(1, count)]
        self.current = [
            jnp.concatenate(sides, axis=0) for sides in zip(*[self.halves(part) for part in parts])
        ]
        return self.current

    def middle(self, *others):
        current = [tied(member, others) for member in self.current]
        self.current = [
            jnp.concatenate([member, hop(member, order[-2])], axis=0)
            for member, order in zip(current, self.orders)
        ]
        return self.current

    def last(self, *others):
        current = [tied(member, others) for member in self.current]
        self.later = [hop(member, order[-1]) for member, order in zip(current, self.orders)]
        self.core_current = [hop(member, CORE) for member in current]
        return self.later

    def core(self, *others):
        self.core_later = [hop(tied(member, others), CORE) for member in self.later]
        return self.core_later

    def pieces(self):
        sides = zip(self.current, self.later, self.core_current, self.core_later)
        return [Piece(side, order, 0, self.width) for side, order in zip(sides, self.orders)]


class WholeGathering:
    def __init__(self, shard, orders, *others):
        self.width, self.orders = shard.shape[1] // 2, orders
        whole = lax.all_gather(tied(shard, others), AXES, tiled=True)
        self.whole = whole.reshape(lax.axis_size("tensor"), -1, shard.shape[1])

    def far(self, *others):
        return [self.whole]

    middle = last = core = far

    def pieces(self):
        return [
            Piece([self.whole], order, side * self.width, self.width)
            for side, order in enumerate(self.orders)
        ]


class Scattering:
    def __init__(self, members, orders, sides):
        self.members, self.orders, self.sides = members, orders, sides
        self.begun = [members[-1][0]]

    def core(self, *others):
        arrived = [hop(tied(send, others), CORE) for keep, send in self.members]
        both = [[keep, come] for (keep, send), come in zip(self.members, arrived)]
        self.parts = [
            [[part[..., first:end] for part in both[member]] for member, first, end in side]
            for side in self.sides
        ]
        return arrived

    def total(self, side, take):
        sums = [
            sum(take(part).astype(jnp.float32) for part in group) for group in self.parts[side]
        ]
        return jnp.concatenate(sums, axis=-1) if len(sums) > 1 else sums[0]

    def halve(self, which, others):
        arrived = []
        for side, order in enumerate(self.orders):
            half = self.parts[side][0][0].shape[0] // 2
            upper = self.total(side, lambda part: part[half:]).astype(jnp.bfloat16)
            come = hop(tied(upper, others), order[which])
            arrived.append(come)
            at = 0
            for group in self.parts[side]:
                width = group[0].shape[-1]
                group[:] = [part[:half] for part in group] + [come[..., at : at + width]]
                at += width
        return arrived

    def last(self, *others):
        return self.halve(-1, others)

    def middle(self, *others):
        return self.halve(-2, others)

    def far(self, *others):
        count = self.parts[0][0][0].shape[0]
        sides = range(len(self.orders))
        mine = jnp.concatenate([self.total(side, lambda part: part[0]) for side in sides], axis=-1)
        arrived = []
        for step in range(1, count):
            upper = jnp.concatenate(
                [self.total(side, lambda part: part[step]) for side in sides], axis=-1
            )
            arrived.append(hop(tied(upper.astype(jnp.bfloat16), others), ("dp", 4 * step)))
        self.result = sum([mine] + [part.astype(jnp.float32) for part in arrived])
        return [self.result]


class WholeScattering:
    def __init__(self, members, orders, sides):
        self.begun = [members[-1][0]]
        mine = [
            lax.psum_scatter(
                whole.reshape(-1, whole.shape[2]), AXES, scatter_dimension=0, tiled=True
            ).astype(jnp.float32)
            for (whole,) in members
        ]
        taken = [mine[member][:, first:end] for side in sides for member, first, end in side]
        self.result = jnp.concatenate(taken, axis=-1)

    def core(self, *others):
        return []

    last = middle = far = core


def sum_over_all(member, routed):
    if not routed:
        return lax.psum(member, AXES)
    total = member
    for dim in (CORE, ("dp", 2), ("tensor", 1)):
        total = total + hop(total, dim)
    parts = [total] + [hop(total, ("dp", bit)) for bit in range(4, lax.axis_size("dp"), 4)]
    far_place = lax.axis_index("dp") // 4
    stacked = jnp.stack(parts)
    return sum(stacked[far_place ^ step] for step in range(len(parts)))


def load_piece(meta, piece, sources, target, columns, sems):
    if len(sources) == 1:
        for half_at in range(2):
            pltpu.make_async_copy(
                sources[0].at[half_at, :, piece.columns], target.at[half_at, :, columns],
                sems.at[half_at],
            ).start()
        return
    table = slot_table(piece.order)
    half = len(table) // 2
    block_rows = sources[0].shape[1]
    for slot, (dp_part, tensor_part) in enumerate(table):
        for core in range(2):
            source = sources[2 * core + slot // half]
            place = meta[0] ^ (dp_part ^ core)
            half_at = meta[1] ^ tensor_part
            rows = pl.ds(pl.multiple_of(place * block_rows, TILE_ROWS), block_rows)
            pltpu.make_async_copy(
                source.at[slot % half, :, piece.columns],
                target.at[half_at, rows, columns],
                sems.at[half_at],
            ).start()


def await_piece(target, half_at, columns, sems):
    view = target.at[half_at, :, columns]
    pltpu.make_async_copy(view, view, sems.at[half_at]).wait()


def store_piece(meta, source, targets, order, relative_half, columns, sem):
    if len(targets) == 1:
        pltpu.make_async_copy(
            source, targets[0].at[meta[1] ^ relative_half, :, columns], sem
        ).start()
        return
    block_rows = targets[0].shape[1]
    tensor_weight = 2 ** order.index(("tensor", 1))
    for slot, (dp_part, tensor_part) in enumerate(slot_table(order)):
        if tensor_part:
            continue
        for core in range(2):
            place = meta[0] ^ (dp_part ^ core)
            rows = pl.ds(pl.multiple_of(place * block_rows, TILE_ROWS), block_rows)
            pltpu.make_async_copy(
                source.at[rows, :],
                targets[core].at[slot + tensor_weight * relative_half, :, columns],
                sem,
            ).start()


def take(refs, *counts):
    groups, at = [], 0
    for count in counts:
        groups.append(refs[at] if count is None else refs[at : at + count])
        at += 1 if count is None else count
    return groups


def await_stored(source, sem):
    pltpu.make_async_copy(source, source, sem).wait()


def norm_stats(residual):
    centered = residual - jnp.mean(residual, axis=-1, keepdims=True)
    inv_spread = lax.rsqrt(jnp.mean(centered * centered, axis=-1, keepdims=True) + norm_eps)
    return centered * inv_spread, inv_spread


def norm_back(gradient, normed, inv_spread, gain):
    scaled = gradient * gain
    inner = jnp.mean(scaled * normed, axis=-1, keepdims=True)
    return inv_spread * (scaled - jnp.mean(scaled, axis=-1, keepdims=True) - normed * inner)


def row_tiles(row_count):
    tile = min(ROW_TILE, row_count)
    return [slice(start, start + tile) for start in range(0, row_count, tile)]


def column_sum(member):
    return jnp.sum(member, axis=0, keepdims=True)


def gelu_parts(inputs):
    bell = jnp.exp(-0.5 * inputs * inputs)
    ratio = 1.0 / (1.0 + erf_slope * jnp.abs(inputs))
    series = 0.5 * erf_terms[0]
    for term in erf_terms[1:]:
        series = series * ratio + 0.5 * term
    tail = series * ratio * bell
    below = jnp.where(inputs < 0, tail, 1.0 - tail)
    return inputs * below, below + inputs * (bell * inv_root_tau)


def load_qkv(meta, pieces, sources, weights, columns, sems):
    load_piece(meta, pieces[0], sources[0], weights, slice(0, 2 * columns), sems[0])
    load_piece(meta, pieces[1], sources[1], weights, slice(2 * columns, 3 * columns), sems[1])


def await_qkv(weights, half_at, columns, sems):
    await_piece(weights, half_at, slice(0, 2 * columns), sems[0])
    await_piece(weights, half_at, slice(2 * columns, 3 * columns), sems[1])


def qkv_forward_kernel(pieces, meta, inputs, bias, *refs):
    qk_sources, v_sources, out, weights, *sems = take(
        refs, len(pieces[0].arrays), len(pieces[1].arrays), None, None, None, None
    )
    step = pl.program_id(0)
    columns = out.shape[2]

    @pl.when(step == 0)
    def _():
        load_qkv(meta, pieces, (qk_sources, v_sources), weights, columns, sems)

    half_at = meta[1] ^ (step // 3)

    @pl.when(step % 3 == 0)
    def _():
        await_qkv(weights, half_at, columns, sems)

    which = pl.ds(pl.multiple_of((step % 3) * columns, 128), columns)
    for rows in row_tiles(inputs.shape[0]):
        out[0, rows, :] = (dot_nn(inputs[rows, :], weights[half_at, :, which]) + bias[0]).astype(
            jnp.bfloat16
        )


def slab_features(meta, slab, slab_rows, k_side, q_side):
    segment_rows = slab_rows // 4
    row = lax.broadcasted_iota(jnp.int32, (slab_rows, PAIR), 0)
    lane = lax.broadcasted_iota(jnp.int32, (slab_rows, PAIR), 1) & (HEAD_DIM - 1)
    short = meta[2 + slab] == 0
    segment = jnp.where(short, row // segment_rows, 0)
    offset = row - segment * segment_rows
    base = 2 + meta_slabs(meta) + 4 * slab
    length = jnp.where(
        segment == 0,
        meta[base],
        jnp.where(segment == 1, meta[base + 1], jnp.where(segment == 2, meta[base + 2], meta[base + 3])),
    )
    same = segment == lane
    k_value = jnp.where(lane < 4, jnp.where(same, 1.0, 0.0), jnp.where(offset >= length, 1.0, 0.0))
    q_value = jnp.where(lane < 4, jnp.where(same, 0.0, big_negative), big_negative)
    k_side[slab] = jnp.where(lane < 5, k_value, 0.0).astype(jnp.bfloat16)
    q_side[slab] = jnp.where(lane < 5, q_value, 0.0).astype(jnp.bfloat16)


def meta_slabs(meta):
    return (meta.shape[0] - 2) // 5


def lane_low(row_count):
    return lax.broadcasted_iota(jnp.int32, (row_count, PAIR), 1) < HEAD_DIM


def attention_forward_kernel(meta, qkv, mixed, logsum, k_side, q_side):
    slab, pair = pl.program_id(1), pl.program_id(0)
    slab_rows = qkv.shape[1]

    @pl.when(pair == 0)
    def _():
        slab_features(meta, slab, slab_rows, k_side, q_side)

    low = lane_low(slab_rows)
    query, key = qkv[0].astype(jnp.float32), qkv[1].astype(jnp.float32)
    k_extra, q_extra = k_side[slab].astype(jnp.float32), q_side[slab].astype(jnp.float32)
    value_flip = flipped(qkv[2])
    sub = lax.broadcasted_iota(jnp.int32, (PAIR, slab_rows), 0)
    outcomes = []
    for head in range(2):
        mine = low if head == 0 else jnp.logical_not(low)
        q_head = jnp.where(mine, query, q_extra).astype(jnp.bfloat16)
        k_head = jnp.where(mine, key, k_extra).astype(jnp.bfloat16)
        scores = dot_nt(k_head, q_head)
        top = jnp.max(scores, axis=0, keepdims=True)
        weight = jnp.exp2((scores - top) * exponent_scale).astype(jnp.bfloat16)
        sum_row = HEAD_DIM if head == 0 else 0
        kept = sub < HEAD_DIM if head == 0 else sub >= HEAD_DIM
        v_head = jnp.where(kept, value_flip, jnp.where(sub == sum_row, 1.0, 0.0))
        blend = dot_nn(v_head.astype(jnp.bfloat16), weight)
        total = blend[sum_row : sum_row + 1, :]
        logsum[0, 0, head : head + 1, :] = top * exponent_scale + jnp.log(total) * log2_e
        outcomes.append(blend / total)
    mixed[...] = jnp.where(sub < HEAD_DIM, outcomes[0], outcomes[1]).T.astype(jnp.bfloat16)


def ffn_forward_kernel(pieces, meta, mixed, inputs, vectors, ffn_bias, *refs):
    out_sources, in_sources, down_sources, outputs, scratch = take(
        refs, *[len(piece.arrays) for piece in pieces], 8, 7
    )
    hidden, normed_one, spread_one, activated, slope, result, normed_two, spread_two = outputs
    out_whole, in_whole, down_whole, total, out_sems, in_sems, down_sems = scratch
    step = pl.program_id(0)
    steps = pl.num_programs(0)
    everything = slice(None)
    out_columns = out_whole.shape[2]
    tiles = row_tiles(inputs.shape[0])
    lanes = spread_one.shape[1]

    @pl.when(step == 0)
    def _():
        load_piece(meta, pieces[0], out_sources, out_whole, everything, out_sems)
        load_piece(meta, pieces[1], in_sources, in_whole, everything, in_sems)
        load_piece(meta, pieces[2], down_sources, down_whole, everything, down_sems)
        for half_at in range(2):
            await_piece(out_whole, half_at, everything, out_sems)
        for rows in tiles:
            attention_out = vectors[0:1, :]
            for half_at in range(2):
                columns = slice(half_at * out_columns, (half_at + 1) * out_columns)
                attention_out = attention_out + dot_nt(mixed[rows, columns], out_whole[half_at])
            normed, spread = norm_stats(inputs[rows, :].astype(jnp.float32) + attention_out)
            low = (normed * vectors[2:3, :] + vectors[4:5, :]).astype(jnp.bfloat16)
            hidden[rows, :] = low
            normed_one[rows, :] = normed.astype(jnp.bfloat16)
            spread_one[rows, :] = jnp.broadcast_to(spread, (spread.shape[0], lanes))
            total[rows, :] = low.astype(jnp.float32) + vectors[1:2, :]

    half_at = meta[1] ^ (step // FFN_PARTS)
    width = activated.shape[1]
    part = pl.ds(pl.multiple_of((step % FFN_PARTS) * width, 128), width)

    @pl.when(step % FFN_PARTS == 0)
    def _():
        await_piece(in_whole, half_at, everything, in_sems)
        await_piece(down_whole, half_at, everything, down_sems)

    for rows in tiles:
        pre_gelu = dot_nn(hidden[rows, :], in_whole[half_at, :, part]) + ffn_bias[0]
        value, steep = gelu_parts(pre_gelu)
        low = value.astype(jnp.bfloat16)
        activated[rows, :] = low
        slope[rows, :] = steep.astype(jnp.bfloat16)
        total[rows, :] += dot_nt(low, down_whole[half_at, :, part])

    @pl.when(step == steps - 1)
    def _():
        for rows in tiles:
            normed, spread = norm_stats(total[rows, :])
            result[rows, :] = (normed * vectors[3:4, :] + vectors[5:6, :]).astype(jnp.bfloat16)
            normed_two[rows, :] = normed.astype(jnp.bfloat16)
            spread_two[rows, :] = jnp.broadcast_to(spread, (spread.shape[0], lanes))


def ffn_backward_kernel(
    pieces, target_count, meta, gradient, normed_two, spread_two, hidden, normed_one, spread_one,
    activated, slope, vectors, *refs
):
    in_sources, down_sources, outputs, targets, scratch = take(
        refs, *[len(piece.arrays) for piece in pieces], 4, target_count, 11
    )
    attention_grad, resid_grad, sums, bias_sums = outputs
    (
        in_whole, down_whole, total, branch, branch_flip, hidden_flip, pre_part, grad_parts,
        in_sems, down_sems, out_sems,
    ) = scratch
    step = pl.program_id(0)
    steps = pl.num_programs(0)
    everything = slice(None)
    tiles = row_tiles(hidden.shape[0])
    slot = step % 2

    @pl.when(step == 0)
    def _():
        load_piece(meta, pieces[0], in_sources, in_whole, everything, in_sems)
        load_piece(meta, pieces[1], down_sources, down_whole, everything, down_sems)
        gain_sum, shift_sum, branch_sum = 0.0, 0.0, 0.0
        for rows in tiles:
            grad = gradient[rows, :].astype(jnp.float32)
            normed = normed_two[rows, :].astype(jnp.float32)
            resid = norm_back(grad, normed, spread_two[rows, 0:1], vectors[3:4, :])
            low = resid.astype(jnp.bfloat16)
            total[rows, :] = resid
            branch[rows, :] = low
            branch_flip[:, rows] = flipped(low).astype(jnp.bfloat16)
            hidden_flip[:, rows] = flipped(hidden[rows, :]).astype(jnp.bfloat16)
            gain_sum += column_sum(grad * normed)
            shift_sum += column_sum(grad)
            branch_sum += column_sum(low.astype(jnp.float32))
        sums[...] = jnp.zeros(sums.shape, jnp.float32)
        sums[1:2, :] = branch_sum
        sums[3:4, :] = gain_sum
        sums[5:6, :] = shift_sum

    half_at = meta[1] ^ (step // FFN_PARTS)
    width = activated.shape[1]
    part = pl.ds(pl.multiple_of((step % FFN_PARTS) * width, 128), width)

    @pl.when(step % FFN_PARTS == 0)
    def _():
        await_piece(in_whole, half_at, everything, in_sems)
        await_piece(down_whole, half_at, everything, down_sems)

    @pl.when(step >= 2)
    def _():
        await_stored(grad_parts.at[slot, 0], out_sems.at[slot, 0])
        await_stored(grad_parts.at[slot, 1], out_sems.at[slot, 1])

    grad_parts[slot, 1] = dot_nn(branch_flip[...], activated[...]).astype(jnp.bfloat16)
    down_part = pl.ds(pl.multiple_of(FFN_PARTS * width + (step % FFN_PARTS) * width, 128), width)
    store_piece(
        meta, grad_parts.at[slot, 1], targets, pieces[1].order, step // FFN_PARTS, down_part,
        out_sems.at[slot, 1],
    )
    bias_sum = 0.0
    for rows in tiles:
        active_grad = dot_nn(branch[rows, :], down_whole[half_at, :, part])
        low = (active_grad * slope[rows, :].astype(jnp.float32)).astype(jnp.bfloat16)
        pre_part[rows, :] = low
        bias_sum += column_sum(low.astype(jnp.float32))
        total[rows, :] += dot_nt(low, in_whole[half_at, :, part])
    bias_sums[0] = bias_sum
    grad_parts[slot, 0] = dot_nn(hidden_flip[...], pre_part[...]).astype(jnp.bfloat16)
    store_piece(
        meta, grad_parts.at[slot, 0], targets, pieces[0].order, step // FFN_PARTS, part,
        out_sems.at[slot, 0],
    )

    @pl.when(step == steps - 1)
    def _():
        gain_sum, shift_sum, branch_sum = 0.0, 0.0, 0.0
        for rows in tiles:
            grad = total[rows, :]
            normed = normed_one[rows, :].astype(jnp.float32)
            resid = norm_back(grad, normed, spread_one[rows, 0:1], vectors[2:3, :])
            low = resid.astype(jnp.bfloat16)
            resid_grad[rows, :] = resid
            attention_grad[rows, :] = low
            gain_sum += column_sum(grad * normed)
            shift_sum += column_sum(grad)
            branch_sum += column_sum(low.astype(jnp.float32))
        sums[0:1, :] = branch_sum
        sums[2:3, :] = gain_sum
        sums[4:5, :] = shift_sum
        for late in range(2):
            await_stored(grad_parts.at[late, 0], out_sems.at[late, 0])
            await_stored(grad_parts.at[late, 1], out_sems.at[late, 1])


def out_backward_kernel(pieces, order, target_count, meta, attention_grad, mixed, *refs):
    sources, mixed_grad, targets, scratch = take(
        refs, len(pieces[0].arrays), None, target_count, 5
    )
    out_whole, grad_flip, grad_parts, load_sems, out_sems = scratch
    step = pl.program_id(0)
    columns = mixed.shape[1]
    everything = slice(None)
    tiles = row_tiles(mixed.shape[0])

    @pl.when(step == 0)
    def _():
        load_piece(meta, pieces[0], sources, out_whole, everything, load_sems)
        for rows in tiles:
            grad_flip[:, rows] = flipped(attention_grad[rows, :]).astype(jnp.bfloat16)

    half_at = meta[1] ^ step
    grad_parts[step] = dot_nn(grad_flip[...], mixed[...]).astype(jnp.bfloat16)
    store_piece(meta, grad_parts.at[step], targets, order, step, everything, out_sems.at[step])
    await_piece(out_whole, half_at, everything, load_sems)
    for rows in tiles:
        mixed_grad[rows, :] = dot_nn(attention_grad[rows, :], out_whole[half_at]).astype(
            jnp.bfloat16
        )

    @pl.when(step == 1)
    def _():
        for late in range(2):
            await_stored(grad_parts.at[late], out_sems.at[late])


def attention_backward_kernel(meta, qkv, mixed, mixed_grad, logsum, grads, sums, k_side, q_side):
    slab, pair = pl.program_id(1), pl.program_id(0)
    slab_rows = qkv.shape[1]

    @pl.when(pair == 0)
    def _():
        slab_features(meta, slab, slab_rows, k_side, q_side)

    low = lane_low(slab_rows)
    query, key, value = (qkv[place].astype(jnp.float32) for place in range(3))
    k_extra, q_extra = k_side[slab].astype(jnp.float32), q_side[slab].astype(jnp.float32)
    grad_low = mixed_grad[...]
    grad = grad_low.astype(jnp.float32)
    product = (grad * mixed[...].astype(jnp.float32)).T
    key_flip = key.T
    sub = lax.broadcasted_iota(jnp.int32, (PAIR, slab_rows), 0)
    query_flip, key_grad, value_grad = 0.0, 0.0, 0.0
    for head in range(2):
        mine = low if head == 0 else jnp.logical_not(low)
        kept = sub < HEAD_DIM if head == 0 else sub >= HEAD_DIM
        span = slice(head * HEAD_DIM, (head + 1) * HEAD_DIM)
        q_head = jnp.where(mine, query, q_extra).astype(jnp.bfloat16)
        k_head = jnp.where(mine, key, k_extra).astype(jnp.bfloat16)
        v_head = jnp.where(mine, value, 0.0).astype(jnp.bfloat16)
        probs = jnp.exp2(
            dot_nt(k_head, q_head) * exponent_scale - logsum[0, 0, head : head + 1, :]
        )
        delta = column_sum(product[span, :])
        raw_grad = (probs * (dot_nt(v_head, grad_low) - delta)).astype(jnp.bfloat16)
        g_head = jnp.where(mine, grad, 0.0).astype(jnp.bfloat16)
        value_grad += dot_nn(probs.astype(jnp.bfloat16), g_head)
        key_grad += dot_nn(raw_grad, jnp.where(mine, query, 0.0).astype(jnp.bfloat16))
        query_flip += dot_nn(jnp.where(kept, key_flip, 0.0).astype(jnp.bfloat16), raw_grad)
    query_low = (query_flip * score_scale).T.astype(jnp.bfloat16)
    value_low = value_grad.astype(jnp.bfloat16)
    grads[0] = query_low
    grads[1] = (key_grad * score_scale).astype(jnp.bfloat16)
    grads[2] = value_low

    @pl.when(slab == 0)
    def _():
        sums[...] = jnp.zeros(sums.shape, jnp.float32)

    sums[0:1, :] += column_sum(query_low.astype(jnp.float32))
    sums[1:2, :] += column_sum(value_low.astype(jnp.float32))


def qkv_grad_kernel(orders, target_count, meta, inputs, grads, *refs):
    targets, (inputs_flip, grad_parts, out_sems) = take(refs, target_count, 3)
    step = pl.program_id(0)
    steps = pl.num_programs(0)
    columns = grads.shape[2]
    slot = step % 2
    which = step % 3

    @pl.when(step == 0)
    def _():
        for rows in row_tiles(inputs.shape[0]):
            inputs_flip[:, rows] = flipped(inputs[rows, :]).astype(jnp.bfloat16)

    @pl.when(step >= 2)
    def _():
        await_stored(grad_parts.at[slot], out_sems.at[slot])

    grad_parts[slot] = dot_nn(inputs_flip[...], grads[0]).astype(jnp.bfloat16)
    span = pl.ds(pl.multiple_of(which * columns, 128), columns)

    @pl.when(which == 0)
    def _():
        store_piece(
            meta, grad_parts.at[slot], targets, orders[0], step // 3, span, out_sems.at[slot]
        )

    @pl.when(which > 0)
    def _():
        store_piece(
            meta, grad_parts.at[slot], targets, orders[1], step // 3, span, out_sems.at[slot]
        )

    @pl.when(step == steps - 1)
    def _():
        for late in range(2):
            await_stored(grad_parts.at[late], out_sems.at[late])


def input_grad_kernel(pieces, meta, grads, resid_grad, *refs):
    qk_sources, v_sources, input_grad, weights, *sems = take(
        refs, len(pieces[0].arrays), len(pieces[1].arrays), None, None, None, None
    )
    step = pl.program_id(0)
    columns = grads.shape[2]
    tiles = row_tiles(resid_grad.shape[0])

    @pl.when(step == 0)
    def _():
        load_qkv(meta, pieces, (qk_sources, v_sources), weights, columns, sems)
        for rows in tiles:
            input_grad[rows, :] = resid_grad[rows, :]

    half_at = meta[1] ^ (step // 3)

    @pl.when(step % 3 == 0)
    def _():
        await_qkv(weights, half_at, columns, sems)

    span = pl.ds(pl.multiple_of((step % 3) * columns, 128), columns)
    for rows in tiles:
        input_grad[rows, :] += dot_nt(grads[0, rows, :], weights[half_at, :, span])


def fixed(shape):
    return pl.BlockSpec(
        shape, lambda *_: (0,) * len(shape), pipeline_mode=pl.Buffered(1)
    )


def fixed_out(shape):
    return pl.BlockSpec(shape, lambda *_: (0,) * len(shape))


ANYWHERE = pl.BlockSpec(memory_space=pl.ANY)


def run_kernel(kernel, meta, grid, ins, outs, scratch, flops, moved, name, after=()):
    used = len(ins)
    ins = list(ins) + [(ANYWHERE, member) for member in after]
    in_specs, operands = zip(*ins)
    out_specs, out_shapes = zip(*outs)

    def body(meta_ref, *refs):
        kernel(meta_ref, *refs[:used], *refs[len(ins) :])

    return pl.pallas_call(
        body,
        grid_spec=pltpu.PrefetchScalarGridSpec(
            num_scalar_prefetch=1,
            grid=grid,
            in_specs=list(in_specs),
            out_specs=list(out_specs),
            scratch_shapes=scratch,
        ),
        out_shape=list(out_shapes),
        compiler_params=pltpu.CompilerParams(vmem_limit_bytes=VMEM_LIMIT),
        cost_estimate=pl.CostEstimate(flops=COST_WEIGHT * flops, bytes_accessed=moved, transcendentals=0),
        name=name,
    )(meta, *operands)


def low_shape(*shape):
    return jax.ShapeDtypeStruct(shape, jnp.bfloat16)


def full_shape(*shape):
    return jax.ShapeDtypeStruct(shape, jnp.float32)


def pair_sems():
    return pltpu.SemaphoreType.DMA((2,))


def half_of(step, meta, count):
    return meta[1] ^ (step // count)


def sources_of(pieces):
    return [(ANYWHERE, member) for piece in pieces for member in piece.arrays]


def targets_of(routed, split, width, block_rows, columns):
    if routed:
        shape = low_shape(split * width // (2 * block_rows), block_rows, columns)
        return [(ANYWHERE, shape), (ANYWHERE, shape)]
    return [(ANYWHERE, low_shape(split, width, columns))]


def qkv_forward(meta, inputs, bias, pieces, after=()):
    rows, width = inputs.shape
    columns = width // 2
    (qkv,) = run_kernel(
        functools.partial(qkv_forward_kernel, pieces),
        meta,
        (6,),
        [
            (fixed((rows, width)), inputs),
            (
                pl.BlockSpec((1, 1, columns), lambda i, m: ((i % 3) * 2 + half_of(i, m, 3), 0, 0)),
                bias,
            ),
        ]
        + sources_of(pieces),
        [
            (
                pl.BlockSpec((1, rows, columns), lambda i, m: (i % 3, 0, half_of(i, m, 3))),
                low_shape(3, rows, width),
            )
        ],
        [pltpu.VMEM((2, width, 3 * columns), jnp.bfloat16), pair_sems(), pair_sems()],
        6 * rows * width * width,
        8 * rows * width + 6 * width * width,
        "qkv_forward",
        after,
    )
    return qkv


def attention_forward(meta, qkv, slab_count, after=()):
    _, rows, width = qkv.shape
    slab_rows = rows // slab_count
    pairs = width // PAIR
    return run_kernel(
        attention_forward_kernel,
        meta,
        (pairs, slab_count),
        [(pl.BlockSpec((3, slab_rows, PAIR), lambda p, s, m: (0, s, p)), qkv)],
        [
            (pl.BlockSpec((slab_rows, PAIR), lambda p, s, m: (s, p)), low_shape(rows, width)),
            (
                pl.BlockSpec((1, 1, 8, slab_rows), lambda p, s, m: (s, p, 0, 0)),
                full_shape(slab_count, pairs, 8, slab_rows),
            ),
        ],
        [pltpu.VMEM((slab_count, slab_rows, PAIR), jnp.bfloat16)] * 2,
        16 * rows * slab_rows * width,
        8 * rows * width,
        "attention_forward",
        after,
    )


def ffn_forward(meta, mixed, inputs, vectors, ffn_bias, pieces, after=()):
    rows, width = inputs.shape
    half_width = pieces[1].count
    part = half_width // FFN_PARTS

    def part_at(i, m):
        return half_of(i, m, FFN_PARTS) * FFN_PARTS + i % FFN_PARTS

    whole_rows = (fixed_out((rows, width)), low_shape(rows, width))
    spread = (fixed_out((rows, 128)), full_shape(rows, 128))
    inner = (
        pl.BlockSpec((rows, part), lambda i, m: (0, part_at(i, m))),
        low_shape(rows, 2 * half_width),
    )
    return run_kernel(
        functools.partial(ffn_forward_kernel, pieces),
        meta,
        (2 * FFN_PARTS,),
        [
            (fixed((rows, width)), mixed),
            (fixed((rows, width)), inputs),
            (fixed((8, width)), vectors),
            (pl.BlockSpec((1, 1, part), lambda i, m: (part_at(i, m), 0, 0)), ffn_bias),
        ]
        + sources_of(pieces),
        [whole_rows, whole_rows, spread, inner, inner, whole_rows, whole_rows, spread],
        [
            pltpu.VMEM((2, width, width // 2), jnp.bfloat16),
            pltpu.VMEM((2, width, half_width), jnp.bfloat16),
            pltpu.VMEM((2, width, half_width), jnp.bfloat16),
            pltpu.VMEM((rows, width), jnp.float32),
            pair_sems(),
            pair_sems(),
            pair_sems(),
        ],
        8 * rows * width * half_width,
        24 * rows * width + 8 * width * half_width,
        "ffn_forward",
        after,
    )


def ffn_backward(meta, gradient, kept, vectors, pieces, targets, after=()):
    hidden, normed_one, spread_one, activated, slope, normed_two, spread_two = kept
    rows, width = hidden.shape
    half_width = pieces[0].count
    part = half_width // FFN_PARTS

    def part_at(i, m):
        return half_of(i, m, FFN_PARTS) * FFN_PARTS + i % FFN_PARTS

    low_rows = fixed((rows, width))
    spread = fixed((rows, 128))
    inner = pl.BlockSpec((rows, part), lambda i, m: (0, part_at(i, m)))
    return run_kernel(
        functools.partial(ffn_backward_kernel, pieces, len(targets)),
        meta,
        (2 * FFN_PARTS,),
        [
            (low_rows, gradient),
            (low_rows, normed_two),
            (spread, spread_two),
            (low_rows, hidden),
            (low_rows, normed_one),
            (spread, spread_one),
            (inner, activated),
            (inner, slope),
            (fixed((8, width)), vectors),
        ]
        + sources_of(pieces),
        [
            (fixed_out((rows, width)), low_shape(rows, width)),
            (fixed_out((rows, width)), full_shape(rows, width)),
            (fixed_out((8, width)), full_shape(8, width)),
            (
                pl.BlockSpec((1, 1, part), lambda i, m: (part_at(i, m), 0, 0)),
                full_shape(2 * FFN_PARTS, 1, part),
            ),
        ]
        + targets,
        [
            pltpu.VMEM((2, width, half_width), jnp.bfloat16),
            pltpu.VMEM((2, width, half_width), jnp.bfloat16),
            pltpu.VMEM((rows, width), jnp.float32),
            pltpu.VMEM((rows, width), jnp.bfloat16),
            pltpu.VMEM((width, rows), jnp.bfloat16),
            pltpu.VMEM((width, rows), jnp.bfloat16),
            pltpu.VMEM((rows, part), jnp.bfloat16),
            pltpu.VMEM((2, 2, width, part), jnp.bfloat16),
            pair_sems(),
            pair_sems(),
            pltpu.SemaphoreType.DMA((2, 2)),
        ],
        16 * rows * width * half_width,
        40 * rows * width + 16 * width * half_width,
        "ffn_backward",
        after,
    )


def out_backward(meta, attention_grad, mixed, piece, order, targets, after=()):
    rows, width = mixed.shape
    columns = width // 2
    half = pl.BlockSpec((rows, columns), lambda i, m: (0, half_of(i, m, 1)))
    return run_kernel(
        functools.partial(out_backward_kernel, [piece], order, len(targets)),
        meta,
        (2,),
        [(fixed((rows, width)), attention_grad), (half, mixed)] + sources_of([piece]),
        [(half, low_shape(rows, width))] + targets,
        [
            pltpu.VMEM((2, width, columns), jnp.bfloat16),
            pltpu.VMEM((width, rows), jnp.bfloat16),
            pltpu.VMEM((2, width, columns), jnp.bfloat16),
            pair_sems(),
            pair_sems(),
        ],
        4 * rows * width * width,
        6 * rows * width + 4 * width * width,
        "out_backward",
        after,
    )


def attention_backward(meta, qkv, mixed, mixed_grad, logsum, slab_count, after=()):
    _, rows, width = qkv.shape
    slab_rows = rows // slab_count
    pairs = width // PAIR
    three = pl.BlockSpec((3, slab_rows, PAIR), lambda p, s, m: (0, s, p))
    one = pl.BlockSpec((slab_rows, PAIR), lambda p, s, m: (s, p))
    return run_kernel(
        attention_backward_kernel,
        meta,
        (pairs, slab_count),
        [
            (three, qkv),
            (one, mixed),
            (one, mixed_grad),
            (pl.BlockSpec((1, 1, 8, slab_rows), lambda p, s, m: (s, p, 0, 0)), logsum),
        ],
        [
            (three, low_shape(3, rows, width)),
            (pl.BlockSpec((8, PAIR), lambda p, s, m: (0, p)), full_shape(8, width)),
        ],
        [pltpu.VMEM((slab_count, slab_rows, PAIR), jnp.bfloat16)] * 2,
        40 * rows * slab_rows * width,
        16 * rows * width,
        "attention_backward",
        after,
    )


def qkv_grad(meta, inputs, grads, orders, targets, after=()):
    rows, width = inputs.shape
    columns = width // 2
    return run_kernel(
        functools.partial(qkv_grad_kernel, orders, len(targets)),
        meta,
        (6,),
        [
            (fixed((rows, width)), inputs),
            (pl.BlockSpec((1, rows, columns), lambda i, m: (i % 3, 0, half_of(i, m, 3))), grads),
        ],
        targets,
        [
            pltpu.VMEM((width, rows), jnp.bfloat16),
            pltpu.VMEM((2, width, columns), jnp.bfloat16),
            pair_sems(),
        ],
        6 * rows * width * width,
        8 * rows * width + 6 * width * width,
        "qkv_grad",
        after,
    )


def input_gradient(meta, grads, resid_grad, pieces, after=()):
    rows, width = resid_grad.shape
    columns = width // 2
    (input_grad,) = run_kernel(
        functools.partial(input_grad_kernel, pieces),
        meta,
        (6,),
        [
            (pl.BlockSpec((1, rows, columns), lambda i, m: (i % 3, 0, half_of(i, m, 3))), grads),
            (fixed((rows, width)), resid_grad),
        ]
        + sources_of(pieces),
        [(fixed_out((rows, width)), full_shape(rows, width))],
        [pltpu.VMEM((2, width, 3 * columns), jnp.bfloat16), pair_sems(), pair_sems()],
        6 * rows * width * width,
        14 * rows * width + 6 * width * width,
        "input_gradient",
        after,
    )
    return input_grad


def both_halves(mine, theirs, place):
    first = jnp.concatenate([mine, theirs], axis=0)
    second = jnp.concatenate([theirs, mine], axis=0)
    return jnp.where(place == 0, first, second)


def on_device(
    tokens,
    cotangent,
    buckets,
    lengths,
    qkv_weight,
    qv_bias,
    out_weight,
    ffn_in_weight,
    ffn_in_bias,
    ffn_out_weight,
    out_bias,
    norm_gain,
    norm_bias,
):
    split = lax.axis_size("tensor")
    dp_size = lax.axis_size("dp")
    place = lax.axis_index("tensor")
    width = tokens.shape[1]
    rows = tokens.shape[0] // split
    slabs = buckets.shape[0] // split
    layer_count = qkv_weight.shape[0]
    block_rows = width // dp_size
    routed = block_rows % TILE_ROWS == 0 and dp_size & (dp_size - 1) == 0
    orders = hop_orders(dp_size if routed else PLANNED_BLOCKS)

    own_tokens = lax.dynamic_slice_in_dim(tokens, place * rows, rows)
    own_cotangent = lax.dynamic_slice_in_dim(cotangent, place * rows, rows)
    own_buckets = lax.dynamic_slice_in_dim(buckets, place * slabs, slabs)
    own_lengths = lax.dynamic_slice_in_dim(lengths, place * slabs, slabs)
    if routed:
        position = jnp.stack([lax.axis_index("dp"), place]).astype(jnp.int32)
    else:
        position = jnp.zeros((2,), jnp.int32)
    meta = jnp.concatenate([position, own_buckets, own_lengths.reshape(-1)])

    bias_flat = jnp.concatenate([qv_bias.reshape(layer_count, -1), ffn_in_bias], axis=1)
    bias_other = hop(bias_flat, ("tensor", 1))
    bias_halves = jnp.where(
        place == 0, jnp.stack([bias_flat, bias_other]), jnp.stack([bias_other, bias_flat])
    )
    qv_columns = qv_bias.shape[2]
    ffn_columns = ffn_in_bias.shape[1]

    def small_inputs(index):
        halves = bias_halves[:, index]
        value = halves[:, : 2 * qv_columns].reshape(2, 2, qv_columns)
        zero = jnp.zeros((2, qv_columns), jnp.float32)
        bias = jnp.stack([value[:, 0], zero, value[:, 1]]).reshape(6, 1, -1)
        vectors = jnp.concatenate(
            [out_bias[index], norm_gain[index], norm_bias[index], jnp.zeros((2, width), jnp.float32)]
        )
        return bias, vectors, halves[:, 2 * qv_columns :].reshape(2 * FFN_PARTS, 1, -1)

    def attention_weights(index, routed, *others):
        shard = jnp.concatenate([*qkv_weight[index], out_weight[index]], axis=1)
        return Gathering(shard, orders) if routed else WholeGathering(shard, orders, *others)

    def ffn_weights(index, routed, *others):
        shard = jnp.concatenate([ffn_in_weight[index], ffn_out_weight[index]], axis=1)
        return Gathering(shard, orders) if routed else WholeGathering(shard, orders, *others)

    def attention_split(pieces):
        return [pieces[0], pieces[1].narrow(0, width // 2)], pieces[1].narrow(width // 2, width // 2)

    hops = [[routed and flag for flag in flags] for flags in HOPS]
    hops_back = [[routed and flag for flag in flags] for flags in HOPS_BACK]

    def waits(flag, members):
        return list(members) if flag else []

    first, first_ffn = attention_weights(0, hops[0][0]), ffn_weights(0, hops[0][1])
    first.far()
    first.middle()
    last = waits(hops[0][0], first.last())
    first.core()
    second, second_ffn = attention_weights(1, hops[1][0], *last), ffn_weights(1, hops[1][1], *last)
    ffn_far = first_ffn.far()
    ffn_middle = first_ffn.middle()
    ffn_last = first_ffn.last()
    bias, vectors, ffn_bias = small_inputs(0)
    qkv_pieces, out_piece = attention_split(first.pieces())
    qkv = qkv_forward(meta, own_tokens, bias, qkv_pieces, waits(hops[0][1], ffn_middle))
    first_ffn.core(qkv)
    second_far = second.far(*last)
    second_middle = second.middle(qkv)
    mixed, logsum = attention_forward(
        meta, qkv, slabs, waits(hops[0][1], ffn_last) + waits(hops[1][0], second_far)
    )
    first_pieces = (qkv_pieces, out_piece, first_ffn.pieces())
    second_ffn_far = second_ffn.far(mixed)
    second_last = second.last(mixed)
    out = ffn_forward(
        meta, mixed, own_tokens, vectors, ffn_bias, [out_piece] + first_pieces[2],
        waits(hops[1][0], second_middle),
    )
    kept_layers = [(own_tokens, qkv, mixed, logsum, vectors, out)]
    layer_one = out[5]
    second.core(layer_one)
    second_ffn_middle = second_ffn.middle(layer_one)
    bias, vectors, ffn_bias = small_inputs(1)
    qkv_pieces, out_piece = attention_split(second.pieces())
    qkv = qkv_forward(
        meta, layer_one, bias, qkv_pieces,
        waits(hops[1][1], second_ffn_far) + waits(hops[1][0], second_last),
    )
    second_ffn.last(qkv)
    mixed, logsum = attention_forward(meta, qkv, slabs, waits(hops[1][1], second_ffn_middle))
    one_other = hop(tied(layer_one, [mixed]), ("tensor", 1))
    second_ffn.core(mixed)
    second_pieces = (qkv_pieces, out_piece, second_ffn.pieces())
    out = ffn_forward(
        meta, mixed, layer_one, vectors, ffn_bias, [out_piece] + second_pieces[2]
    )
    kept_layers.append((layer_one, qkv, mixed, logsum, vectors, out))
    layer_two = out[5]
    two_other = hop(layer_two, ("tensor", 1))

    def targets(flag, columns):
        return targets_of(flag, split, width, block_rows, columns)

    def scattering(flag, members, sides):
        kind = Scattering if flag else WholeScattering
        return kind(members, orders, sides)

    half_ffn = first_ffn.width

    def ffn_back(index, gradient, pieces, after=()):
        inputs, qkv, mixed, logsum, vectors, out = kept_layers[index]
        hidden, normed_one, spread_one, activated, slope, _, normed_two, spread_two = out
        kept = (hidden, normed_one, spread_one, activated, slope, normed_two, spread_two)
        attention_grad, resid_grad, sums, ffn_sums, *members = ffn_backward(
            meta, gradient, kept, vectors, pieces[2], targets(hops_back[index][1], 2 * half_ffn), after
        )
        scatter = scattering(
            hops_back[index][1], [members], [[(0, 0, half_ffn)], [(0, half_ffn, 2 * half_ffn)]]
        )
        return attention_grad, resid_grad, (sums, ffn_sums), scatter

    def out_back(index, attention_grad, pieces, after=()):
        mixed = kept_layers[index][2]
        return out_backward(
            meta, attention_grad, mixed, pieces[1], orders[0], targets(hops_back[index][0], width // 2), after
        )

    def attention_back(index, mixed_grad, after=()):
        _, qkv, mixed, logsum, _, _ = kept_layers[index]
        return attention_backward(meta, qkv, mixed, mixed_grad, logsum, slabs, after)

    def qkv_grads(index, grads, out_members, after=()):
        members = qkv_grad(
            meta, kept_layers[index][0], grads, orders,
            targets(hops_back[index][0], 3 * width // 2), after,
        )
        columns = width // 2
        return scattering(
            hops_back[index][0],
            [out_members, members],
            [[(0, 0, columns), (1, 0, columns)], [(1, columns, 3 * columns)]],
        )

    def flat_smalls(sums, ffn_sums, qkv_sums):
        return jnp.concatenate(
            [sums[:6].reshape(-1), qkv_sums[:2].reshape(-1), ffn_sums.reshape(-1)]
        )

    attention_grad, resid_grad, sums, ffn_one = ffn_back(1, own_cotangent, second_pieces, [one_other])
    layer_one_whole = both_halves(layer_one, one_other, place)
    ffn_core = ffn_one.core()
    mixed_grad, *out_members = out_back(1, attention_grad, second_pieces, [two_other])
    layer_two_whole = both_halves(layer_two, two_other, place)
    grads, qkv_sums = attention_back(1, mixed_grad, ffn_core)
    smalls_one = flat_smalls(*sums, qkv_sums)
    ffn_last = ffn_one.last(mixed_grad)
    attention_one = qkv_grads(1, grads, out_members, waits(hops_back[1][1], ffn_last))
    attention_core = attention_one.core()
    gradient = input_gradient(meta, grads, resid_grad, second_pieces[0], attention_one.begun)
    ffn_middle = ffn_one.middle(gradient)
    attention_last = attention_one.last(gradient)
    attention_grad, resid_grad, sums, ffn_zero = ffn_back(
        0, gradient, first_pieces, waits(hops_back[1][1], ffn_middle) + attention_core
    )
    ffn_far = ffn_one.far(attention_grad)
    ffn_core = ffn_zero.core()
    attention_middle = attention_one.middle(attention_grad)
    mixed_grad, *out_members = out_back(
        0, attention_grad, first_pieces, waits(hops_back[1][0], attention_last)
    )
    ffn_last = ffn_zero.last(mixed_grad)
    attention_far = attention_one.far(mixed_grad)
    grads, qkv_sums = attention_back(
        0, mixed_grad, ffn_core + waits(hops_back[1][0], attention_middle)
    )
    smalls_zero = flat_smalls(*sums, qkv_sums)
    ffn_middle = ffn_zero.middle(grads)
    before = ffn_last + waits(hops_back[1][0], attention_far) + waits(hops_back[1][1], ffn_far)
    if LATE_WEIGHTS:
        gradient = input_gradient(meta, grads, resid_grad, first_pieces[0], before)
        attention_zero = qkv_grads(0, grads, out_members, [gradient, *ffn_middle])
        attention_zero.core()
    else:
        attention_zero = qkv_grads(0, grads, out_members, before)
        attention_zero.core()
        gradient = input_gradient(
            meta, grads, resid_grad, first_pieces[0], attention_zero.begun + ffn_middle
        )
    ffn_zero.far()
    attention_last = attention_zero.last(gradient)
    attention_zero.middle()
    attention_zero.far()

    low_gradient = gradient.astype(jnp.bfloat16)
    if HOLD_TOKENS:
        low_gradient = tied(low_gradient, waits(hops_back[0][0], attention_last))
    token_grad = both_halves(
        gradient, hop(low_gradient, ("tensor", 1)).astype(jnp.float32), place
    )
    matrix_grads = []
    for attention, ffn in ((attention_zero, ffn_zero), (attention_one, ffn_one)):
        out_part, *qkv_parts = jnp.split(attention.result, 4, axis=1)
        matrix_grads.append((jnp.stack(qkv_parts), out_part, *jnp.split(ffn.result, 2, axis=1)))
    smalls = tied(jnp.stack([smalls_zero, smalls_one]), [gradient])
    smalls = sum_over_all(smalls, routed)
    eight = smalls[:, : 8 * width].reshape(layer_count, 4, 2, width)
    ffn_total = smalls[:, 8 * width :]
    return (
        layer_one_whole,
        layer_two_whole,
        token_grad,
        jnp.stack([member[0] for member in matrix_grads]),
        lax.dynamic_slice_in_dim(eight[:, 3], place * qv_columns, qv_columns, axis=2),
        jnp.stack([member[1] for member in matrix_grads]),
        jnp.stack([member[2] for member in matrix_grads]),
        lax.dynamic_slice_in_dim(ffn_total, place * ffn_columns, ffn_columns, axis=1),
        jnp.stack([member[3] for member in matrix_grads]),
        eight[:, 0],
        eight[:, 1],
        eight[:, 2],
    )


def solution(mesh):
    placed = (
        P("dp", None),
        P("dp", None),
        P("dp"),
        P("dp", None),
        P(None, None, "dp", "tensor"),
        P(None, None, "tensor"),
        P(None, "dp", "tensor"),
        P(None, "dp", "tensor"),
        P(None, "tensor"),
        P(None, "dp", "tensor"),
        P(),
        P(),
        P(),
    )
    return jax.shard_map(
        on_device,
        mesh=mesh,
        in_specs=placed,
        out_specs=(
            P("dp", None),
            P("dp", None),
            P("dp", None),
            P(None, None, "dp", "tensor"),
            P(None, None, "tensor"),
            P(None, "dp", "tensor"),
            P(None, "dp", "tensor"),
            P(None, "tensor"),
            P(None, "dp", "tensor"),
            P(),
            P(),
            P(),
        ),
        check_vma=False,
    )
```

```python
import functools

import jax
import jax.numpy as jnp
from jax import lax
from jax.experimental import pallas as pl
from jax.experimental.pallas import tpu as pltpu
from jax.sharding import PartitionSpec as P

HEAD_DIM = 64
PAIR = 2 * HEAD_DIM
AXES = ("tensor", "dp")
CORE = ("dp", 1)
FFN_PARTS = 2
ROW_TILE = 512
TILE_ROWS = 16
PLANNED_BLOCKS = 16
HOPS_BACK = ((True, True), (True, False))
COST_WEIGHT = 8
BACK_WEIGHT = 16
SPLIT_DOWN = False
HOLD_TOKENS = True
VMEM_LIMIT = 58 * 1024 * 1024

norm_eps = 1e-06
big_negative = -1e30
inv_root_tau = 0.3989422804014327
log2_e = 1.4426950408889634
score_scale = HEAD_DIM ** (-0.5)
exponent_scale = score_scale * log2_e
erf_slope = 0.3275911 * 0.7071067811865476
erf_terms = (1.061405429, -1.453152027, 1.421413741, -0.284496736, 0.254829592)


def dot_nn(left, right):
    return lax.dot_general(
        left, right, (((1,), (0,)), ((), ())), preferred_element_type=jnp.float32
    )


def dot_nt(left, right):
    return lax.dot_general(
        left, right, (((1,), (1,)), ((), ())), preferred_element_type=jnp.float32
    )


def flipped(member):
    return member.astype(jnp.float32).T


def hop_orders(block_count):
    far = []
    bit = 4
    while bit < block_count:
        far.append(("dp", bit))
        bit *= 2
    across, along = ("dp", 2), ("tensor", 1)
    return (far + [across, along], far + [along, across])


def slot_table(order):
    table = []
    for slot in range(2 ** len(order)):
        dp_part, tensor_part = 0, 0
        for position, (axis, bit) in enumerate(order):
            if slot >> position & 1:
                if axis == "dp":
                    dp_part ^= bit
                else:
                    tensor_part ^= bit
        table.append((dp_part, tensor_part))
    return table


def hop(member, dim):
    axis, bit = dim
    pairs = [(place, place ^ bit) for place in range(lax.axis_size(axis))]
    return lax.ppermute(member, axis, pairs)


def tied(member, others):
    return lax.optimization_barrier((member, *others))[0] if others else member


class Piece:
    def __init__(self, arrays, order, first, count):
        self.arrays, self.order, self.columns = tuple(arrays), order, slice(first, first + count)
        self.count = count

    def narrow(self, first, count):
        return Piece(self.arrays, self.order, self.columns.start + first, count)


class Joined:
    def __init__(self, parts):
        self.parts, self.count = tuple(parts), sum(part.count for part in parts)
        self.arrays = tuple(member for part in parts for member in part.arrays)


class Gathering:
    def __init__(self, shard, orders):
        self.shard, self.orders, self.width = shard[None], orders, shard.shape[1] // 2

    def halves(self, member):
        return [member[..., : self.width], member[..., self.width :]]

    def send_far(self, *others):
        shard = tied(self.shard, others)
        count = 2 ** (len(self.orders[0]) - 2)
        self.coming = [hop(shard, ("dp", 4 * step)) for step in range(1, count)]

    def land_far(self, *others):
        parts = [self.shard] + [tied(member, others) for member in self.coming]
        self.current = [
            jnp.concatenate(sides, axis=0) for sides in zip(*[self.halves(part) for part in parts])
        ]
        return self.current

    def send_middle(self, *others):
        self.coming = [
            hop(tied(member, others), order[-2])
            for member, order in zip(self.current, self.orders)
        ]

    def land_middle(self, *others):
        self.current = [
            jnp.concatenate([member, tied(come, others)], axis=0)
            for member, come in zip(self.current, self.coming)
        ]
        return self.current

    def send_last(self, *others):
        current = [tied(member, others) for member in self.current]
        self.later = [hop(member, order[-1]) for member, order in zip(current, self.orders)]
        self.core_current = [hop(member, CORE) for member in current]
        return self.later

    def send_core(self, *others):
        self.core_later = [hop(tied(member, others), CORE) for member in self.later]
        return self.core_later

    def pieces(self):
        sides = zip(self.current, self.later, self.core_current, self.core_later)
        return [Piece(side, order, 0, self.width) for side, order in zip(sides, self.orders)]


class WholeGathering:
    def __init__(self, shard, orders):
        self.width, self.orders = shard.shape[1] // 2, orders
        whole = lax.all_gather(shard, AXES, tiled=True)
        self.whole = whole.reshape(lax.axis_size("tensor"), -1, shard.shape[1])

    def send_far(self, *others):
        return []

    land_far = send_middle = land_middle = send_last = send_core = send_far

    def pieces(self):
        return [
            Piece([self.whole], order, side * self.width, self.width)
            for side, order in enumerate(self.orders)
        ]


class Scattering:
    def __init__(self, members, orders, sides):
        self.members, self.orders, self.sides = members, orders, sides
        self.begun = [members[-1][0]]

    def send_core(self, *others):
        self.coming = [hop(tied(send, others), CORE) for keep, send in self.members]
        return self.coming

    def land_core(self, *others):
        both = [
            [keep, tied(come, others)] for (keep, send), come in zip(self.members, self.coming)
        ]
        self.parts = [
            [[part[..., first:end] for part in both[member]] for member, first, end in side]
            for side in self.sides
        ]

    def total(self, side, take):
        sums = [
            sum(take(part).astype(jnp.float32) for part in group) for group in self.parts[side]
        ]
        return jnp.concatenate(sums, axis=-1) if len(sums) > 1 else sums[0]

    def halve(self, which, others):
        self.coming = []
        for side, order in enumerate(self.orders):
            half = self.parts[side][0][0].shape[0] // 2
            upper = self.total(side, lambda part: part[half:]).astype(jnp.bfloat16)
            self.coming.append(hop(tied(upper, others), order[which]))
        return self.coming

    def land(self, *others):
        for groups, come in zip(self.parts, self.coming):
            come, at = tied(come, others), 0
            for group in groups:
                width, half = group[0].shape[-1], group[0].shape[0] // 2
                group[:] = [part[:half] for part in group] + [come[..., at : at + width]]
                at += width

    def send_last(self, *others):
        return self.halve(-1, others)

    def send_middle(self, *others):
        return self.halve(-2, others)

    def send_far(self, *others):
        count = self.parts[0][0][0].shape[0]
        sides = range(len(self.orders))
        self.mine = jnp.concatenate(
            [self.total(side, lambda part: part[0]) for side in sides], axis=-1
        )
        self.coming = []
        for step in range(1, count):
            upper = jnp.concatenate(
                [self.total(side, lambda part: part[step]) for side in sides], axis=-1
            )
            self.coming.append(hop(tied(upper.astype(jnp.bfloat16), others), ("dp", 4 * step)))
        return self.coming

    def land_far(self, *others):
        come = [tied(part, others).astype(jnp.float32) for part in self.coming]
        self.result = sum([self.mine] + come)
        return [self.result]


class WholeScattering:
    def __init__(self, members, orders, sides):
        self.begun = [members[-1][0]]
        mine = [
            lax.psum_scatter(
                whole.reshape(-1, whole.shape[2]), AXES, scatter_dimension=0, tiled=True
            ).astype(jnp.float32)
            for (whole,) in members
        ]
        taken = [mine[member][:, first:end] for side in sides for member, first, end in side]
        self.result = jnp.concatenate(taken, axis=-1)

    def send_core(self, *others):
        return []

    land_core = send_last = send_middle = land = send_far = land_far = send_core


class Totals:
    def __init__(self, member, routed):
        self.routed, self.total = routed, member if routed else lax.psum(member, AXES)

    def send(self, axis, first, count, *others):
        if self.routed:
            total = tied(self.total, others)
            self.place = lax.axis_index(axis) // first % count
            self.coming = [hop(total, (axis, first * step)) for step in range(1, count)]

    def land(self, *others):
        if self.routed:
            stacked = jnp.stack([self.total] + [tied(come, others) for come in self.coming])
            self.total = sum(stacked[self.place ^ step] for step in range(len(self.coming) + 1))


def load_piece(meta, piece, sources, target, columns, sems):
    if isinstance(piece, Joined):
        at = 0
        for part in piece.parts:
            load_piece(
                meta, part, sources[: len(part.arrays)], target, slice(at, at + part.count), sems
            )
            sources, at = sources[len(part.arrays) :], at + part.count
        return
    if len(sources) == 1:
        for half_at in range(2):
            pltpu.make_async_copy(
                sources[0].at[half_at, :, piece.columns], target.at[half_at, :, columns],
                sems.at[half_at],
            ).start()
        return
    table = slot_table(piece.order)
    half = len(table) // 2
    block_rows = sources[0].shape[1]
    for slot, (dp_part, tensor_part) in enumerate(table):
        for core in range(2):
            source = sources[2 * core + slot // half]
            place = meta[0] ^ (dp_part ^ core)
            half_at = meta[1] ^ tensor_part
            rows = pl.ds(pl.multiple_of(place * block_rows, TILE_ROWS), block_rows)
            pltpu.make_async_copy(
                source.at[slot % half, :, piece.columns],
                target.at[half_at, rows, columns],
                sems.at[half_at],
            ).start()


def load_flat(meta, piece, sources, target, sem):
    count = piece.count
    if len(sources) == 1:
        for half_at in range(2):
            pltpu.make_async_copy(
                sources[0].at[half_at, :, piece.columns],
                target.at[:, slice(half_at * count, (half_at + 1) * count)], sem,
            ).start()
        return
    table = slot_table(piece.order)
    half = len(table) // 2
    block_rows = sources[0].shape[1]
    for slot, (dp_part, tensor_part) in enumerate(table):
        columns = pl.ds(pl.multiple_of((meta[1] ^ tensor_part) * count, 128), count)
        for core in range(2):
            place = meta[0] ^ (dp_part ^ core)
            rows = pl.ds(pl.multiple_of(place * block_rows, TILE_ROWS), block_rows)
            pltpu.make_async_copy(
                sources[2 * core + slot // half].at[slot % half, :, piece.columns],
                target.at[rows, columns],
                sem,
            ).start()


def await_piece(target, half_at, columns, sems):
    view = target.at[half_at, :, columns]
    pltpu.make_async_copy(view, view, sems.at[half_at]).wait()


def store_flat(meta, source, targets, order, columns, sem):
    count = source.shape[1] // 2
    if len(targets) == 1:
        for half_at in range(2):
            pltpu.make_async_copy(
                source.at[:, slice(half_at * count, (half_at + 1) * count)],
                targets[0].at[half_at, :, columns], sem,
            ).start()
        return
    block_rows = targets[0].shape[1]
    for slot, (dp_part, tensor_part) in enumerate(slot_table(order)):
        mine = pl.ds(pl.multiple_of((meta[1] ^ tensor_part) * count, 128), count)
        for core in range(2):
            place = meta[0] ^ (dp_part ^ core)
            rows = pl.ds(pl.multiple_of(place * block_rows, TILE_ROWS), block_rows)
            pltpu.make_async_copy(
                source.at[rows, mine], targets[core].at[slot, :, columns], sem
            ).start()


def store_piece(meta, source, targets, order, relative_half, columns, sem):
    if len(targets) == 1:
        pltpu.make_async_copy(
            source, targets[0].at[meta[1] ^ relative_half, :, columns], sem
        ).start()
        return
    block_rows = targets[0].shape[1]
    tensor_weight = 2 ** order.index(("tensor", 1))
    for slot, (dp_part, tensor_part) in enumerate(slot_table(order)):
        if tensor_part:
            continue
        for core in range(2):
            place = meta[0] ^ (dp_part ^ core)
            rows = pl.ds(pl.multiple_of(place * block_rows, TILE_ROWS), block_rows)
            pltpu.make_async_copy(
                source.at[rows, :],
                targets[core].at[slot + tensor_weight * relative_half, :, columns],
                sem,
            ).start()


def take(refs, *counts):
    groups, at = [], 0
    for count in counts:
        groups.append(refs[at] if count is None else refs[at : at + count])
        at += 1 if count is None else count
    return groups


def await_stored(source, sem):
    pltpu.make_async_copy(source, source, sem).wait()


def norm_stats(residual):
    centered = residual - jnp.mean(residual, axis=-1, keepdims=True)
    inv_spread = lax.rsqrt(jnp.mean(centered * centered, axis=-1, keepdims=True) + norm_eps)
    return centered * inv_spread, inv_spread


def norm_back(gradient, normed, inv_spread, gain):
    scaled = gradient * gain
    inner = jnp.mean(scaled * normed, axis=-1, keepdims=True)
    return inv_spread * (scaled - jnp.mean(scaled, axis=-1, keepdims=True) - normed * inner)


def row_tiles(row_count):
    tile = min(ROW_TILE, row_count)
    return [slice(start, start + tile) for start in range(0, row_count, tile)]


def column_sum(member):
    return jnp.sum(member, axis=0, keepdims=True)


def gelu_parts(inputs):
    bell = jnp.exp(-0.5 * inputs * inputs)
    ratio = 1.0 / (1.0 + erf_slope * jnp.abs(inputs))
    series = 0.5 * erf_terms[0]
    for term in erf_terms[1:]:
        series = series * ratio + 0.5 * term
    tail = series * ratio * bell
    below = jnp.where(inputs < 0, tail, 1.0 - tail)
    return inputs * below, below + inputs * (bell * inv_root_tau)


def qkv_forward_kernel(pieces, meta, inputs, bias, *refs):
    *sources, (out, weights, sems) = take(refs, *[len(piece.arrays) for piece in pieces], 3)
    step = pl.program_id(0)

    @pl.when(step == 0)
    def _():
        for which, piece in enumerate(pieces):
            load_flat(meta, piece, sources[which], weights.at[which], sems.at[which])

    await_stored(weights.at[step], sems.at[step])
    for rows in row_tiles(inputs.shape[0]):
        out[0, rows, :] = (dot_nn(inputs[rows, :], weights[step]) + bias[0]).astype(jnp.bfloat16)


def slab_features(meta, slab, slab_rows, k_side, q_side):
    segment_rows = slab_rows // 4
    row = lax.broadcasted_iota(jnp.int32, (slab_rows, PAIR), 0)
    lane = lax.broadcasted_iota(jnp.int32, (slab_rows, PAIR), 1) & (HEAD_DIM - 1)
    short = meta[2 + slab] == 0
    segment = jnp.where(short, row // segment_rows, 0)
    offset = row - segment * segment_rows
    base = 2 + meta_slabs(meta) + 4 * slab
    length = jnp.where(
        segment == 0,
        meta[base],
        jnp.where(segment == 1, meta[base + 1], jnp.where(segment == 2, meta[base + 2], meta[base + 3])),
    )
    same = segment == lane
    k_value = jnp.where(lane < 4, jnp.where(same, 1.0, 0.0), jnp.where(offset >= length, 1.0, 0.0))
    q_value = jnp.where(lane < 4, jnp.where(same, 0.0, big_negative), big_negative)
    k_side[slab] = jnp.where(lane < 5, k_value, 0.0).astype(jnp.bfloat16)
    q_side[slab] = jnp.where(lane < 5, q_value, 0.0).astype(jnp.bfloat16)


def meta_slabs(meta):
    return (meta.shape[0] - 2) // 5


def lane_low(row_count):
    return lax.broadcasted_iota(jnp.int32, (row_count, PAIR), 1) < HEAD_DIM


def attention_forward_kernel(meta, qkv, mixed, logsum, k_side, q_side):
    slab, pair = pl.program_id(1), pl.program_id(0)
    slab_rows = qkv.shape[1]

    @pl.when(pair == 0)
    def _():
        slab_features(meta, slab, slab_rows, k_side, q_side)

    low = lane_low(slab_rows)
    query, key = qkv[0].astype(jnp.float32), qkv[1].astype(jnp.float32)
    k_extra, q_extra = k_side[slab].astype(jnp.float32), q_side[slab].astype(jnp.float32)
    value_flip = flipped(qkv[2])
    sub = lax.broadcasted_iota(jnp.int32, (PAIR, slab_rows), 0)
    outcomes = []
    for head in range(2):
        mine = low if head == 0 else jnp.logical_not(low)
        q_head = jnp.where(mine, query, q_extra).astype(jnp.bfloat16)
        k_head = jnp.where(mine, key, k_extra).astype(jnp.bfloat16)
        scores = dot_nt(k_head, q_head)
        top = jnp.max(scores, axis=0, keepdims=True)
        weight = jnp.exp2((scores - top) * exponent_scale).astype(jnp.bfloat16)
        sum_row = HEAD_DIM if head == 0 else 0
        kept = sub < HEAD_DIM if head == 0 else sub >= HEAD_DIM
        v_head = jnp.where(kept, value_flip, jnp.where(sub == sum_row, 1.0, 0.0))
        blend = dot_nn(v_head.astype(jnp.bfloat16), weight)
        total = blend[sum_row : sum_row + 1, :]
        logsum[0, 0, head : head + 1, :] = top * exponent_scale + jnp.log(total) * log2_e
        outcomes.append(blend / total)
    mixed[...] = jnp.where(sub < HEAD_DIM, outcomes[0], outcomes[1]).T.astype(jnp.bfloat16)


def ffn_forward_kernel(pieces, meta, mixed, inputs, vectors, ffn_bias, *refs):
    out_sources, in_sources, down_sources, outputs, scratch = take(
        refs, *[len(piece.arrays) for piece in pieces], 8, 7
    )
    hidden, normed_one, spread_one, activated, slope, result, normed_two, spread_two = outputs
    out_whole, in_whole, down_whole, total, out_sems, in_sems, down_sems = scratch
    step = pl.program_id(0)
    steps = pl.num_programs(0)
    everything = slice(None)
    out_columns = out_whole.shape[2]
    tiles = row_tiles(inputs.shape[0])
    lanes = spread_one.shape[1]

    @pl.when(step == 0)
    def _():
        load_piece(meta, pieces[0], out_sources, out_whole, everything, out_sems)
        load_piece(meta, pieces[1], in_sources, in_whole, everything, in_sems)
        load_piece(meta, pieces[2], down_sources, down_whole, everything, down_sems)
        for half_at in range(2):
            await_piece(out_whole, half_at, everything, out_sems)
        for rows in tiles:
            attention_out = vectors[0:1, :]
            for half_at in range(2):
                columns = slice(half_at * out_columns, (half_at + 1) * out_columns)
                attention_out = attention_out + dot_nt(mixed[rows, columns], out_whole[half_at])
            normed, spread = norm_stats(inputs[rows, :].astype(jnp.float32) + attention_out)
            low = (normed * vectors[2:3, :] + vectors[4:5, :]).astype(jnp.bfloat16)
            hidden[rows, :] = low
            normed_one[rows, :] = normed.astype(jnp.bfloat16)
            spread_one[rows, :] = jnp.broadcast_to(spread, (spread.shape[0], lanes))
            total[rows, :] = low.astype(jnp.float32) + vectors[1:2, :]

    half_at = meta[1] ^ (step // FFN_PARTS)
    width = activated.shape[1]
    part = pl.ds(pl.multiple_of((step % FFN_PARTS) * width, 128), width)

    @pl.when(step % FFN_PARTS == 0)
    def _():
        await_piece(in_whole, half_at, everything, in_sems)
        await_piece(down_whole, half_at, everything, down_sems)

    for rows in tiles:
        pre_gelu = dot_nn(hidden[rows, :], in_whole[half_at, :, part]) + ffn_bias[0]
        value, steep = gelu_parts(pre_gelu)
        low = value.astype(jnp.bfloat16)
        activated[rows, :] = low
        slope[rows, :] = steep.astype(jnp.bfloat16)
        total[rows, :] += dot_nt(low, down_whole[half_at, :, part])

    @pl.when(step == steps - 1)
    def _():
        for rows in tiles:
            normed, spread = norm_stats(total[rows, :])
            result[rows, :] = (normed * vectors[3:4, :] + vectors[5:6, :]).astype(jnp.bfloat16)
            normed_two[rows, :] = normed.astype(jnp.bfloat16)
            spread_two[rows, :] = jnp.broadcast_to(spread, (spread.shape[0], lanes))


def ffn_backward_kernel(
    pieces, orders, target_count, meta, gradient, normed_two, spread_two, hidden, normed_one, spread_one,
    activated, slope, vectors, *refs
):
    in_sources, down_sources, outputs, targets, scratch = take(
        refs, *[len(piece.arrays) for piece in pieces], 4, target_count, 11
    )
    attention_grad, resid_grad, sums, bias_sums = outputs
    (
        in_whole, down_whole, total, branch, branch_flip, hidden_flip, pre_part, grad_parts,
        in_sems, down_sems, out_sems,
    ) = scratch
    step = pl.program_id(0)
    steps = pl.num_programs(0)
    everything = slice(None)
    tiles = row_tiles(hidden.shape[0])
    slot = step % 2

    @pl.when(step == 0)
    def _():
        load_piece(meta, pieces[0], in_sources, in_whole, everything, in_sems)
        load_piece(meta, pieces[1], down_sources, down_whole, everything, down_sems)
        gain_sum, shift_sum, branch_sum = 0.0, 0.0, 0.0
        for rows in tiles:
            grad = gradient[rows, :].astype(jnp.float32)
            normed = normed_two[rows, :].astype(jnp.float32)
            resid = norm_back(grad, normed, spread_two[rows, 0:1], vectors[3:4, :])
            low = resid.astype(jnp.bfloat16)
            total[rows, :] = resid
            branch[rows, :] = low
            branch_flip[:, rows] = flipped(low).astype(jnp.bfloat16)
            hidden_flip[:, rows] = flipped(hidden[rows, :]).astype(jnp.bfloat16)
            gain_sum += column_sum(grad * normed)
            shift_sum += column_sum(grad)
            branch_sum += column_sum(low.astype(jnp.float32))
        sums[...] = jnp.zeros(sums.shape, jnp.float32)
        sums[1:2, :] = branch_sum
        sums[3:4, :] = gain_sum
        sums[5:6, :] = shift_sum

    half_at = meta[1] ^ (step // FFN_PARTS)
    width = activated.shape[1]
    part = pl.ds(pl.multiple_of((step % FFN_PARTS) * width, 128), width)

    @pl.when(step % FFN_PARTS == 0)
    def _():
        await_piece(in_whole, half_at, everything, in_sems)
        await_piece(down_whole, half_at, everything, down_sems)

    @pl.when(step >= 2)
    def _():
        await_stored(grad_parts.at[slot, 0], out_sems.at[slot, 0])
        await_stored(grad_parts.at[slot, 1], out_sems.at[slot, 1])

    grad_parts[slot, 1] = dot_nn(branch_flip[...], activated[...]).astype(jnp.bfloat16)
    down_part = pl.ds(pl.multiple_of(FFN_PARTS * width + (step % FFN_PARTS) * width, 128), width)
    store_piece(
        meta, grad_parts.at[slot, 1], targets, orders[1], step // FFN_PARTS, down_part,
        out_sems.at[slot, 1],
    )
    bias_sum = 0.0
    for rows in tiles:
        active_grad = dot_nn(branch[rows, :], down_whole[half_at, :, part])
        low = (active_grad * slope[rows, :].astype(jnp.float32)).astype(jnp.bfloat16)
        pre_part[rows, :] = low
        bias_sum += column_sum(low.astype(jnp.float32))
        total[rows, :] += dot_nt(low, in_whole[half_at, :, part])
    bias_sums[0] = bias_sum
    grad_parts[slot, 0] = dot_nn(hidden_flip[...], pre_part[...]).astype(jnp.bfloat16)
    store_piece(
        meta, grad_parts.at[slot, 0], targets, orders[0], step // FFN_PARTS, part,
        out_sems.at[slot, 0],
    )

    @pl.when(step == steps - 1)
    def _():
        gain_sum, shift_sum, branch_sum = 0.0, 0.0, 0.0
        for rows in tiles:
            grad = total[rows, :]
            normed = normed_one[rows, :].astype(jnp.float32)
            resid = norm_back(grad, normed, spread_one[rows, 0:1], vectors[2:3, :])
            low = resid.astype(jnp.bfloat16)
            resid_grad[rows, :] = resid
            attention_grad[rows, :] = low
            gain_sum += column_sum(grad * normed)
            shift_sum += column_sum(grad)
            branch_sum += column_sum(low.astype(jnp.float32))
        sums[0:1, :] = branch_sum
        sums[2:3, :] = gain_sum
        sums[4:5, :] = shift_sum
        for late in range(2):
            await_stored(grad_parts.at[late, 0], out_sems.at[late, 0])
            await_stored(grad_parts.at[late, 1], out_sems.at[late, 1])


def out_backward_kernel(pieces, order, target_count, meta, attention_grad, mixed, *refs):
    sources, mixed_grad, targets, scratch = take(
        refs, len(pieces[0].arrays), None, target_count, 5
    )
    out_whole, grad_flip, grad_part, load_sem, out_sem = scratch
    tiles = row_tiles(mixed.shape[0])
    load_flat(meta, pieces[0], sources, out_whole, load_sem)
    for rows in tiles:
        grad_flip[:, rows] = flipped(attention_grad[rows, :]).astype(jnp.bfloat16)
    grad_part[...] = dot_nn(grad_flip[...], mixed[...]).astype(jnp.bfloat16)
    store_flat(meta, grad_part, targets, order, slice(None), out_sem)
    await_stored(out_whole, load_sem)
    for rows in tiles:
        mixed_grad[rows, :] = dot_nn(attention_grad[rows, :], out_whole[...]).astype(jnp.bfloat16)
    await_stored(grad_part, out_sem)


def attention_backward_kernel(meta, qkv, mixed, mixed_grad, logsum, grads, sums, k_side, q_side):
    slab, pair = pl.program_id(1), pl.program_id(0)
    slab_rows = qkv.shape[1]

    @pl.when(pair == 0)
    def _():
        slab_features(meta, slab, slab_rows, k_side, q_side)

    low = lane_low(slab_rows)
    query, key, value = (qkv[place].astype(jnp.float32) for place in range(3))
    k_extra, q_extra = k_side[slab].astype(jnp.float32), q_side[slab].astype(jnp.float32)
    grad_low = mixed_grad[...]
    grad = grad_low.astype(jnp.float32)
    product = (grad * mixed[...].astype(jnp.float32)).T
    key_flip = key.T
    sub = lax.broadcasted_iota(jnp.int32, (PAIR, slab_rows), 0)
    query_flip, key_grad, value_grad = 0.0, 0.0, 0.0
    for head in range(2):
        mine = low if head == 0 else jnp.logical_not(low)
        kept = sub < HEAD_DIM if head == 0 else sub >= HEAD_DIM
        span = slice(head * HEAD_DIM, (head + 1) * HEAD_DIM)
        q_head = jnp.where(mine, query, q_extra).astype(jnp.bfloat16)
        k_head = jnp.where(mine, key, k_extra).astype(jnp.bfloat16)
        v_head = jnp.where(mine, value, 0.0).astype(jnp.bfloat16)
        probs = jnp.exp2(
            dot_nt(k_head, q_head) * exponent_scale - logsum[0, 0, head : head + 1, :]
        )
        delta = column_sum(product[span, :])
        raw_grad = (probs * (dot_nt(v_head, grad_low) - delta)).astype(jnp.bfloat16)
        g_head = jnp.where(mine, grad, 0.0).astype(jnp.bfloat16)
        value_grad += dot_nn(probs.astype(jnp.bfloat16), g_head)
        key_grad += dot_nn(raw_grad, jnp.where(mine, query, 0.0).astype(jnp.bfloat16))
        query_flip += dot_nn(jnp.where(kept, key_flip, 0.0).astype(jnp.bfloat16), raw_grad)
    query_low = (query_flip * score_scale).T.astype(jnp.bfloat16)
    value_low = value_grad.astype(jnp.bfloat16)
    grads[0] = query_low
    grads[1] = (key_grad * score_scale).astype(jnp.bfloat16)
    grads[2] = value_low

    @pl.when(slab == 0)
    def _():
        sums[...] = jnp.zeros(sums.shape, jnp.float32)

    sums[0:1, :] += column_sum(query_low.astype(jnp.float32))
    sums[1:2, :] += column_sum(value_low.astype(jnp.float32))


def qkv_grad_kernel(orders, target_count, meta, inputs, grads, *refs):
    targets, (inputs_flip, grad_parts, out_sems) = take(refs, target_count, 3)
    step = pl.program_id(0)
    columns = grads.shape[2] // 2

    @pl.when(step == 0)
    def _():
        for rows in row_tiles(inputs.shape[0]):
            inputs_flip[:, rows] = flipped(inputs[rows, :]).astype(jnp.bfloat16)

    grad_parts[step] = dot_nn(inputs_flip[...], grads[0]).astype(jnp.bfloat16)
    for which, order in enumerate((orders[0], orders[1], orders[1])):

        @pl.when(step == which)
        def _():
            span = slice(which * columns, (which + 1) * columns)
            store_flat(meta, grad_parts.at[which], targets, order, span, out_sems.at[which])

    @pl.when(step == 2)
    def _():
        for which in range(3):
            await_stored(grad_parts.at[which], out_sems.at[which])


def input_grad_kernel(pieces, meta, grads, resid_grad, *refs):
    *sources, outputs, (weights, sems) = take(
        refs, *[len(piece.arrays) for piece in pieces], len(refs) - 2 - sum(
            len(piece.arrays) for piece in pieces
        ), 2,
    )
    input_grad = outputs[0]
    step = pl.program_id(0)
    tiles = row_tiles(resid_grad.shape[0])

    @pl.when(step == 0)
    def _():
        for which, piece in enumerate(pieces):
            load_flat(meta, piece, sources[which], weights.at[which], sems.at[which])
        for rows in tiles:
            input_grad[rows, :] = resid_grad[rows, :]

    await_stored(weights.at[step], sems.at[step])
    for rows in tiles:
        input_grad[rows, :] += dot_nt(grads[0, rows, :], weights[step])

    if len(outputs) > 1:

        @pl.when(step == 2)
        def _():
            outputs[1][...] = input_grad[...].astype(jnp.bfloat16)


def fixed(shape):
    return pl.BlockSpec(
        shape, lambda *_: (0,) * len(shape), pipeline_mode=pl.Buffered(1)
    )


def fixed_out(shape):
    return pl.BlockSpec(shape, lambda *_: (0,) * len(shape))


ANYWHERE = pl.BlockSpec(memory_space=pl.ANY)


def run_kernel(kernel, meta, grid, ins, outs, scratch, flops, moved, name, after=()):
    used = len(ins)
    ins = list(ins) + [(ANYWHERE, member) for member in after]
    in_specs, operands = zip(*ins)
    out_specs, out_shapes = zip(*outs)

    def body(meta_ref, *refs):
        kernel(meta_ref, *refs[:used], *refs[len(ins) :])

    return pl.pallas_call(
        body,
        grid_spec=pltpu.PrefetchScalarGridSpec(
            num_scalar_prefetch=1,
            grid=grid,
            in_specs=list(in_specs),
            out_specs=list(out_specs),
            scratch_shapes=scratch,
        ),
        out_shape=list(out_shapes),
        compiler_params=pltpu.CompilerParams(vmem_limit_bytes=VMEM_LIMIT),
        cost_estimate=pl.CostEstimate(flops=(BACK_WEIGHT if "forward" not in name else COST_WEIGHT) * flops, bytes_accessed=moved, transcendentals=0),
        name=name,
    )(meta, *operands)


def low_shape(*shape):
    return jax.ShapeDtypeStruct(shape, jnp.bfloat16)


def full_shape(*shape):
    return jax.ShapeDtypeStruct(shape, jnp.float32)


def pair_sems():
    return pltpu.SemaphoreType.DMA((2,))


def half_of(step, meta, count):
    return meta[1] ^ (step // count)


def sources_of(pieces):
    return [(ANYWHERE, member) for piece in pieces for member in piece.arrays]


def targets_of(routed, split, width, block_rows, columns):
    if routed:
        shape = low_shape(split * width // (2 * block_rows), block_rows, columns)
        return [(ANYWHERE, shape), (ANYWHERE, shape)]
    return [(ANYWHERE, low_shape(split, width, columns))]


def three_sems():
    return pltpu.SemaphoreType.DMA((3,))


def qkv_forward(meta, inputs, bias, pieces, after=()):
    rows, width = inputs.shape
    (qkv,) = run_kernel(
        functools.partial(qkv_forward_kernel, pieces),
        meta,
        (3,),
        [
            (fixed((rows, width)), inputs),
            (pl.BlockSpec((1, 1, width), lambda i, m: (i, 0, 0)), bias),
        ]
        + sources_of(pieces),
        [(pl.BlockSpec((1, rows, width), lambda i, m: (i, 0, 0)), low_shape(3, rows, width))],
        [pltpu.VMEM((3, width, width), jnp.bfloat16), three_sems()],
        6 * rows * width * width,
        8 * rows * width + 6 * width * width,
        "qkv_forward",
        after,
    )
    return qkv


def attention_forward(meta, qkv, slab_count, after=()):
    _, rows, width = qkv.shape
    slab_rows = rows // slab_count
    pairs = width // PAIR
    return run_kernel(
        attention_forward_kernel,
        meta,
        (pairs, slab_count),
        [(pl.BlockSpec((3, slab_rows, PAIR), lambda p, s, m: (0, s, p)), qkv)],
        [
            (pl.BlockSpec((slab_rows, PAIR), lambda p, s, m: (s, p)), low_shape(rows, width)),
            (
                pl.BlockSpec((1, 1, 8, slab_rows), lambda p, s, m: (s, p, 0, 0)),
                full_shape(slab_count, pairs, 8, slab_rows),
            ),
        ],
        [pltpu.VMEM((slab_count, slab_rows, PAIR), jnp.bfloat16)] * 2,
        16 * rows * slab_rows * width,
        8 * rows * width,
        "attention_forward",
        after,
    )


def ffn_forward(meta, mixed, inputs, vectors, ffn_bias, pieces, after=()):
    rows, width = inputs.shape
    half_width = pieces[1].count
    part = half_width // FFN_PARTS

    def part_at(i, m):
        return half_of(i, m, FFN_PARTS) * FFN_PARTS + i % FFN_PARTS

    whole_rows = (fixed_out((rows, width)), low_shape(rows, width))
    spread = (fixed_out((rows, 128)), full_shape(rows, 128))
    inner = (
        pl.BlockSpec((rows, part), lambda i, m: (0, part_at(i, m))),
        low_shape(rows, 2 * half_width),
    )
    return run_kernel(
        functools.partial(ffn_forward_kernel, pieces),
        meta,
        (2 * FFN_PARTS,),
        [
            (fixed((rows, width)), mixed),
            (fixed((rows, width)), inputs),
            (fixed((8, width)), vectors),
            (pl.BlockSpec((1, 1, part), lambda i, m: (part_at(i, m), 0, 0)), ffn_bias),
        ]
        + sources_of(pieces),
        [whole_rows, whole_rows, spread, inner, inner, whole_rows, whole_rows, spread],
        [
            pltpu.VMEM((2, width, width // 2), jnp.bfloat16),
            pltpu.VMEM((2, width, half_width), jnp.bfloat16),
            pltpu.VMEM((2, width, half_width), jnp.bfloat16),
            pltpu.VMEM((rows, width), jnp.float32),
            pair_sems(),
            pair_sems(),
            pair_sems(),
        ],
        8 * rows * width * half_width,
        24 * rows * width + 8 * width * half_width,
        "ffn_forward",
        after,
    )


def ffn_backward(meta, gradient, kept, vectors, pieces, orders, targets, after=()):
    hidden, normed_one, spread_one, activated, slope, normed_two, spread_two = kept
    rows, width = hidden.shape
    half_width = pieces[0].count
    part = half_width // FFN_PARTS

    def part_at(i, m):
        return half_of(i, m, FFN_PARTS) * FFN_PARTS + i % FFN_PARTS

    low_rows = fixed((rows, width))
    spread = fixed((rows, 128))
    inner = pl.BlockSpec((rows, part), lambda i, m: (0, part_at(i, m)))
    return run_kernel(
        functools.partial(ffn_backward_kernel, pieces, orders, len(targets)),
        meta,
        (2 * FFN_PARTS,),
        [
            (low_rows, gradient),
            (low_rows, normed_two),
            (spread, spread_two),
            (low_rows, hidden),
            (low_rows, normed_one),
            (spread, spread_one),
            (inner, activated),
            (inner, slope),
            (fixed((8, width)), vectors),
        ]
        + sources_of(pieces),
        [
            (fixed_out((rows, width)), low_shape(rows, width)),
            (fixed_out((rows, width)), full_shape(rows, width)),
            (fixed_out((8, width)), full_shape(8, width)),
            (
                pl.BlockSpec((1, 1, part), lambda i, m: (part_at(i, m), 0, 0)),
                full_shape(2 * FFN_PARTS, 1, part),
            ),
        ]
        + targets,
        [
            pltpu.VMEM((2, width, half_width), jnp.bfloat16),
            pltpu.VMEM((2, width, half_width), jnp.bfloat16),
            pltpu.VMEM((rows, width), jnp.float32),
            pltpu.VMEM((rows, width), jnp.bfloat16),
            pltpu.VMEM((width, rows), jnp.bfloat16),
            pltpu.VMEM((width, rows), jnp.bfloat16),
            pltpu.VMEM((rows, part), jnp.bfloat16),
            pltpu.VMEM((2, 2, width, part), jnp.bfloat16),
            pair_sems(),
            pair_sems(),
            pltpu.SemaphoreType.DMA((2, 2)),
        ],
        16 * rows * width * half_width,
        40 * rows * width + 16 * width * half_width,
        "ffn_backward",
        after,
    )


def out_backward(meta, attention_grad, mixed, piece, order, targets, after=()):
    rows, width = mixed.shape
    return run_kernel(
        functools.partial(out_backward_kernel, [piece], order, len(targets)),
        meta,
        (1,),
        [(fixed((rows, width)), attention_grad), (fixed((rows, width)), mixed)]
        + sources_of([piece]),
        [(fixed_out((rows, width)), low_shape(rows, width))] + targets,
        [
            pltpu.VMEM((width, width), jnp.bfloat16),
            pltpu.VMEM((width, rows), jnp.bfloat16),
            pltpu.VMEM((width, width), jnp.bfloat16),
            pltpu.SemaphoreType.DMA,
            pltpu.SemaphoreType.DMA,
        ],
        4 * rows * width * width,
        6 * rows * width + 4 * width * width,
        "out_backward",
        after,
    )


def attention_backward(meta, qkv, mixed, mixed_grad, logsum, slab_count, after=()):
    _, rows, width = qkv.shape
    slab_rows = rows // slab_count
    pairs = width // PAIR
    three = pl.BlockSpec((3, slab_rows, PAIR), lambda p, s, m: (0, s, p))
    one = pl.BlockSpec((slab_rows, PAIR), lambda p, s, m: (s, p))
    return run_kernel(
        attention_backward_kernel,
        meta,
        (pairs, slab_count),
        [
            (three, qkv),
            (one, mixed),
            (one, mixed_grad),
            (pl.BlockSpec((1, 1, 8, slab_rows), lambda p, s, m: (s, p, 0, 0)), logsum),
        ],
        [
            (three, low_shape(3, rows, width)),
            (pl.BlockSpec((8, PAIR), lambda p, s, m: (0, p)), full_shape(8, width)),
        ],
        [pltpu.VMEM((slab_count, slab_rows, PAIR), jnp.bfloat16)] * 2,
        40 * rows * slab_rows * width,
        16 * rows * width,
        "attention_backward",
        after,
    )


def qkv_grad(meta, inputs, grads, orders, targets, after=()):
    rows, width = inputs.shape
    return run_kernel(
        functools.partial(qkv_grad_kernel, orders, len(targets)),
        meta,
        (3,),
        [
            (fixed((rows, width)), inputs),
            (pl.BlockSpec((1, rows, width), lambda i, m: (i, 0, 0)), grads),
        ],
        targets,
        [
            pltpu.VMEM((width, rows), jnp.bfloat16),
            pltpu.VMEM((3, width, width), jnp.bfloat16),
            three_sems(),
        ],
        6 * rows * width * width,
        8 * rows * width + 6 * width * width,
        "qkv_grad",
        after,
    )


def input_gradient(meta, grads, resid_grad, pieces, after=(), low=False):
    rows, width = resid_grad.shape
    outs = [(fixed_out((rows, width)), full_shape(rows, width))]
    if low:
        outs.append((fixed_out((rows, width)), low_shape(rows, width)))
    return run_kernel(
        functools.partial(input_grad_kernel, pieces),
        meta,
        (3,),
        [
            (pl.BlockSpec((1, rows, width), lambda i, m: (i, 0, 0)), grads),
            (fixed((rows, width)), resid_grad),
        ]
        + sources_of(pieces),
        outs,
        [pltpu.VMEM((3, width, width), jnp.bfloat16), three_sems()],
        6 * rows * width * width,
        14 * rows * width + 6 * width * width,
        "input_gradient",
        after,
    )


def both_halves(mine, theirs, place):
    first = jnp.concatenate([mine, theirs], axis=0)
    second = jnp.concatenate([theirs, mine], axis=0)
    return jnp.where(place == 0, first, second)


def on_device(
    tokens,
    cotangent,
    buckets,
    lengths,
    qkv_weight,
    qv_bias,
    out_weight,
    ffn_in_weight,
    ffn_in_bias,
    ffn_out_weight,
    out_bias,
    norm_gain,
    norm_bias,
):
    split = lax.axis_size("tensor")
    dp_size = lax.axis_size("dp")
    place = lax.axis_index("tensor")
    width = tokens.shape[1]
    rows = tokens.shape[0] // split
    slabs = buckets.shape[0] // split
    layer_count = qkv_weight.shape[0]
    block_rows = width // dp_size
    routed = block_rows % TILE_ROWS == 0 and dp_size & (dp_size - 1) == 0
    orders = hop_orders(dp_size if routed else PLANNED_BLOCKS)

    own_tokens = lax.dynamic_slice_in_dim(tokens, place * rows, rows)
    own_cotangent = lax.dynamic_slice_in_dim(cotangent, place * rows, rows)
    own_buckets = lax.dynamic_slice_in_dim(buckets, place * slabs, slabs)
    own_lengths = lax.dynamic_slice_in_dim(lengths, place * slabs, slabs)
    if routed:
        position = jnp.stack([lax.axis_index("dp"), place]).astype(jnp.int32)
    else:
        position = jnp.zeros((2,), jnp.int32)
    meta = jnp.concatenate([position, own_buckets, own_lengths.reshape(-1)])

    bias_flat = jnp.concatenate([qv_bias.reshape(layer_count, -1), ffn_in_bias], axis=1)
    bias_other = hop(bias_flat, ("tensor", 1))
    bias_halves = jnp.where(
        place == 0, jnp.stack([bias_flat, bias_other]), jnp.stack([bias_other, bias_flat])
    )
    qv_columns = qv_bias.shape[2]
    ffn_columns = ffn_in_bias.shape[1]

    def small_inputs(index):
        halves = bias_halves[:, index]
        value = halves[:, : 2 * qv_columns].reshape(2, 2, qv_columns)
        zero = jnp.zeros((2, qv_columns), jnp.float32)
        bias = jnp.stack([value[:, 0], zero, value[:, 1]]).reshape(3, 1, -1)
        vectors = jnp.concatenate(
            [out_bias[index], norm_gain[index], norm_bias[index], jnp.zeros((2, width), jnp.float32)]
        )
        return bias, vectors, halves[:, 2 * qv_columns :].reshape(2 * FFN_PARTS, 1, -1)

    def gathering(flag, *members):
        shard = jnp.concatenate(members, axis=1)
        return (Gathering if flag else WholeGathering)(shard, orders)

    def attention_split(pieces):
        half = width // 2
        query_key, value_out = pieces
        qkv = [query_key.narrow(0, half), query_key.narrow(half, half), value_out.narrow(0, half)]
        return qkv, value_out.narrow(half, half)

    hops_back = [[routed and flag for flag in flags] for flags in HOPS_BACK]

    def waits(flag, members):
        return list(members) if flag else []

    first = gathering(routed, *qkv_weight[0], out_weight[0])
    first_ffn = gathering(False, ffn_in_weight[0], ffn_out_weight[0])
    second = gathering(routed, *qkv_weight[1], out_weight[1])
    if SPLIT_DOWN:
        second_in = gathering(False, ffn_in_weight[1])
        second_down = gathering(routed, ffn_out_weight[1])
    else:
        second_in = gathering(False, ffn_in_weight[1], ffn_out_weight[1])
        second_down = second_in
    first.send_far()
    first.land_far()
    first.send_middle()
    first.land_middle()
    last = first.send_last()
    first.send_core()
    second.send_far(*waits(routed, last))
    bias, vectors, ffn_bias = small_inputs(0)
    qkv_pieces, out_piece = attention_split(first.pieces())
    qkv = qkv_forward(meta, own_tokens, bias, qkv_pieces)
    second.land_far(qkv)
    second.send_middle(qkv)
    mixed, logsum = attention_forward(meta, qkv, slabs)
    second.land_middle(mixed)
    second_last = second.send_last(mixed)
    if SPLIT_DOWN:
        second_down.send_far(mixed)
    first_pieces = (qkv_pieces, out_piece, first_ffn.pieces())
    out = ffn_forward(
        meta, mixed, own_tokens, vectors, ffn_bias, [out_piece] + first_pieces[2]
    )
    kept_layers = [(own_tokens, qkv, mixed, logsum, vectors, out)]
    layer_one = out[5]
    second.send_core(layer_one)
    if SPLIT_DOWN:
        second_down.land_far(layer_one)
        second_down.send_middle(layer_one)
    bias, vectors, ffn_bias = small_inputs(1)
    qkv_pieces, out_piece = attention_split(second.pieces())
    qkv = qkv_forward(meta, layer_one, bias, qkv_pieces, waits(routed, second_last))
    if SPLIT_DOWN:
        second_down.land_middle(qkv)
        second_down.send_last(qkv)
    mixed, logsum = attention_forward(meta, qkv, slabs)
    if SPLIT_DOWN:
        second_down.send_core(mixed)
        ffn_pieces = [Joined(second_in.pieces()), Joined(second_down.pieces())]
    else:
        ffn_pieces = second_in.pieces()
    one_other = hop(tied(layer_one, [mixed]), ("tensor", 1))
    second_pieces = (qkv_pieces, out_piece, ffn_pieces)
    out = ffn_forward(
        meta, mixed, layer_one, vectors, ffn_bias, [out_piece] + second_pieces[2]
    )
    kept_layers.append((layer_one, qkv, mixed, logsum, vectors, out))
    layer_two = out[5]
    two_other = hop(layer_two, ("tensor", 1))
    layer_one_whole = both_halves(layer_one, tied(one_other, [layer_two]), place)

    def targets(flag, columns):
        return targets_of(flag, split, width, block_rows, columns)

    def scattering(flag, members, sides):
        kind = Scattering if flag else WholeScattering
        return kind(members, orders, sides)

    half_ffn = ffn_in_weight.shape[2]

    def ffn_back(index, gradient, pieces, after=()):
        inputs, qkv, mixed, logsum, vectors, out = kept_layers[index]
        hidden, normed_one, spread_one, activated, slope, _, normed_two, spread_two = out
        kept = (hidden, normed_one, spread_one, activated, slope, normed_two, spread_two)
        attention_grad, resid_grad, sums, ffn_sums, *members = ffn_backward(
            meta, gradient, kept, vectors, pieces[2], orders, targets(hops_back[index][1], 2 * half_ffn), after
        )
        scatter = scattering(
            hops_back[index][1], [members], [[(0, 0, half_ffn)], [(0, half_ffn, 2 * half_ffn)]]
        )
        return attention_grad, resid_grad, (sums, ffn_sums), scatter

    def out_back(index, attention_grad, pieces, after=()):
        mixed = kept_layers[index][2]
        return out_backward(
            meta, attention_grad, mixed, pieces[1], orders[0], targets(hops_back[index][0], width // 2), after
        )

    def attention_back(index, mixed_grad, after=()):
        _, qkv, mixed, logsum, _, _ = kept_layers[index]
        return attention_backward(meta, qkv, mixed, mixed_grad, logsum, slabs, after)

    def qkv_grads(index, grads, out_members, after=()):
        members = qkv_grad(
            meta, kept_layers[index][0], grads, orders,
            targets(hops_back[index][0], 3 * width // 2), after,
        )
        columns = width // 2
        return scattering(
            hops_back[index][0],
            [out_members, members],
            [[(0, 0, columns), (1, 0, columns)], [(1, columns, 3 * columns)]],
        )

    def flat_smalls(sums, ffn_sums, qkv_sums):
        return jnp.concatenate(
            [sums[:6].reshape(-1), qkv_sums[:2].reshape(-1), ffn_sums.reshape(-1)]
        )

    attention_grad, resid_grad, sums, ffn_one = ffn_back(1, own_cotangent, second_pieces, [one_other])
    layer_two_whole = both_halves(layer_two, tied(two_other, [attention_grad]), place)
    ffn_one.send_core()
    mixed_grad, *out_members = out_back(1, attention_grad, second_pieces, [two_other])
    ffn_one.land_core(mixed_grad)
    ffn_one.send_last(mixed_grad)
    grads, qkv_sums = attention_back(1, mixed_grad)
    ffn_one.land(grads)
    smalls_one = flat_smalls(*sums, qkv_sums)
    attention_one = qkv_grads(1, grads, out_members)
    begun = attention_one.begun
    one_core = attention_one.send_core()
    ffn_one.send_middle(*begun)
    (gradient,) = input_gradient(meta, grads, resid_grad, second_pieces[0], begun)
    attention_one.land_core(gradient)
    ffn_one.land(gradient)
    one_last = attention_one.send_last(gradient)
    ffn_one.send_far(gradient)
    attention_grad, resid_grad, sums, ffn_zero = ffn_back(
        0, gradient, first_pieces, waits(hops_back[1][0], one_core)
    )
    attention_one.land(attention_grad)
    ffn_one.land_far(attention_grad)
    one_middle = attention_one.send_middle(attention_grad)
    zero_core = ffn_zero.send_core(attention_grad)
    mixed_grad, *out_members = out_back(
        0, attention_grad, first_pieces, waits(hops_back[1][0], one_last)
    )
    ffn_zero.land_core(mixed_grad)
    attention_one.land(mixed_grad)
    ffn_last = ffn_zero.send_last(mixed_grad)
    one_far = attention_one.send_far(mixed_grad)
    grads, qkv_sums = attention_back(0, mixed_grad, waits(routed, one_middle + zero_core))
    ffn_zero.land(grads)
    attention_one.land_far(grads)
    smalls_zero = flat_smalls(*sums, qkv_sums)
    totals = Totals(jnp.stack([smalls_zero, smalls_one]), routed)
    totals.send("dp", 1, 4, grads)
    zero_middle = ffn_zero.send_middle(grads)
    attention_zero = qkv_grads(0, grads, out_members, waits(routed, ffn_last + one_far))
    begun = attention_zero.begun
    totals.land(*begun)
    totals.send("dp", 4, dp_size // 4, *begun)
    attention_zero.send_core(*begun)
    gradient, token_low = input_gradient(
        meta, grads, resid_grad, first_pieces[0], begun + waits(routed, zero_middle), True
    )
    totals.land(gradient)
    attention_zero.land_core(gradient)
    zero_last = attention_zero.send_last(gradient)
    ffn_zero.land(gradient)
    ffn_zero.send_far(gradient)
    if HOLD_TOKENS:
        token_low = tied(token_low, waits(routed, zero_last))
    token_other = hop(token_low, ("tensor", 1))
    totals.send("tensor", 1, 2, gradient, *waits(routed, zero_last))
    attention_zero.land(gradient)
    zero_middle = attention_zero.send_middle(gradient)
    totals.land(gradient, *waits(routed, zero_middle))
    smalls = totals.total
    ffn_zero.land_far(gradient, *waits(routed, zero_middle))
    attention_zero.land(gradient)
    attention_zero.send_far(gradient)
    attention_zero.land_far(gradient)
    token_grad = both_halves(gradient, token_other.astype(jnp.float32), place)
    matrix_grads = []
    for attention, ffn in ((attention_zero, ffn_zero), (attention_one, ffn_one)):
        out_part, *qkv_parts = jnp.split(attention.result, 4, axis=1)
        matrix_grads.append((jnp.stack(qkv_parts), out_part, *jnp.split(ffn.result, 2, axis=1)))
    eight = smalls[:, : 8 * width].reshape(layer_count, 4, 2, width)
    ffn_total = smalls[:, 8 * width :]
    return (
        layer_one_whole,
        layer_two_whole,
        token_grad,
        jnp.stack([member[0] for member in matrix_grads]),
        lax.dynamic_slice_in_dim(eight[:, 3], place * qv_columns, qv_columns, axis=2),
        jnp.stack([member[1] for member in matrix_grads]),
        jnp.stack([member[2] for member in matrix_grads]),
        lax.dynamic_slice_in_dim(ffn_total, place * ffn_columns, ffn_columns, axis=1),
        jnp.stack([member[3] for member in matrix_grads]),
        eight[:, 0],
        eight[:, 1],
        eight[:, 2],
    )


def solution(mesh):
    placed = (
        P("dp", None),
        P("dp", None),
        P("dp"),
        P("dp", None),
        P(None, None, "dp", "tensor"),
        P(None, None, "tensor"),
        P(None, "dp", "tensor"),
        P(None, "dp", "tensor"),
        P(None, "tensor"),
        P(None, "dp", "tensor"),
        P(),
        P(),
        P(),
    )
    return jax.shard_map(
        on_device,
        mesh=mesh,
        in_specs=placed,
        out_specs=(
            P("dp", None),
            P("dp", None),
            P("dp", None),
            P(None, None, "dp", "tensor"),
            P(None, None, "tensor"),
            P(None, "dp", "tensor"),
            P(None, "dp", "tensor"),
            P(None, "tensor"),
            P(None, "dp", "tensor"),
            P(),
            P(),
            P(),
        ),
        check_vma=False,
    )
```

```python
import functools

import jax
import jax.numpy as jnp
from jax import lax
from jax.experimental import pallas as pl
from jax.experimental.pallas import tpu as pltpu
from jax.sharding import PartitionSpec as P

HEAD_DIM = 64
PAIR = 2 * HEAD_DIM
AXES = ("tensor", "dp")
CORE = ("dp", 1)
FFN_PARTS = 2
ROW_TILE = 512
TILE_ROWS = 16
PLANNED_BLOCKS = 16
HOPS_BACK = ((True, True), (True, False))
COST_WEIGHT = 8
BACK_WEIGHT = 16
SPLIT_DOWN = False
HOLD_TOKENS = True
VMEM_LIMIT = 58 * 1024 * 1024

norm_eps = 1e-06
big_negative = -1e30
inv_root_tau = 0.3989422804014327
log2_e = 1.4426950408889634
score_scale = HEAD_DIM ** (-0.5)
exponent_scale = score_scale * log2_e
erf_slope = 0.3275911 * 0.7071067811865476
erf_terms = (1.061405429, -1.453152027, 1.421413741, -0.284496736, 0.254829592)


def dot_nn(left, right):
    return lax.dot_general(
        left, right, (((1,), (0,)), ((), ())), preferred_element_type=jnp.float32
    )


def dot_nt(left, right):
    return lax.dot_general(
        left, right, (((1,), (1,)), ((), ())), preferred_element_type=jnp.float32
    )


def flipped(member):
    return member.astype(jnp.float32).T


def hop_orders(block_count):
    far = []
    bit = 4
    while bit < block_count:
        far.append(("dp", bit))
        bit *= 2
    across, along = ("dp", 2), ("tensor", 1)
    return (far + [across, along], far + [along, across])


def slot_table(order):
    table = []
    for slot in range(2 ** len(order)):
        dp_part, tensor_part = 0, 0
        for position, (axis, bit) in enumerate(order):
            if slot >> position & 1:
                if axis == "dp":
                    dp_part ^= bit
                else:
                    tensor_part ^= bit
        table.append((dp_part, tensor_part))
    return table


def hop(member, dim):
    axis, bit = dim
    pairs = [(place, place ^ bit) for place in range(lax.axis_size(axis))]
    return lax.ppermute(member, axis, pairs)


def tied(member, others):
    return lax.optimization_barrier((member, *others))[0] if others else member


class Piece:
    def __init__(self, arrays, order, first, count):
        self.arrays, self.order, self.columns = tuple(arrays), order, slice(first, first + count)
        self.count = count

    def narrow(self, first, count):
        return Piece(self.arrays, self.order, self.columns.start + first, count)


class Joined:
    def __init__(self, parts):
        self.parts, self.count = tuple(parts), sum(part.count for part in parts)
        self.arrays = tuple(member for part in parts for member in part.arrays)


class Gathering:
    def __init__(self, shard, orders):
        self.shard, self.orders, self.width = shard[None], orders, shard.shape[1] // 2

    def halves(self, member):
        return [member[..., : self.width], member[..., self.width :]]

    def send_far(self, *others):
        shard = tied(self.shard, others)
        count = 2 ** (len(self.orders[0]) - 2)
        self.coming = [hop(shard, ("dp", 4 * step)) for step in range(1, count)]

    def land_far(self, *others):
        parts = [self.shard] + [tied(member, others) for member in self.coming]
        self.current = [
            jnp.concatenate(sides, axis=0) for sides in zip(*[self.halves(part) for part in parts])
        ]
        return self.current

    def send_middle(self, *others):
        self.coming = [
            hop(tied(member, others), order[-2])
            for member, order in zip(self.current, self.orders)
        ]

    def land_middle(self, *others):
        self.current = [
            jnp.concatenate([member, tied(come, others)], axis=0)
            for member, come in zip(self.current, self.coming)
        ]
        return self.current

    def send_last(self, *others):
        current = [tied(member, others) for member in self.current]
        self.later = [hop(member, order[-1]) for member, order in zip(current, self.orders)]
        self.core_current = [hop(member, CORE) for member in current]
        return self.later

    def send_core(self, *others):
        self.core_later = [hop(tied(member, others), CORE) for member in self.later]
        return self.core_later

    def pieces(self):
        sides = zip(self.current, self.later, self.core_current, self.core_later)
        return [Piece(side, order, 0, self.width) for side, order in zip(sides, self.orders)]


class WholeGathering:
    def __init__(self, shard, orders):
        self.width, self.orders = shard.shape[1] // 2, orders
        whole = lax.all_gather(shard, AXES, tiled=True)
        self.whole = whole.reshape(lax.axis_size("tensor"), -1, shard.shape[1])

    def send_far(self, *others):
        return []

    land_far = send_middle = land_middle = send_last = send_core = send_far

    def pieces(self):
        return [
            Piece([self.whole], order, side * self.width, self.width)
            for side, order in enumerate(self.orders)
        ]


class Scattering:
    def __init__(self, members, orders, sides):
        self.members, self.orders, self.sides = members, orders, sides
        self.begun = [members[-1][0]]

    def send_core(self, *others):
        self.coming = [hop(tied(send, others), CORE) for keep, send in self.members]
        return self.coming

    def land_core(self, *others):
        both = [
            [keep, tied(come, others)] for (keep, send), come in zip(self.members, self.coming)
        ]
        self.parts = [
            [[part[..., first:end] for part in both[member]] for member, first, end in side]
            for side in self.sides
        ]

    def total(self, side, take):
        sums = [
            sum(take(part).astype(jnp.float32) for part in group) for group in self.parts[side]
        ]
        return jnp.concatenate(sums, axis=-1) if len(sums) > 1 else sums[0]

    def halve(self, which, others):
        self.coming = []
        for side, order in enumerate(self.orders):
            half = self.parts[side][0][0].shape[0] // 2
            upper = self.total(side, lambda part: part[half:]).astype(jnp.bfloat16)
            self.coming.append(hop(tied(upper, others), order[which]))
        return self.coming

    def land(self, *others):
        for groups, come in zip(self.parts, self.coming):
            come, at = tied(come, others), 0
            for group in groups:
                width, half = group[0].shape[-1], group[0].shape[0] // 2
                group[:] = [part[:half] for part in group] + [come[..., at : at + width]]
                at += width

    def send_last(self, *others):
        return self.halve(-1, others)

    def send_middle(self, *others):
        return self.halve(-2, others)

    def send_far(self, *others):
        count = self.parts[0][0][0].shape[0]
        sides = range(len(self.orders))
        self.mine = jnp.concatenate(
            [self.total(side, lambda part: part[0]) for side in sides], axis=-1
        )
        self.coming = []
        for step in range(1, count):
            upper = jnp.concatenate(
                [self.total(side, lambda part: part[step]) for side in sides], axis=-1
            )
            self.coming.append(hop(tied(upper.astype(jnp.bfloat16), others), ("dp", 4 * step)))
        return self.coming

    def land_far(self, *others):
        come = [tied(part, others).astype(jnp.float32) for part in self.coming]
        self.result = sum([self.mine] + come)
        return [self.result]


class WholeScattering:
    def __init__(self, members, orders, sides):
        self.begun = [members[-1][0]]
        mine = [
            lax.psum_scatter(
                whole.reshape(-1, whole.shape[2]), AXES, scatter_dimension=0, tiled=True
            ).astype(jnp.float32)
            for (whole,) in members
        ]
        taken = [mine[member][:, first:end] for side in sides for member, first, end in side]
        self.result = jnp.concatenate(taken, axis=-1)

    def send_core(self, *others):
        return []

    land_core = send_last = send_middle = land = send_far = land_far = send_core


class Totals:
    def __init__(self, member, routed):
        self.routed, self.total = routed, member if routed else lax.psum(member, AXES)

    def send(self, axis, first, count, *others):
        if self.routed:
            total = tied(self.total, others)
            self.place = lax.axis_index(axis) // first % count
            self.coming = [hop(total, (axis, first * step)) for step in range(1, count)]

    def land(self, *others):
        if self.routed:
            stacked = jnp.stack([self.total] + [tied(come, others) for come in self.coming])
            self.total = sum(stacked[self.place ^ step] for step in range(len(self.coming) + 1))


def load_piece(meta, piece, sources, target, columns, sems):
    if isinstance(piece, Joined):
        at = 0
        for part in piece.parts:
            load_piece(
                meta, part, sources[: len(part.arrays)], target, slice(at, at + part.count), sems
            )
            sources, at = sources[len(part.arrays) :], at + part.count
        return
    if len(sources) == 1:
        for half_at in range(2):
            pltpu.make_async_copy(
                sources[0].at[half_at, :, piece.columns], target.at[half_at, :, columns],
                sems.at[half_at],
            ).start()
        return
    table = slot_table(piece.order)
    half = len(table) // 2
    block_rows = sources[0].shape[1]
    for slot, (dp_part, tensor_part) in enumerate(table):
        for core in range(2):
            source = sources[2 * core + slot // half]
            place = meta[0] ^ (dp_part ^ core)
            half_at = meta[1] ^ tensor_part
            rows = pl.ds(pl.multiple_of(place * block_rows, TILE_ROWS), block_rows)
            pltpu.make_async_copy(
                source.at[slot % half, :, piece.columns],
                target.at[half_at, rows, columns],
                sems.at[half_at],
            ).start()


def load_flat(meta, piece, sources, target, sem):
    count = piece.count
    if len(sources) == 1:
        for half_at in range(2):
            pltpu.make_async_copy(
                sources[0].at[half_at, :, piece.columns],
                target.at[:, slice(half_at * count, (half_at + 1) * count)], sem,
            ).start()
        return
    table = slot_table(piece.order)
    half = len(table) // 2
    block_rows = sources[0].shape[1]
    for slot, (dp_part, tensor_part) in enumerate(table):
        columns = pl.ds(pl.multiple_of((meta[1] ^ tensor_part) * count, 128), count)
        for core in range(2):
            place = meta[0] ^ (dp_part ^ core)
            rows = pl.ds(pl.multiple_of(place * block_rows, TILE_ROWS), block_rows)
            pltpu.make_async_copy(
                sources[2 * core + slot // half].at[slot % half, :, piece.columns],
                target.at[rows, columns],
                sem,
            ).start()


def await_piece(target, half_at, columns, sems):
    view = target.at[half_at, :, columns]
    pltpu.make_async_copy(view, view, sems.at[half_at]).wait()


def store_flat(meta, source, targets, order, columns, sem):
    count = source.shape[1] // 2
    if len(targets) == 1:
        for half_at in range(2):
            pltpu.make_async_copy(
                source.at[:, slice(half_at * count, (half_at + 1) * count)],
                targets[0].at[half_at, :, columns], sem,
            ).start()
        return
    block_rows = targets[0].shape[1]
    for slot, (dp_part, tensor_part) in enumerate(slot_table(order)):
        mine = pl.ds(pl.multiple_of((meta[1] ^ tensor_part) * count, 128), count)
        for core in range(2):
            place = meta[0] ^ (dp_part ^ core)
            rows = pl.ds(pl.multiple_of(place * block_rows, TILE_ROWS), block_rows)
            pltpu.make_async_copy(
                source.at[rows, mine], targets[core].at[slot, :, columns], sem
            ).start()


def store_piece(meta, source, targets, order, relative_half, columns, sem):
    if len(targets) == 1:
        pltpu.make_async_copy(
            source, targets[0].at[meta[1] ^ relative_half, :, columns], sem
        ).start()
        return
    block_rows = targets[0].shape[1]
    tensor_weight = 2 ** order.index(("tensor", 1))
    for slot, (dp_part, tensor_part) in enumerate(slot_table(order)):
        if tensor_part:
            continue
        for core in range(2):
            place = meta[0] ^ (dp_part ^ core)
            rows = pl.ds(pl.multiple_of(place * block_rows, TILE_ROWS), block_rows)
            pltpu.make_async_copy(
                source.at[rows, :],
                targets[core].at[slot + tensor_weight * relative_half, :, columns],
                sem,
            ).start()


def take(refs, *counts):
    groups, at = [], 0
    for count in counts:
        groups.append(refs[at] if count is None else refs[at : at + count])
        at += 1 if count is None else count
    return groups


def await_stored(source, sem):
    pltpu.make_async_copy(source, source, sem).wait()


def norm_stats(residual):
    centered = residual - jnp.mean(residual, axis=-1, keepdims=True)
    inv_spread = lax.rsqrt(jnp.mean(centered * centered, axis=-1, keepdims=True) + norm_eps)
    return centered * inv_spread, inv_spread


def norm_back(gradient, normed, inv_spread, gain):
    scaled = gradient * gain
    inner = jnp.mean(scaled * normed, axis=-1, keepdims=True)
    return inv_spread * (scaled - jnp.mean(scaled, axis=-1, keepdims=True) - normed * inner)


def row_tiles(row_count):
    tile = min(ROW_TILE, row_count)
    return [slice(start, start + tile) for start in range(0, row_count, tile)]


def column_sum(member):
    return jnp.sum(member, axis=0, keepdims=True)


def gelu_parts(inputs):
    bell = jnp.exp(-0.5 * inputs * inputs)
    ratio = 1.0 / (1.0 + erf_slope * jnp.abs(inputs))
    series = 0.5 * erf_terms[0]
    for term in erf_terms[1:]:
        series = series * ratio + 0.5 * term
    tail = series * ratio * bell
    below = jnp.where(inputs < 0, tail, 1.0 - tail)
    return inputs * below, below + inputs * (bell * inv_root_tau)


def qkv_forward_kernel(pieces, meta, inputs, bias, *refs):
    *sources, (out, weights, sems) = take(refs, *[len(piece.arrays) for piece in pieces], 3)
    step = pl.program_id(0)

    @pl.when(step == 0)
    def _():
        for which, piece in enumerate(pieces):
            load_flat(meta, piece, sources[which], weights.at[which], sems.at[which])

    await_stored(weights.at[step], sems.at[step])
    for rows in row_tiles(inputs.shape[0]):
        out[0, rows, :] = (dot_nn(inputs[rows, :], weights[step]) + bias[0]).astype(jnp.bfloat16)


def slab_features(meta, slab, slab_rows, k_side, q_side):
    segment_rows = slab_rows // 4
    row = lax.broadcasted_iota(jnp.int32, (slab_rows, PAIR), 0)
    lane = lax.broadcasted_iota(jnp.int32, (slab_rows, PAIR), 1) & (HEAD_DIM - 1)
    short = meta[2 + slab] == 0
    segment = jnp.where(short, row // segment_rows, 0)
    offset = row - segment * segment_rows
    base = 2 + meta_slabs(meta) + 4 * slab
    length = jnp.where(
        segment == 0,
        meta[base],
        jnp.where(segment == 1, meta[base + 1], jnp.where(segment == 2, meta[base + 2], meta[base + 3])),
    )
    same = segment == lane
    k_value = jnp.where(lane < 4, jnp.where(same, 1.0, 0.0), jnp.where(offset >= length, 1.0, 0.0))
    q_value = jnp.where(lane < 4, jnp.where(same, 0.0, big_negative), big_negative)
    k_side[slab] = jnp.where(lane < 5, k_value, 0.0).astype(jnp.bfloat16)
    q_side[slab] = jnp.where(lane < 5, q_value, 0.0).astype(jnp.bfloat16)


def meta_slabs(meta):
    return (meta.shape[0] - 2) // 5


def lane_low(row_count):
    return lax.broadcasted_iota(jnp.int32, (row_count, PAIR), 1) < HEAD_DIM


def attention_forward_kernel(meta, qkv, mixed, logsum, k_side, q_side):
    slab, pair = pl.program_id(1), pl.program_id(0)
    slab_rows = qkv.shape[1]

    @pl.when(pair == 0)
    def _():
        slab_features(meta, slab, slab_rows, k_side, q_side)

    low = lane_low(slab_rows)
    query, key = qkv[0].astype(jnp.float32), qkv[1].astype(jnp.float32)
    k_extra, q_extra = k_side[slab].astype(jnp.float32), q_side[slab].astype(jnp.float32)
    value_flip = flipped(qkv[2])
    sub = lax.broadcasted_iota(jnp.int32, (PAIR, slab_rows), 0)
    outcomes = []
    for head in range(2):
        mine = low if head == 0 else jnp.logical_not(low)
        q_head = jnp.where(mine, query, q_extra).astype(jnp.bfloat16)
        k_head = jnp.where(mine, key, k_extra).astype(jnp.bfloat16)
        scores = dot_nt(k_head, q_head)
        top = jnp.max(scores, axis=0, keepdims=True)
        weight = jnp.exp2((scores - top) * exponent_scale).astype(jnp.bfloat16)
        sum_row = HEAD_DIM if head == 0 else 0
        kept = sub < HEAD_DIM if head == 0 else sub >= HEAD_DIM
        v_head = jnp.where(kept, value_flip, jnp.where(sub == sum_row, 1.0, 0.0))
        blend = dot_nn(v_head.astype(jnp.bfloat16), weight)
        total = blend[sum_row : sum_row + 1, :]
        logsum[0, 0, head : head + 1, :] = top * exponent_scale + jnp.log(total) * log2_e
        outcomes.append(blend / total)
    mixed[...] = jnp.where(sub < HEAD_DIM, outcomes[0], outcomes[1]).T.astype(jnp.bfloat16)


def ffn_forward_kernel(pieces, meta, mixed, inputs, vectors, ffn_bias, *refs):
    out_sources, in_sources, down_sources, outputs, scratch = take(
        refs, *[len(piece.arrays) for piece in pieces], 8, 7
    )
    hidden, normed_one, spread_one, activated, slope, result, normed_two, spread_two = outputs
    out_whole, in_whole, down_whole, total, out_sems, in_sems, down_sems = scratch
    step = pl.program_id(0)
    steps = pl.num_programs(0)
    everything = slice(None)
    out_columns = out_whole.shape[2]
    tiles = row_tiles(inputs.shape[0])
    lanes = spread_one.shape[1]

    @pl.when(step == 0)
    def _():
        load_piece(meta, pieces[0], out_sources, out_whole, everything, out_sems)
        load_piece(meta, pieces[1], in_sources, in_whole, everything, in_sems)
        load_piece(meta, pieces[2], down_sources, down_whole, everything, down_sems)
        for half_at in range(2):
            await_piece(out_whole, half_at, everything, out_sems)
        for rows in tiles:
            attention_out = vectors[0:1, :]
            for half_at in range(2):
                columns = slice(half_at * out_columns, (half_at + 1) * out_columns)
                attention_out = attention_out + dot_nt(mixed[rows, columns], out_whole[half_at])
            normed, spread = norm_stats(inputs[rows, :].astype(jnp.float32) + attention_out)
            low = (normed * vectors[2:3, :] + vectors[4:5, :]).astype(jnp.bfloat16)
            hidden[rows, :] = low
            normed_one[rows, :] = normed.astype(jnp.bfloat16)
            spread_one[rows, :] = jnp.broadcast_to(spread, (spread.shape[0], lanes))
            total[rows, :] = low.astype(jnp.float32) + vectors[1:2, :]

    half_at = meta[1] ^ (step // FFN_PARTS)
    width = activated.shape[1]
    part = pl.ds(pl.multiple_of((step % FFN_PARTS) * width, 128), width)

    @pl.when(step % FFN_PARTS == 0)
    def _():
        await_piece(in_whole, half_at, everything, in_sems)
        await_piece(down_whole, half_at, everything, down_sems)

    for rows in tiles:
        pre_gelu = dot_nn(hidden[rows, :], in_whole[half_at, :, part]) + ffn_bias[0]
        value, steep = gelu_parts(pre_gelu)
        low = value.astype(jnp.bfloat16)
        activated[rows, :] = low
        slope[rows, :] = steep.astype(jnp.bfloat16)
        total[rows, :] += dot_nt(low, down_whole[half_at, :, part])

    @pl.when(step == steps - 1)
    def _():
        for rows in tiles:
            normed, spread = norm_stats(total[rows, :])
            result[rows, :] = (normed * vectors[3:4, :] + vectors[5:6, :]).astype(jnp.bfloat16)
            normed_two[rows, :] = normed.astype(jnp.bfloat16)
            spread_two[rows, :] = jnp.broadcast_to(spread, (spread.shape[0], lanes))


def ffn_backward_kernel(
    pieces, orders, target_count, meta, gradient, normed_two, spread_two, hidden, normed_one, spread_one,
    activated, slope, vectors, *refs
):
    in_sources, down_sources, outputs, targets, scratch = take(
        refs, *[len(piece.arrays) for piece in pieces], 4, target_count, 11
    )
    attention_grad, resid_grad, sums, bias_sums = outputs
    (
        in_whole, down_whole, total, branch, branch_flip, hidden_flip, pre_part, grad_parts,
        in_sems, down_sems, out_sems,
    ) = scratch
    step = pl.program_id(0)
    steps = pl.num_programs(0)
    everything = slice(None)
    tiles = row_tiles(hidden.shape[0])
    slot = step % 2

    @pl.when(step == 0)
    def _():
        load_piece(meta, pieces[0], in_sources, in_whole, everything, in_sems)
        load_piece(meta, pieces[1], down_sources, down_whole, everything, down_sems)
        gain_sum, shift_sum, branch_sum = 0.0, 0.0, 0.0
        for rows in tiles:
            grad = gradient[rows, :].astype(jnp.float32)
            normed = normed_two[rows, :].astype(jnp.float32)
            resid = norm_back(grad, normed, spread_two[rows, 0:1], vectors[3:4, :])
            low = resid.astype(jnp.bfloat16)
            total[rows, :] = resid
            branch[rows, :] = low
            branch_flip[:, rows] = flipped(low).astype(jnp.bfloat16)
            hidden_flip[:, rows] = flipped(hidden[rows, :]).astype(jnp.bfloat16)
            gain_sum += column_sum(grad * normed)
            shift_sum += column_sum(grad)
            branch_sum += column_sum(low.astype(jnp.float32))
        sums[...] = jnp.zeros(sums.shape, jnp.float32)
        sums[1:2, :] = branch_sum
        sums[3:4, :] = gain_sum
        sums[5:6, :] = shift_sum

    half_at = meta[1] ^ (step // FFN_PARTS)
    width = activated.shape[1]
    part = pl.ds(pl.multiple_of((step % FFN_PARTS) * width, 128), width)

    @pl.when(step % FFN_PARTS == 0)
    def _():
        await_piece(in_whole, half_at, everything, in_sems)
        await_piece(down_whole, half_at, everything, down_sems)

    @pl.when(step >= 2)
    def _():
        await_stored(grad_parts.at[slot, 0], out_sems.at[slot, 0])
        await_stored(grad_parts.at[slot, 1], out_sems.at[slot, 1])

    grad_parts[slot, 1] = dot_nn(branch_flip[...], activated[...]).astype(jnp.bfloat16)
    down_part = pl.ds(pl.multiple_of(FFN_PARTS * width + (step % FFN_PARTS) * width, 128), width)
    store_piece(
        meta, grad_parts.at[slot, 1], targets, orders[1], step // FFN_PARTS, down_part,
        out_sems.at[slot, 1],
    )
    bias_sum = 0.0
    for rows in tiles:
        active_grad = dot_nn(branch[rows, :], down_whole[half_at, :, part])
        low = (active_grad * slope[rows, :].astype(jnp.float32)).astype(jnp.bfloat16)
        pre_part[rows, :] = low
        bias_sum += column_sum(low.astype(jnp.float32))
        total[rows, :] += dot_nt(low, in_whole[half_at, :, part])
    bias_sums[0] = bias_sum
    grad_parts[slot, 0] = dot_nn(hidden_flip[...], pre_part[...]).astype(jnp.bfloat16)
    store_piece(
        meta, grad_parts.at[slot, 0], targets, orders[0], step // FFN_PARTS, part,
        out_sems.at[slot, 0],
    )

    @pl.when(step == steps - 1)
    def _():
        gain_sum, shift_sum, branch_sum = 0.0, 0.0, 0.0
        for rows in tiles:
            grad = total[rows, :]
            normed = normed_one[rows, :].astype(jnp.float32)
            resid = norm_back(grad, normed, spread_one[rows, 0:1], vectors[2:3, :])
            low = resid.astype(jnp.bfloat16)
            resid_grad[rows, :] = resid
            attention_grad[rows, :] = low
            gain_sum += column_sum(grad * normed)
            shift_sum += column_sum(grad)
            branch_sum += column_sum(low.astype(jnp.float32))
        sums[0:1, :] = branch_sum
        sums[2:3, :] = gain_sum
        sums[4:5, :] = shift_sum
        for late in range(2):
            await_stored(grad_parts.at[late, 0], out_sems.at[late, 0])
            await_stored(grad_parts.at[late, 1], out_sems.at[late, 1])


def out_backward_kernel(pieces, order, target_count, meta, attention_grad, mixed, *refs):
    sources, mixed_grad, targets, scratch = take(
        refs, len(pieces[0].arrays), None, target_count, 5
    )
    out_whole, grad_flip, grad_part, load_sem, out_sem = scratch
    tiles = row_tiles(mixed.shape[0])
    load_flat(meta, pieces[0], sources, out_whole, load_sem)
    for rows in tiles:
        grad_flip[:, rows] = flipped(attention_grad[rows, :]).astype(jnp.bfloat16)
    grad_part[...] = dot_nn(grad_flip[...], mixed[...]).astype(jnp.bfloat16)
    store_flat(meta, grad_part, targets, order, slice(None), out_sem)
    await_stored(out_whole, load_sem)
    for rows in tiles:
        mixed_grad[rows, :] = dot_nn(attention_grad[rows, :], out_whole[...]).astype(jnp.bfloat16)
    await_stored(grad_part, out_sem)


def attention_backward_kernel(meta, qkv, mixed, mixed_grad, logsum, grads, sums, k_side, q_side):
    slab, pair = pl.program_id(1), pl.program_id(0)
    slab_rows = qkv.shape[1]

    @pl.when(pair == 0)
    def _():
        slab_features(meta, slab, slab_rows, k_side, q_side)

    low = lane_low(slab_rows)
    query, key, value = (qkv[place].astype(jnp.float32) for place in range(3))
    k_extra, q_extra = k_side[slab].astype(jnp.float32), q_side[slab].astype(jnp.float32)
    grad_low = mixed_grad[...]
    grad = grad_low.astype(jnp.float32)
    product = (grad * mixed[...].astype(jnp.float32)).T
    key_flip = key.T
    sub = lax.broadcasted_iota(jnp.int32, (PAIR, slab_rows), 0)
    query_flip, key_grad, value_grad = 0.0, 0.0, 0.0
    for head in range(2):
        mine = low if head == 0 else jnp.logical_not(low)
        kept = sub < HEAD_DIM if head == 0 else sub >= HEAD_DIM
        span = slice(head * HEAD_DIM, (head + 1) * HEAD_DIM)
        q_head = jnp.where(mine, query, q_extra).astype(jnp.bfloat16)
        k_head = jnp.where(mine, key, k_extra).astype(jnp.bfloat16)
        v_head = jnp.where(mine, value, 0.0).astype(jnp.bfloat16)
        probs = jnp.exp2(
            dot_nt(k_head, q_head) * exponent_scale - logsum[0, 0, head : head + 1, :]
        )
        delta = column_sum(product[span, :])
        raw_grad = (probs * (dot_nt(v_head, grad_low) - delta)).astype(jnp.bfloat16)
        g_head = jnp.where(mine, grad, 0.0).astype(jnp.bfloat16)
        value_grad += dot_nn(probs.astype(jnp.bfloat16), g_head)
        key_grad += dot_nn(raw_grad, jnp.where(mine, query, 0.0).astype(jnp.bfloat16))
        query_flip += dot_nn(jnp.where(kept, key_flip, 0.0).astype(jnp.bfloat16), raw_grad)
    query_low = (query_flip * score_scale).T.astype(jnp.bfloat16)
    value_low = value_grad.astype(jnp.bfloat16)
    grads[0] = query_low
    grads[1] = (key_grad * score_scale).astype(jnp.bfloat16)
    grads[2] = value_low

    @pl.when(slab == 0)
    def _():
        sums[...] = jnp.zeros(sums.shape, jnp.float32)

    sums[0:1, :] += column_sum(query_low.astype(jnp.float32))
    sums[1:2, :] += column_sum(value_low.astype(jnp.float32))


def qkv_grad_kernel(orders, target_count, meta, inputs, grads, *refs):
    targets, (inputs_flip, grad_parts, out_sems) = take(refs, target_count, 3)
    step = pl.program_id(0)
    columns = grads.shape[2] // 2

    @pl.when(step == 0)
    def _():
        for rows in row_tiles(inputs.shape[0]):
            inputs_flip[:, rows] = flipped(inputs[rows, :]).astype(jnp.bfloat16)

    grad_parts[step] = dot_nn(inputs_flip[...], grads[0]).astype(jnp.bfloat16)
    for which, order in enumerate((orders[0], orders[1], orders[1])):

        @pl.when(step == which)
        def _():
            span = slice(which * columns, (which + 1) * columns)
            store_flat(meta, grad_parts.at[which], targets, order, span, out_sems.at[which])

    @pl.when(step == 2)
    def _():
        for which in range(3):
            await_stored(grad_parts.at[which], out_sems.at[which])


def input_grad_kernel(pieces, meta, grads, resid_grad, *refs):
    *sources, outputs, (weights, sems) = take(
        refs, *[len(piece.arrays) for piece in pieces], len(refs) - 2 - sum(
            len(piece.arrays) for piece in pieces
        ), 2,
    )
    input_grad = outputs[0]
    step = pl.program_id(0)
    tiles = row_tiles(resid_grad.shape[0])

    @pl.when(step == 0)
    def _():
        for which, piece in enumerate(pieces):
            load_flat(meta, piece, sources[which], weights.at[which], sems.at[which])
        for rows in tiles:
            input_grad[rows, :] = resid_grad[rows, :]

    await_stored(weights.at[step], sems.at[step])
    for rows in tiles:
        input_grad[rows, :] += dot_nt(grads[0, rows, :], weights[step])

    if len(outputs) > 1:

        @pl.when(step == 2)
        def _():
            outputs[1][...] = input_grad[...].astype(jnp.bfloat16)


def fixed(shape):
    return pl.BlockSpec(
        shape, lambda *_: (0,) * len(shape), pipeline_mode=pl.Buffered(1)
    )


def fixed_out(shape):
    return pl.BlockSpec(shape, lambda *_: (0,) * len(shape))


ANYWHERE = pl.BlockSpec(memory_space=pl.ANY)


def run_kernel(kernel, meta, grid, ins, outs, scratch, flops, moved, name, after=()):
    used = len(ins)
    ins = list(ins) + [(ANYWHERE, member) for member in after]
    in_specs, operands = zip(*ins)
    out_specs, out_shapes = zip(*outs)

    def body(meta_ref, *refs):
        kernel(meta_ref, *refs[:used], *refs[len(ins) :])

    return pl.pallas_call(
        body,
        grid_spec=pltpu.PrefetchScalarGridSpec(
            num_scalar_prefetch=1,
            grid=grid,
            in_specs=list(in_specs),
            out_specs=list(out_specs),
            scratch_shapes=scratch,
        ),
        out_shape=list(out_shapes),
        compiler_params=pltpu.CompilerParams(vmem_limit_bytes=VMEM_LIMIT),
        cost_estimate=pl.CostEstimate(flops=(BACK_WEIGHT if "forward" not in name else COST_WEIGHT) * flops, bytes_accessed=moved, transcendentals=0),
        name=name,
    )(meta, *operands)


def low_shape(*shape):
    return jax.ShapeDtypeStruct(shape, jnp.bfloat16)


def full_shape(*shape):
    return jax.ShapeDtypeStruct(shape, jnp.float32)


def pair_sems():
    return pltpu.SemaphoreType.DMA((2,))


def half_of(step, meta, count):
    return meta[1] ^ (step // count)


def sources_of(pieces):
    return [(ANYWHERE, member) for piece in pieces for member in piece.arrays]


def targets_of(routed, split, width, block_rows, columns):
    if routed:
        shape = low_shape(split * width // (2 * block_rows), block_rows, columns)
        return [(ANYWHERE, shape), (ANYWHERE, shape)]
    return [(ANYWHERE, low_shape(split, width, columns))]


def three_sems():
    return pltpu.SemaphoreType.DMA((3,))


def qkv_forward(meta, inputs, bias, pieces, after=()):
    rows, width = inputs.shape
    (qkv,) = run_kernel(
        functools.partial(qkv_forward_kernel, pieces),
        meta,
        (3,),
        [
            (fixed((rows, width)), inputs),
            (pl.BlockSpec((1, 1, width), lambda i, m: (i, 0, 0)), bias),
        ]
        + sources_of(pieces),
        [(pl.BlockSpec((1, rows, width), lambda i, m: (i, 0, 0)), low_shape(3, rows, width))],
        [pltpu.VMEM((3, width, width), jnp.bfloat16), three_sems()],
        6 * rows * width * width,
        8 * rows * width + 6 * width * width,
        "qkv_forward",
        after,
    )
    return qkv


def attention_forward(meta, qkv, slab_count, after=()):
    _, rows, width = qkv.shape
    slab_rows = rows // slab_count
    pairs = width // PAIR
    return run_kernel(
        attention_forward_kernel,
        meta,
        (pairs, slab_count),
        [(pl.BlockSpec((3, slab_rows, PAIR), lambda p, s, m: (0, s, p)), qkv)],
        [
            (pl.BlockSpec((slab_rows, PAIR), lambda p, s, m: (s, p)), low_shape(rows, width)),
            (
                pl.BlockSpec((1, 1, 8, slab_rows), lambda p, s, m: (s, p, 0, 0)),
                full_shape(slab_count, pairs, 8, slab_rows),
            ),
        ],
        [pltpu.VMEM((slab_count, slab_rows, PAIR), jnp.bfloat16)] * 2,
        16 * rows * slab_rows * width,
        8 * rows * width,
        "attention_forward",
        after,
    )


def ffn_forward(meta, mixed, inputs, vectors, ffn_bias, pieces, after=()):
    rows, width = inputs.shape
    half_width = pieces[1].count
    part = half_width // FFN_PARTS

    def part_at(i, m):
        return half_of(i, m, FFN_PARTS) * FFN_PARTS + i % FFN_PARTS

    whole_rows = (fixed_out((rows, width)), low_shape(rows, width))
    spread = (fixed_out((rows, 128)), full_shape(rows, 128))
    inner = (
        pl.BlockSpec((rows, part), lambda i, m: (0, part_at(i, m))),
        low_shape(rows, 2 * half_width),
    )
    return run_kernel(
        functools.partial(ffn_forward_kernel, pieces),
        meta,
        (2 * FFN_PARTS,),
        [
            (fixed((rows, width)), mixed),
            (fixed((rows, width)), inputs),
            (fixed((8, width)), vectors),
            (pl.BlockSpec((1, 1, part), lambda i, m: (part_at(i, m), 0, 0)), ffn_bias),
        ]
        + sources_of(pieces),
        [whole_rows, whole_rows, spread, inner, inner, whole_rows, whole_rows, spread],
        [
            pltpu.VMEM((2, width, width // 2), jnp.bfloat16),
            pltpu.VMEM((2, width, half_width), jnp.bfloat16),
            pltpu.VMEM((2, width, half_width), jnp.bfloat16),
            pltpu.VMEM((rows, width), jnp.float32),
            pair_sems(),
            pair_sems(),
            pair_sems(),
        ],
        8 * rows * width * half_width,
        24 * rows * width + 8 * width * half_width,
        "ffn_forward",
        after,
    )


def ffn_backward(meta, gradient, kept, vectors, pieces, orders, targets, after=()):
    hidden, normed_one, spread_one, activated, slope, normed_two, spread_two = kept
    rows, width = hidden.shape
    half_width = pieces[0].count
    part = half_width // FFN_PARTS

    def part_at(i, m):
        return half_of(i, m, FFN_PARTS) * FFN_PARTS + i % FFN_PARTS

    low_rows = fixed((rows, width))
    spread = fixed((rows, 128))
    inner = pl.BlockSpec((rows, part), lambda i, m: (0, part_at(i, m)))
    return run_kernel(
        functools.partial(ffn_backward_kernel, pieces, orders, len(targets)),
        meta,
        (2 * FFN_PARTS,),
        [
            (low_rows, gradient),
            (low_rows, normed_two),
            (spread, spread_two),
            (low_rows, hidden),
            (low_rows, normed_one),
            (spread, spread_one),
            (inner, activated),
            (inner, slope),
            (fixed((8, width)), vectors),
        ]
        + sources_of(pieces),
        [
            (fixed_out((rows, width)), low_shape(rows, width)),
            (fixed_out((rows, width)), full_shape(rows, width)),
            (fixed_out((8, width)), full_shape(8, width)),
            (
                pl.BlockSpec((1, 1, part), lambda i, m: (part_at(i, m), 0, 0)),
                full_shape(2 * FFN_PARTS, 1, part),
            ),
        ]
        + targets,
        [
            pltpu.VMEM((2, width, half_width), jnp.bfloat16),
            pltpu.VMEM((2, width, half_width), jnp.bfloat16),
            pltpu.VMEM((rows, width), jnp.float32),
            pltpu.VMEM((rows, width), jnp.bfloat16),
            pltpu.VMEM((width, rows), jnp.bfloat16),
            pltpu.VMEM((width, rows), jnp.bfloat16),
            pltpu.VMEM((rows, part), jnp.bfloat16),
            pltpu.VMEM((2, 2, width, part), jnp.bfloat16),
            pair_sems(),
            pair_sems(),
            pltpu.SemaphoreType.DMA((2, 2)),
        ],
        16 * rows * width * half_width,
        40 * rows * width + 16 * width * half_width,
        "ffn_backward",
        after,
    )


def out_backward(meta, attention_grad, mixed, piece, order, targets, after=()):
    rows, width = mixed.shape
    return run_kernel(
        functools.partial(out_backward_kernel, [piece], order, len(targets)),
        meta,
        (1,),
        [(fixed((rows, width)), attention_grad), (fixed((rows, width)), mixed)]
        + sources_of([piece]),
        [(fixed_out((rows, width)), low_shape(rows, width))] + targets,
        [
            pltpu.VMEM((width, width), jnp.bfloat16),
            pltpu.VMEM((width, rows), jnp.bfloat16),
            pltpu.VMEM((width, width), jnp.bfloat16),
            pltpu.SemaphoreType.DMA,
            pltpu.SemaphoreType.DMA,
        ],
        4 * rows * width * width,
        6 * rows * width + 4 * width * width,
        "out_backward",
        after,
    )


def attention_backward(meta, qkv, mixed, mixed_grad, logsum, slab_count, after=()):
    _, rows, width = qkv.shape
    slab_rows = rows // slab_count
    pairs = width // PAIR
    three = pl.BlockSpec((3, slab_rows, PAIR), lambda p, s, m: (0, s, p))
    one = pl.BlockSpec((slab_rows, PAIR), lambda p, s, m: (s, p))
    return run_kernel(
        attention_backward_kernel,
        meta,
        (pairs, slab_count),
        [
            (three, qkv),
            (one, mixed),
            (one, mixed_grad),
            (pl.BlockSpec((1, 1, 8, slab_rows), lambda p, s, m: (s, p, 0, 0)), logsum),
        ],
        [
            (three, low_shape(3, rows, width)),
            (pl.BlockSpec((8, PAIR), lambda p, s, m: (0, p)), full_shape(8, width)),
        ],
        [pltpu.VMEM((slab_count, slab_rows, PAIR), jnp.bfloat16)] * 2,
        40 * rows * slab_rows * width,
        16 * rows * width,
        "attention_backward",
        after,
    )


def qkv_grad(meta, inputs, grads, orders, targets, after=()):
    rows, width = inputs.shape
    return run_kernel(
        functools.partial(qkv_grad_kernel, orders, len(targets)),
        meta,
        (3,),
        [
            (fixed((rows, width)), inputs),
            (pl.BlockSpec((1, rows, width), lambda i, m: (i, 0, 0)), grads),
        ],
        targets,
        [
            pltpu.VMEM((width, rows), jnp.bfloat16),
            pltpu.VMEM((3, width, width), jnp.bfloat16),
            three_sems(),
        ],
        6 * rows * width * width,
        8 * rows * width + 6 * width * width,
        "qkv_grad",
        after,
    )


def input_gradient(meta, grads, resid_grad, pieces, after=(), low=False):
    rows, width = resid_grad.shape
    outs = [(fixed_out((rows, width)), full_shape(rows, width))]
    if low:
        outs.append((fixed_out((rows, width)), low_shape(rows, width)))
    return run_kernel(
        functools.partial(input_grad_kernel, pieces),
        meta,
        (3,),
        [
            (pl.BlockSpec((1, rows, width), lambda i, m: (i, 0, 0)), grads),
            (fixed((rows, width)), resid_grad),
        ]
        + sources_of(pieces),
        outs,
        [pltpu.VMEM((3, width, width), jnp.bfloat16), three_sems()],
        6 * rows * width * width,
        14 * rows * width + 6 * width * width,
        "input_gradient",
        after,
    )


def both_halves(mine, theirs, place):
    first = jnp.concatenate([mine, theirs], axis=0)
    second = jnp.concatenate([theirs, mine], axis=0)
    return jnp.where(place == 0, first, second)


def on_device(
    tokens,
    cotangent,
    buckets,
    lengths,
    qkv_weight,
    qv_bias,
    out_weight,
    ffn_in_weight,
    ffn_in_bias,
    ffn_out_weight,
    out_bias,
    norm_gain,
    norm_bias,
):
    split = lax.axis_size("tensor")
    dp_size = lax.axis_size("dp")
    place = lax.axis_index("tensor")
    width = tokens.shape[1]
    rows = tokens.shape[0] // split
    slabs = buckets.shape[0] // split
    layer_count = qkv_weight.shape[0]
    block_rows = width // dp_size
    routed = block_rows % TILE_ROWS == 0 and dp_size & (dp_size - 1) == 0
    orders = hop_orders(dp_size if routed else PLANNED_BLOCKS)

    own_tokens = lax.dynamic_slice_in_dim(tokens, place * rows, rows)
    own_cotangent = lax.dynamic_slice_in_dim(cotangent, place * rows, rows)
    own_buckets = lax.dynamic_slice_in_dim(buckets, place * slabs, slabs)
    own_lengths = lax.dynamic_slice_in_dim(lengths, place * slabs, slabs)
    if routed:
        position = jnp.stack([lax.axis_index("dp"), place]).astype(jnp.int32)
    else:
        position = jnp.zeros((2,), jnp.int32)
    meta = jnp.concatenate([position, own_buckets, own_lengths.reshape(-1)])

    bias_flat = jnp.concatenate([qv_bias.reshape(layer_count, -1), ffn_in_bias], axis=1)
    bias_other = hop(bias_flat, ("tensor", 1))
    bias_halves = jnp.where(
        place == 0, jnp.stack([bias_flat, bias_other]), jnp.stack([bias_other, bias_flat])
    )
    qv_columns = qv_bias.shape[2]
    ffn_columns = ffn_in_bias.shape[1]

    def small_inputs(index):
        halves = bias_halves[:, index]
        value = halves[:, : 2 * qv_columns].reshape(2, 2, qv_columns)
        zero = jnp.zeros((2, qv_columns), jnp.float32)
        bias = jnp.stack([value[:, 0], zero, value[:, 1]]).reshape(3, 1, -1)
        vectors = jnp.concatenate(
            [out_bias[index], norm_gain[index], norm_bias[index], jnp.zeros((2, width), jnp.float32)]
        )
        return bias, vectors, halves[:, 2 * qv_columns :].reshape(2 * FFN_PARTS, 1, -1)

    def gathering(flag, *members):
        shard = jnp.concatenate(members, axis=1)
        return (Gathering if flag else WholeGathering)(shard, orders)

    def attention_split(pieces):
        half = width // 2
        query_key, value_out = pieces
        qkv = [query_key.narrow(0, half), query_key.narrow(half, half), value_out.narrow(0, half)]
        return qkv, value_out.narrow(half, half)

    hops_back = [[routed and flag for flag in flags] for flags in HOPS_BACK]

    def waits(flag, members):
        return list(members) if flag else []

    first = gathering(routed, *qkv_weight[0], out_weight[0])
    first_ffn = gathering(False, ffn_in_weight[0], ffn_out_weight[0])
    second = gathering(routed, *qkv_weight[1], out_weight[1])
    if SPLIT_DOWN:
        second_in = gathering(False, ffn_in_weight[1])
        second_down = gathering(routed, ffn_out_weight[1])
    else:
        second_in = gathering(False, ffn_in_weight[1], ffn_out_weight[1])
        second_down = second_in
    first.send_far()
    first.land_far()
    first.send_middle()
    first.land_middle()
    last = first.send_last()
    first.send_core()
    second.send_far(*waits(routed, last))
    bias, vectors, ffn_bias = small_inputs(0)
    qkv_pieces, out_piece = attention_split(first.pieces())
    qkv = qkv_forward(meta, own_tokens, bias, qkv_pieces)
    second.land_far(qkv)
    second.send_middle(qkv)
    mixed, logsum = attention_forward(meta, qkv, slabs)
    second.land_middle(mixed)
    second_last = second.send_last(mixed)
    if SPLIT_DOWN:
        second_down.send_far(mixed)
    first_pieces = (qkv_pieces, out_piece, first_ffn.pieces())
    out = ffn_forward(
        meta, mixed, own_tokens, vectors, ffn_bias, [out_piece] + first_pieces[2]
    )
    kept_layers = [(own_tokens, qkv, mixed, logsum, vectors, out)]
    layer_one = out[5]
    second.send_core(layer_one)
    if SPLIT_DOWN:
        second_down.land_far(layer_one)
        second_down.send_middle(layer_one)
    bias, vectors, ffn_bias = small_inputs(1)
    qkv_pieces, out_piece = attention_split(second.pieces())
    qkv = qkv_forward(meta, layer_one, bias, qkv_pieces, waits(routed, second_last))
    if SPLIT_DOWN:
        second_down.land_middle(qkv)
        second_down.send_last(qkv)
    mixed, logsum = attention_forward(meta, qkv, slabs)
    if SPLIT_DOWN:
        second_down.send_core(mixed)
        ffn_pieces = [Joined(second_in.pieces()), Joined(second_down.pieces())]
    else:
        ffn_pieces = second_in.pieces()
    one_other = hop(tied(layer_one, [mixed]), ("tensor", 1))
    second_pieces = (qkv_pieces, out_piece, ffn_pieces)
    out = ffn_forward(
        meta, mixed, layer_one, vectors, ffn_bias, [out_piece] + second_pieces[2]
    )
    kept_layers.append((layer_one, qkv, mixed, logsum, vectors, out))
    layer_two = out[5]
    two_other = hop(layer_two, ("tensor", 1))
    layer_one_whole = both_halves(layer_one, tied(one_other, [layer_two]), place)

    def targets(flag, columns):
        return targets_of(flag, split, width, block_rows, columns)

    def scattering(flag, members, sides):
        kind = Scattering if flag else WholeScattering
        return kind(members, orders, sides)

    half_ffn = ffn_in_weight.shape[2]

    def ffn_back(index, gradient, pieces, after=()):
        inputs, qkv, mixed, logsum, vectors, out = kept_layers[index]
        hidden, normed_one, spread_one, activated, slope, _, normed_two, spread_two = out
        kept = (hidden, normed_one, spread_one, activated, slope, normed_two, spread_two)
        attention_grad, resid_grad, sums, ffn_sums, *members = ffn_backward(
            meta, gradient, kept, vectors, pieces[2], orders, targets(hops_back[index][1], 2 * half_ffn), after
        )
        scatter = scattering(
            hops_back[index][1], [members], [[(0, 0, half_ffn)], [(0, half_ffn, 2 * half_ffn)]]
        )
        return attention_grad, resid_grad, (sums, ffn_sums), scatter

    def out_back(index, attention_grad, pieces, after=()):
        mixed = kept_layers[index][2]
        return out_backward(
            meta, attention_grad, mixed, pieces[1], orders[0], targets(hops_back[index][0], width // 2), after
        )

    def attention_back(index, mixed_grad, after=()):
        _, qkv, mixed, logsum, _, _ = kept_layers[index]
        return attention_backward(meta, qkv, mixed, mixed_grad, logsum, slabs, after)

    def qkv_grads(index, grads, out_members, after=()):
        members = qkv_grad(
            meta, kept_layers[index][0], grads, orders,
            targets(hops_back[index][0], 3 * width // 2), after,
        )
        columns = width // 2
        return scattering(
            hops_back[index][0],
            [out_members, members],
            [[(0, 0, columns), (1, 0, columns)], [(1, columns, 3 * columns)]],
        )

    def flat_smalls(sums, ffn_sums, qkv_sums):
        return jnp.concatenate(
            [sums[:6].reshape(-1), qkv_sums[:2].reshape(-1), ffn_sums.reshape(-1)]
        )

    attention_grad, resid_grad, sums, ffn_one = ffn_back(1, own_cotangent, second_pieces, [one_other])
    layer_two_whole = both_halves(layer_two, tied(two_other, [attention_grad]), place)
    ffn_one.send_core()
    mixed_grad, *out_members = out_back(1, attention_grad, second_pieces, [two_other])
    ffn_one.land_core(mixed_grad)
    ffn_one.send_last(mixed_grad)
    grads, qkv_sums = attention_back(1, mixed_grad)
    ffn_one.land(grads)
    smalls_one = flat_smalls(*sums, qkv_sums)
    attention_one = qkv_grads(1, grads, out_members)
    begun = attention_one.begun
    one_core = attention_one.send_core()
    ffn_one.send_middle(*begun)
    (gradient,) = input_gradient(meta, grads, resid_grad, second_pieces[0], begun)
    attention_one.land_core(gradient)
    ffn_one.land(gradient)
    one_last = attention_one.send_last(gradient)
    ffn_one.send_far(gradient)
    attention_grad, resid_grad, sums, ffn_zero = ffn_back(
        0, gradient, first_pieces, waits(hops_back[1][0], one_core)
    )
    attention_one.land(attention_grad)
    ffn_one.land_far(attention_grad)
    one_middle = attention_one.send_middle(attention_grad)
    zero_core = ffn_zero.send_core(attention_grad)
    mixed_grad, *out_members = out_back(
        0, attention_grad, first_pieces, waits(hops_back[1][0], one_last)
    )
    ffn_zero.land_core(mixed_grad)
    attention_one.land(mixed_grad)
    ffn_last = ffn_zero.send_last(mixed_grad)
    one_far = attention_one.send_far(mixed_grad)
    grads, qkv_sums = attention_back(0, mixed_grad, waits(routed, one_middle + zero_core))
    ffn_zero.land(grads)
    attention_one.land_far(grads)
    smalls_zero = flat_smalls(*sums, qkv_sums)
    totals = Totals(jnp.stack([smalls_zero, smalls_one]), routed)
    totals.send("dp", 1, 4, grads)
    zero_middle = ffn_zero.send_middle(grads)
    attention_zero = qkv_grads(0, grads, out_members, waits(routed, ffn_last + one_far))
    begun = attention_zero.begun
    totals.land(*begun)
    totals.send("dp", 4, dp_size // 4, *begun)
    attention_zero.send_core(*begun)
    gradient, token_low = input_gradient(
        meta, grads, resid_grad, first_pieces[0], begun, True
    )
    totals.land(gradient)
    attention_zero.land_core(gradient)
    zero_last = attention_zero.send_last(gradient)
    ffn_zero.land(gradient)
    ffn_zero.send_far(gradient)
    if HOLD_TOKENS:
        token_low = tied(token_low, waits(routed, zero_last))
    token_other = hop(token_low, ("tensor", 1))
    totals.send("tensor", 1, 2, gradient, *waits(routed, zero_last))
    attention_zero.land(gradient)
    zero_middle = attention_zero.send_middle(gradient)
    totals.land(gradient, *waits(routed, zero_middle))
    smalls = totals.total
    ffn_zero.land_far(gradient, *waits(routed, zero_middle))
    attention_zero.land(gradient)
    attention_zero.send_far(gradient)
    attention_zero.land_far(gradient)
    token_grad = both_halves(gradient, token_other.astype(jnp.float32), place)
    matrix_grads = []
    for attention, ffn in ((attention_zero, ffn_zero), (attention_one, ffn_one)):
        out_part, *qkv_parts = jnp.split(attention.result, 4, axis=1)
        matrix_grads.append((jnp.stack(qkv_parts), out_part, *jnp.split(ffn.result, 2, axis=1)))
    eight = smalls[:, : 8 * width].reshape(layer_count, 4, 2, width)
    ffn_total = smalls[:, 8 * width :]
    return (
        layer_one_whole,
        layer_two_whole,
        token_grad,
        jnp.stack([member[0] for member in matrix_grads]),
        lax.dynamic_slice_in_dim(eight[:, 3], place * qv_columns, qv_columns, axis=2),
        jnp.stack([member[1] for member in matrix_grads]),
        jnp.stack([member[2] for member in matrix_grads]),
        lax.dynamic_slice_in_dim(ffn_total, place * ffn_columns, ffn_columns, axis=1),
        jnp.stack([member[3] for member in matrix_grads]),
        eight[:, 0],
        eight[:, 1],
        eight[:, 2],
    )


def solution(mesh):
    placed = (
        P("dp", None),
        P("dp", None),
        P("dp"),
        P("dp", None),
        P(None, None, "dp", "tensor"),
        P(None, None, "tensor"),
        P(None, "dp", "tensor"),
        P(None, "dp", "tensor"),
        P(None, "tensor"),
        P(None, "dp", "tensor"),
        P(),
        P(),
        P(),
    )
    return jax.shard_map(
        on_device,
        mesh=mesh,
        in_specs=placed,
        out_specs=(
            P("dp", None),
            P("dp", None),
            P("dp", None),
            P(None, None, "dp", "tensor"),
            P(None, None, "tensor"),
            P(None, "dp", "tensor"),
            P(None, "dp", "tensor"),
            P(None, "tensor"),
            P(None, "dp", "tensor"),
            P(),
            P(),
            P(),
        ),
        check_vma=False,
    )
```

```python
import functools

import jax
import jax.numpy as jnp
from jax import lax
from jax.experimental import pallas as pl
from jax.experimental.pallas import tpu as pltpu
from jax.sharding import PartitionSpec as P

HEAD_DIM = 64
PAIR = 2 * HEAD_DIM
AXES = ("tensor", "dp")
CORE = ("dp", 1)
FFN_PARTS = 2
ROW_TILE = 512
TILE_ROWS = 16
PLANNED_BLOCKS = 16
HOPS_BACK = ((True, True), (True, False))
COST_WEIGHT = 8
BACK_WEIGHT = 16
SPLIT_DOWN = False
HOLD_TOKENS = True
VMEM_LIMIT = 58 * 1024 * 1024

norm_eps = 1e-06
big_negative = -1e30
inv_root_tau = 0.3989422804014327
log2_e = 1.4426950408889634
score_scale = HEAD_DIM ** (-0.5)
exponent_scale = score_scale * log2_e
erf_slope = 0.3275911 * 0.7071067811865476
erf_terms = (1.061405429, -1.453152027, 1.421413741, -0.284496736, 0.254829592)


def dot_nn(left, right):
    return lax.dot_general(
        left, right, (((1,), (0,)), ((), ())), preferred_element_type=jnp.float32
    )


def dot_nt(left, right):
    return lax.dot_general(
        left, right, (((1,), (1,)), ((), ())), preferred_element_type=jnp.float32
    )


def flipped(member):
    return member.astype(jnp.float32).T


def hop_orders(block_count):
    far = []
    bit = 4
    while bit < block_count:
        far.append(("dp", bit))
        bit *= 2
    across, along = ("dp", 2), ("tensor", 1)
    return (far + [across, along], far + [along, across])


def slot_table(order):
    table = []
    for slot in range(2 ** len(order)):
        dp_part, tensor_part = 0, 0
        for position, (axis, bit) in enumerate(order):
            if slot >> position & 1:
                if axis == "dp":
                    dp_part ^= bit
                else:
                    tensor_part ^= bit
        table.append((dp_part, tensor_part))
    return table


def hop(member, dim):
    axis, bit = dim
    pairs = [(place, place ^ bit) for place in range(lax.axis_size(axis))]
    return lax.ppermute(member, axis, pairs)


def tied(member, others):
    return lax.optimization_barrier((member, *others))[0] if others else member


class Piece:
    def __init__(self, arrays, order, first, count):
        self.arrays, self.order, self.columns = tuple(arrays), order, slice(first, first + count)
        self.count = count

    def narrow(self, first, count):
        return Piece(self.arrays, self.order, self.columns.start + first, count)


class Joined:
    def __init__(self, parts):
        self.parts, self.count = tuple(parts), sum(part.count for part in parts)
        self.arrays = tuple(member for part in parts for member in part.arrays)


class Gathering:
    def __init__(self, shard, orders):
        self.shard, self.orders, self.width = shard[None], orders, shard.shape[1] // 2

    def halves(self, member):
        return [member[..., : self.width], member[..., self.width :]]

    def send_far(self, *others):
        shard = tied(self.shard, others)
        count = 2 ** (len(self.orders[0]) - 2)
        self.coming = [hop(shard, ("dp", 4 * step)) for step in range(1, count)]

    def land_far(self, *others):
        parts = [self.shard] + [tied(member, others) for member in self.coming]
        self.current = [
            jnp.concatenate(sides, axis=0) for sides in zip(*[self.halves(part) for part in parts])
        ]
        return self.current

    def send_middle(self, *others):
        self.coming = [
            hop(tied(member, others), order[-2])
            for member, order in zip(self.current, self.orders)
        ]

    def land_middle(self, *others):
        self.current = [
            jnp.concatenate([member, tied(come, others)], axis=0)
            for member, come in zip(self.current, self.coming)
        ]
        return self.current

    def send_last(self, *others):
        current = [tied(member, others) for member in self.current]
        self.later = [hop(member, order[-1]) for member, order in zip(current, self.orders)]
        self.core_current = [hop(member, CORE) for member in current]
        return self.later

    def send_core(self, *others):
        self.core_later = [hop(tied(member, others), CORE) for member in self.later]
        return self.core_later

    def pieces(self):
        sides = zip(self.current, self.later, self.core_current, self.core_later)
        return [Piece(side, order, 0, self.width) for side, order in zip(sides, self.orders)]


class WholeGathering:
    def __init__(self, shard, orders):
        self.width, self.orders = shard.shape[1] // 2, orders
        whole = lax.all_gather(shard, AXES, tiled=True)
        self.whole = whole.reshape(lax.axis_size("tensor"), -1, shard.shape[1])

    def send_far(self, *others):
        return []

    land_far = send_middle = land_middle = send_last = send_core = send_far

    def pieces(self):
        return [
            Piece([self.whole], order, side * self.width, self.width)
            for side, order in enumerate(self.orders)
        ]


class Scattering:
    def __init__(self, members, orders, sides):
        self.members, self.orders, self.sides = members, orders, sides
        self.begun = [members[-1][0]]

    def send_core(self, *others):
        self.coming = [hop(tied(send, others), CORE) for keep, send in self.members]
        return self.coming

    def land_core(self, *others):
        both = [
            [keep, tied(come, others)] for (keep, send), come in zip(self.members, self.coming)
        ]
        self.parts = [
            [[part[..., first:end] for part in both[member]] for member, first, end in side]
            for side in self.sides
        ]

    def total(self, side, take):
        sums = [
            sum(take(part).astype(jnp.float32) for part in group) for group in self.parts[side]
        ]
        return jnp.concatenate(sums, axis=-1) if len(sums) > 1 else sums[0]

    def halve(self, which, others):
        self.coming = []
        for side, order in enumerate(self.orders):
            half = self.parts[side][0][0].shape[0] // 2
            upper = self.total(side, lambda part: part[half:]).astype(jnp.bfloat16)
            self.coming.append(hop(tied(upper, others), order[which]))
        return self.coming

    def land(self, *others):
        for groups, come in zip(self.parts, self.coming):
            come, at = tied(come, others), 0
            for group in groups:
                width, half = group[0].shape[-1], group[0].shape[0] // 2
                group[:] = [part[:half] for part in group] + [come[..., at : at + width]]
                at += width

    def send_last(self, *others):
        return self.halve(-1, others)

    def send_middle(self, *others):
        return self.halve(-2, others)

    def send_far(self, *others):
        count = self.parts[0][0][0].shape[0]
        sides = range(len(self.orders))
        self.mine = jnp.concatenate(
            [self.total(side, lambda part: part[0]) for side in sides], axis=-1
        )
        self.coming = []
        for step in range(1, count):
            upper = jnp.concatenate(
                [self.total(side, lambda part: part[step]) for side in sides], axis=-1
            )
            self.coming.append(hop(tied(upper.astype(jnp.bfloat16), others), ("dp", 4 * step)))
        return self.coming

    def land_far(self, *others):
        come = [tied(part, others).astype(jnp.float32) for part in self.coming]
        self.result = sum([self.mine] + come)
        return [self.result]


class WholeScattering:
    def __init__(self, members, orders, sides):
        self.begun = [members[-1][0]]
        mine = [
            lax.psum_scatter(
                whole.reshape(-1, whole.shape[2]), AXES, scatter_dimension=0, tiled=True
            ).astype(jnp.float32)
            for (whole,) in members
        ]
        taken = [mine[member][:, first:end] for side in sides for member, first, end in side]
        self.result = jnp.concatenate(taken, axis=-1)

    def send_core(self, *others):
        return []

    land_core = send_last = send_middle = land = send_far = land_far = send_core


class Totals:
    def __init__(self, member, routed):
        self.routed, self.total = routed, member if routed else lax.psum(member, AXES)

    def send(self, axis, first, count, *others):
        if self.routed:
            total = tied(self.total, others)
            self.place = lax.axis_index(axis) // first % count
            self.coming = [hop(total, (axis, first * step)) for step in range(1, count)]

    def land(self, *others):
        if self.routed:
            stacked = jnp.stack([self.total] + [tied(come, others) for come in self.coming])
            self.total = sum(stacked[self.place ^ step] for step in range(len(self.coming) + 1))


def load_piece(meta, piece, sources, target, columns, sems):
    if isinstance(piece, Joined):
        at = 0
        for part in piece.parts:
            load_piece(
                meta, part, sources[: len(part.arrays)], target, slice(at, at + part.count), sems
            )
            sources, at = sources[len(part.arrays) :], at + part.count
        return
    if len(sources) == 1:
        for half_at in range(2):
            pltpu.make_async_copy(
                sources[0].at[half_at, :, piece.columns], target.at[half_at, :, columns],
                sems.at[half_at],
            ).start()
        return
    table = slot_table(piece.order)
    half = len(table) // 2
    block_rows = sources[0].shape[1]
    for slot, (dp_part, tensor_part) in enumerate(table):
        for core in range(2):
            source = sources[2 * core + slot // half]
            place = meta[0] ^ (dp_part ^ core)
            half_at = meta[1] ^ tensor_part
            rows = pl.ds(pl.multiple_of(place * block_rows, TILE_ROWS), block_rows)
            pltpu.make_async_copy(
                source.at[slot % half, :, piece.columns],
                target.at[half_at, rows, columns],
                sems.at[half_at],
            ).start()


def load_flat(meta, piece, sources, target, sem):
    count = piece.count
    if len(sources) == 1:
        for half_at in range(2):
            pltpu.make_async_copy(
                sources[0].at[half_at, :, piece.columns],
                target.at[:, slice(half_at * count, (half_at + 1) * count)], sem,
            ).start()
        return
    table = slot_table(piece.order)
    half = len(table) // 2
    block_rows = sources[0].shape[1]
    for slot, (dp_part, tensor_part) in enumerate(table):
        columns = pl.ds(pl.multiple_of((meta[1] ^ tensor_part) * count, 128), count)
        for core in range(2):
            place = meta[0] ^ (dp_part ^ core)
            rows = pl.ds(pl.multiple_of(place * block_rows, TILE_ROWS), block_rows)
            pltpu.make_async_copy(
                sources[2 * core + slot // half].at[slot % half, :, piece.columns],
                target.at[rows, columns],
                sem,
            ).start()


def await_piece(target, half_at, columns, sems):
    view = target.at[half_at, :, columns]
    pltpu.make_async_copy(view, view, sems.at[half_at]).wait()


def store_flat(meta, source, targets, order, columns, sem):
    count = source.shape[1] // 2
    if len(targets) == 1:
        for half_at in range(2):
            pltpu.make_async_copy(
                source.at[:, slice(half_at * count, (half_at + 1) * count)],
                targets[0].at[half_at, :, columns], sem,
            ).start()
        return
    block_rows = targets[0].shape[1]
    for slot, (dp_part, tensor_part) in enumerate(slot_table(order)):
        mine = pl.ds(pl.multiple_of((meta[1] ^ tensor_part) * count, 128), count)
        for core in range(2):
            place = meta[0] ^ (dp_part ^ core)
            rows = pl.ds(pl.multiple_of(place * block_rows, TILE_ROWS), block_rows)
            pltpu.make_async_copy(
                source.at[rows, mine], targets[core].at[slot, :, columns], sem
            ).start()


def store_piece(meta, source, targets, order, relative_half, columns, sem):
    if len(targets) == 1:
        pltpu.make_async_copy(
            source, targets[0].at[meta[1] ^ relative_half, :, columns], sem
        ).start()
        return
    block_rows = targets[0].shape[1]
    tensor_weight = 2 ** order.index(("tensor", 1))
    for slot, (dp_part, tensor_part) in enumerate(slot_table(order)):
        if tensor_part:
            continue
        for core in range(2):
            place = meta[0] ^ (dp_part ^ core)
            rows = pl.ds(pl.multiple_of(place * block_rows, TILE_ROWS), block_rows)
            pltpu.make_async_copy(
                source.at[rows, :],
                targets[core].at[slot + tensor_weight * relative_half, :, columns],
                sem,
            ).start()


def take(refs, *counts):
    groups, at = [], 0
    for count in counts:
        groups.append(refs[at] if count is None else refs[at : at + count])
        at += 1 if count is None else count
    return groups


def await_stored(source, sem):
    pltpu.make_async_copy(source, source, sem).wait()


def norm_stats(residual):
    centered = residual - jnp.mean(residual, axis=-1, keepdims=True)
    inv_spread = lax.rsqrt(jnp.mean(centered * centered, axis=-1, keepdims=True) + norm_eps)
    return centered * inv_spread, inv_spread


def norm_back(gradient, normed, inv_spread, gain):
    scaled = gradient * gain
    inner = jnp.mean(scaled * normed, axis=-1, keepdims=True)
    return inv_spread * (scaled - jnp.mean(scaled, axis=-1, keepdims=True) - normed * inner)


def row_tiles(row_count):
    tile = min(ROW_TILE, row_count)
    return [slice(start, start + tile) for start in range(0, row_count, tile)]


def column_sum(member):
    return jnp.sum(member, axis=0, keepdims=True)


def gelu_parts(inputs):
    bell = jnp.exp(-0.5 * inputs * inputs)
    ratio = 1.0 / (1.0 + erf_slope * jnp.abs(inputs))
    series = 0.5 * erf_terms[0]
    for term in erf_terms[1:]:
        series = series * ratio + 0.5 * term
    tail = series * ratio * bell
    below = jnp.where(inputs < 0, tail, 1.0 - tail)
    return inputs * below, below + inputs * (bell * inv_root_tau)


def qkv_forward_kernel(pieces, meta, inputs, bias, *refs):
    *sources, (out, weights, sems) = take(refs, *[len(piece.arrays) for piece in pieces], 3)
    step = pl.program_id(0)

    @pl.when(step == 0)
    def _():
        for which, piece in enumerate(pieces):
            load_flat(meta, piece, sources[which], weights.at[which], sems.at[which])

    await_stored(weights.at[step], sems.at[step])
    for rows in row_tiles(inputs.shape[0]):
        out[0, rows, :] = (dot_nn(inputs[rows, :], weights[step]) + bias[0]).astype(jnp.bfloat16)


def slab_features(meta, slab, slab_rows, k_side, q_side):
    segment_rows = slab_rows // 4
    row = lax.broadcasted_iota(jnp.int32, (slab_rows, PAIR), 0)
    lane = lax.broadcasted_iota(jnp.int32, (slab_rows, PAIR), 1) & (HEAD_DIM - 1)
    short = meta[2 + slab] == 0
    segment = jnp.where(short, row // segment_rows, 0)
    offset = row - segment * segment_rows
    base = 2 + meta_slabs(meta) + 4 * slab
    length = jnp.where(
        segment == 0,
        meta[base],
        jnp.where(segment == 1, meta[base + 1], jnp.where(segment == 2, meta[base + 2], meta[base + 3])),
    )
    same = segment == lane
    k_value = jnp.where(lane < 4, jnp.where(same, 1.0, 0.0), jnp.where(offset >= length, 1.0, 0.0))
    q_value = jnp.where(lane < 4, jnp.where(same, 0.0, big_negative), big_negative)
    k_side[slab] = jnp.where(lane < 5, k_value, 0.0).astype(jnp.bfloat16)
    q_side[slab] = jnp.where(lane < 5, q_value, 0.0).astype(jnp.bfloat16)


def meta_slabs(meta):
    return (meta.shape[0] - 2) // 5


def lane_low(row_count):
    return lax.broadcasted_iota(jnp.int32, (row_count, PAIR), 1) < HEAD_DIM


def attention_forward_kernel(meta, qkv, mixed, logsum, k_side, q_side):
    slab, pair = pl.program_id(1), pl.program_id(0)
    slab_rows = qkv.shape[1]

    @pl.when(pair == 0)
    def _():
        slab_features(meta, slab, slab_rows, k_side, q_side)

    low = lane_low(slab_rows)
    query, key = qkv[0].astype(jnp.float32), qkv[1].astype(jnp.float32)
    k_extra, q_extra = k_side[slab].astype(jnp.float32), q_side[slab].astype(jnp.float32)
    value_flip = flipped(qkv[2])
    sub = lax.broadcasted_iota(jnp.int32, (PAIR, slab_rows), 0)
    outcomes = []
    for head in range(2):
        mine = low if head == 0 else jnp.logical_not(low)
        q_head = jnp.where(mine, query, q_extra).astype(jnp.bfloat16)
        k_head = jnp.where(mine, key, k_extra).astype(jnp.bfloat16)
        scores = dot_nt(k_head, q_head)
        top = jnp.max(scores, axis=0, keepdims=True)
        weight = jnp.exp2((scores - top) * exponent_scale).astype(jnp.bfloat16)
        sum_row = HEAD_DIM if head == 0 else 0
        kept = sub < HEAD_DIM if head == 0 else sub >= HEAD_DIM
        v_head = jnp.where(kept, value_flip, jnp.where(sub == sum_row, 1.0, 0.0))
        blend = dot_nn(v_head.astype(jnp.bfloat16), weight)
        total = blend[sum_row : sum_row + 1, :]
        logsum[0, 0, head : head + 1, :] = top * exponent_scale + jnp.log(total) * log2_e
        outcomes.append(blend / total)
    mixed[...] = jnp.where(sub < HEAD_DIM, outcomes[0], outcomes[1]).T.astype(jnp.bfloat16)


def ffn_forward_kernel(pieces, meta, mixed, inputs, vectors, ffn_bias, *refs):
    out_sources, in_sources, down_sources, outputs, scratch = take(
        refs, *[len(piece.arrays) for piece in pieces], 8, 7
    )
    hidden, normed_one, spread_one, activated, slope, result, normed_two, spread_two = outputs
    out_whole, in_whole, down_whole, total, out_sems, in_sems, down_sems = scratch
    step = pl.program_id(0)
    steps = pl.num_programs(0)
    everything = slice(None)
    out_columns = out_whole.shape[2]
    tiles = row_tiles(inputs.shape[0])
    lanes = spread_one.shape[1]

    @pl.when(step == 0)
    def _():
        load_piece(meta, pieces[0], out_sources, out_whole, everything, out_sems)
        load_piece(meta, pieces[1], in_sources, in_whole, everything, in_sems)
        load_piece(meta, pieces[2], down_sources, down_whole, everything, down_sems)
        for half_at in range(2):
            await_piece(out_whole, half_at, everything, out_sems)
        for rows in tiles:
            attention_out = vectors[0:1, :]
            for half_at in range(2):
                columns = slice(half_at * out_columns, (half_at + 1) * out_columns)
                attention_out = attention_out + dot_nt(mixed[rows, columns], out_whole[half_at])
            normed, spread = norm_stats(inputs[rows, :].astype(jnp.float32) + attention_out)
            low = (normed * vectors[2:3, :] + vectors[4:5, :]).astype(jnp.bfloat16)
            hidden[rows, :] = low
            normed_one[rows, :] = normed.astype(jnp.bfloat16)
            spread_one[rows, :] = jnp.broadcast_to(spread, (spread.shape[0], lanes))
            total[rows, :] = low.astype(jnp.float32) + vectors[1:2, :]

    half_at = meta[1] ^ (step // FFN_PARTS)
    width = activated.shape[1]
    part = pl.ds(pl.multiple_of((step % FFN_PARTS) * width, 128), width)

    @pl.when(step % FFN_PARTS == 0)
    def _():
        await_piece(in_whole, half_at, everything, in_sems)
        await_piece(down_whole, half_at, everything, down_sems)

    for rows in tiles:
        pre_gelu = dot_nn(hidden[rows, :], in_whole[half_at, :, part]) + ffn_bias[0]
        value, steep = gelu_parts(pre_gelu)
        low = value.astype(jnp.bfloat16)
        activated[rows, :] = low
        slope[rows, :] = steep.astype(jnp.bfloat16)
        total[rows, :] += dot_nt(low, down_whole[half_at, :, part])

    @pl.when(step == steps - 1)
    def _():
        for rows in tiles:
            normed, spread = norm_stats(total[rows, :])
            result[rows, :] = (normed * vectors[3:4, :] + vectors[5:6, :]).astype(jnp.bfloat16)
            normed_two[rows, :] = normed.astype(jnp.bfloat16)
            spread_two[rows, :] = jnp.broadcast_to(spread, (spread.shape[0], lanes))


def ffn_backward_kernel(
    pieces, orders, target_count, meta, gradient, normed_two, spread_two, hidden, normed_one, spread_one,
    activated, slope, vectors, *refs
):
    in_sources, down_sources, outputs, targets, scratch = take(
        refs, *[len(piece.arrays) for piece in pieces], 4, target_count, 11
    )
    attention_grad, resid_grad, sums, bias_sums = outputs
    (
        in_whole, down_whole, total, branch, branch_flip, hidden_flip, pre_part, grad_parts,
        in_sems, down_sems, out_sems,
    ) = scratch
    step = pl.program_id(0)
    steps = pl.num_programs(0)
    everything = slice(None)
    tiles = row_tiles(hidden.shape[0])
    slot = step % 2

    @pl.when(step == 0)
    def _():
        load_piece(meta, pieces[0], in_sources, in_whole, everything, in_sems)
        load_piece(meta, pieces[1], down_sources, down_whole, everything, down_sems)
        gain_sum, shift_sum, branch_sum = 0.0, 0.0, 0.0
        for rows in tiles:
            grad = gradient[rows, :].astype(jnp.float32)
            normed = normed_two[rows, :].astype(jnp.float32)
            resid = norm_back(grad, normed, spread_two[rows, 0:1], vectors[3:4, :])
            low = resid.astype(jnp.bfloat16)
            total[rows, :] = resid
            branch[rows, :] = low
            branch_flip[:, rows] = flipped(low).astype(jnp.bfloat16)
            hidden_flip[:, rows] = flipped(hidden[rows, :]).astype(jnp.bfloat16)
            gain_sum += column_sum(grad * normed)
            shift_sum += column_sum(grad)
            branch_sum += column_sum(low.astype(jnp.float32))
        sums[...] = jnp.zeros(sums.shape, jnp.float32)
        sums[1:2, :] = branch_sum
        sums[3:4, :] = gain_sum
        sums[5:6, :] = shift_sum

    half_at = meta[1] ^ (step // FFN_PARTS)
    width = activated.shape[1]
    part = pl.ds(pl.multiple_of((step % FFN_PARTS) * width, 128), width)

    @pl.when(step % FFN_PARTS == 0)
    def _():
        await_piece(in_whole, half_at, everything, in_sems)
        await_piece(down_whole, half_at, everything, down_sems)

    @pl.when(step >= 2)
    def _():
        await_stored(grad_parts.at[slot, 0], out_sems.at[slot, 0])
        await_stored(grad_parts.at[slot, 1], out_sems.at[slot, 1])

    grad_parts[slot, 1] = dot_nn(branch_flip[...], activated[...]).astype(jnp.bfloat16)
    down_part = pl.ds(pl.multiple_of(FFN_PARTS * width + (step % FFN_PARTS) * width, 128), width)
    store_piece(
        meta, grad_parts.at[slot, 1], targets, orders[1], step // FFN_PARTS, down_part,
        out_sems.at[slot, 1],
    )
    bias_sum = 0.0
    for rows in tiles:
        active_grad = dot_nn(branch[rows, :], down_whole[half_at, :, part])
        low = (active_grad * slope[rows, :].astype(jnp.float32)).astype(jnp.bfloat16)
        pre_part[rows, :] = low
        bias_sum += column_sum(low.astype(jnp.float32))
        total[rows, :] += dot_nt(low, in_whole[half_at, :, part])
    bias_sums[0] = bias_sum
    grad_parts[slot, 0] = dot_nn(hidden_flip[...], pre_part[...]).astype(jnp.bfloat16)
    store_piece(
        meta, grad_parts.at[slot, 0], targets, orders[0], step // FFN_PARTS, part,
        out_sems.at[slot, 0],
    )

    @pl.when(step == steps - 1)
    def _():
        gain_sum, shift_sum, branch_sum = 0.0, 0.0, 0.0
        for rows in tiles:
            grad = total[rows, :]
            normed = normed_one[rows, :].astype(jnp.float32)
            resid = norm_back(grad, normed, spread_one[rows, 0:1], vectors[2:3, :])
            low = resid.astype(jnp.bfloat16)
            resid_grad[rows, :] = resid
            attention_grad[rows, :] = low
            gain_sum += column_sum(grad * normed)
            shift_sum += column_sum(grad)
            branch_sum += column_sum(low.astype(jnp.float32))
        sums[0:1, :] = branch_sum
        sums[2:3, :] = gain_sum
        sums[4:5, :] = shift_sum
        for late in range(2):
            await_stored(grad_parts.at[late, 0], out_sems.at[late, 0])
            await_stored(grad_parts.at[late, 1], out_sems.at[late, 1])


def out_backward_kernel(pieces, order, target_count, meta, attention_grad, mixed, *refs):
    sources, mixed_grad, targets, scratch = take(
        refs, len(pieces[0].arrays), None, target_count, 5
    )
    out_whole, grad_flip, grad_part, load_sem, out_sem = scratch
    tiles = row_tiles(mixed.shape[0])
    load_flat(meta, pieces[0], sources, out_whole, load_sem)
    for rows in tiles:
        grad_flip[:, rows] = flipped(attention_grad[rows, :]).astype(jnp.bfloat16)
    grad_part[...] = dot_nn(grad_flip[...], mixed[...]).astype(jnp.bfloat16)
    store_flat(meta, grad_part, targets, order, slice(None), out_sem)
    await_stored(out_whole, load_sem)
    for rows in tiles:
        mixed_grad[rows, :] = dot_nn(attention_grad[rows, :], out_whole[...]).astype(jnp.bfloat16)
    await_stored(grad_part, out_sem)


def attention_backward_kernel(meta, qkv, mixed, mixed_grad, logsum, grads, sums, k_side, q_side):
    slab, pair = pl.program_id(1), pl.program_id(0)
    slab_rows = qkv.shape[1]

    @pl.when(pair == 0)
    def _():
        slab_features(meta, slab, slab_rows, k_side, q_side)

    low = lane_low(slab_rows)
    query, key, value = (qkv[place].astype(jnp.float32) for place in range(3))
    k_extra, q_extra = k_side[slab].astype(jnp.float32), q_side[slab].astype(jnp.float32)
    grad_low = mixed_grad[...]
    grad = grad_low.astype(jnp.float32)
    product = (grad * mixed[...].astype(jnp.float32)).T
    key_flip = key.T
    sub = lax.broadcasted_iota(jnp.int32, (PAIR, slab_rows), 0)
    query_flip, key_grad, value_grad = 0.0, 0.0, 0.0
    for head in range(2):
        mine = low if head == 0 else jnp.logical_not(low)
        kept = sub < HEAD_DIM if head == 0 else sub >= HEAD_DIM
        span = slice(head * HEAD_DIM, (head + 1) * HEAD_DIM)
        q_head = jnp.where(mine, query, q_extra).astype(jnp.bfloat16)
        k_head = jnp.where(mine, key, k_extra).astype(jnp.bfloat16)
        v_head = jnp.where(mine, value, 0.0).astype(jnp.bfloat16)
        probs = jnp.exp2(
            dot_nt(k_head, q_head) * exponent_scale - logsum[0, 0, head : head + 1, :]
        )
        delta = column_sum(product[span, :])
        raw_grad = (probs * (dot_nt(v_head, grad_low) - delta)).astype(jnp.bfloat16)
        g_head = jnp.where(mine, grad, 0.0).astype(jnp.bfloat16)
        value_grad += dot_nn(probs.astype(jnp.bfloat16), g_head)
        key_grad += dot_nn(raw_grad, jnp.where(mine, query, 0.0).astype(jnp.bfloat16))
        query_flip += dot_nn(jnp.where(kept, key_flip, 0.0).astype(jnp.bfloat16), raw_grad)
    query_low = (query_flip * score_scale).T.astype(jnp.bfloat16)
    value_low = value_grad.astype(jnp.bfloat16)
    grads[0] = query_low
    grads[1] = (key_grad * score_scale).astype(jnp.bfloat16)
    grads[2] = value_low

    @pl.when(slab == 0)
    def _():
        sums[...] = jnp.zeros(sums.shape, jnp.float32)

    sums[0:1, :] += column_sum(query_low.astype(jnp.float32))
    sums[1:2, :] += column_sum(value_low.astype(jnp.float32))


def qkv_grad_kernel(orders, target_count, meta, inputs, grads, *refs):
    targets, (inputs_flip, grad_parts, out_sems) = take(refs, target_count, 3)
    step = pl.program_id(0)
    columns = grads.shape[2] // 2

    @pl.when(step == 0)
    def _():
        for rows in row_tiles(inputs.shape[0]):
            inputs_flip[:, rows] = flipped(inputs[rows, :]).astype(jnp.bfloat16)

    grad_parts[step] = dot_nn(inputs_flip[...], grads[0]).astype(jnp.bfloat16)
    for which, order in enumerate((orders[0], orders[1], orders[1])):

        @pl.when(step == which)
        def _():
            span = slice(which * columns, (which + 1) * columns)
            store_flat(meta, grad_parts.at[which], targets, order, span, out_sems.at[which])

    @pl.when(step == 2)
    def _():
        for which in range(3):
            await_stored(grad_parts.at[which], out_sems.at[which])


def input_grad_kernel(pieces, meta, grads, resid_grad, *refs):
    *sources, outputs, (weights, sems) = take(
        refs, *[len(piece.arrays) for piece in pieces], len(refs) - 2 - sum(
            len(piece.arrays) for piece in pieces
        ), 2,
    )
    input_grad = outputs[0]
    step = pl.program_id(0)
    tiles = row_tiles(resid_grad.shape[0])

    @pl.when(step == 0)
    def _():
        for which, piece in enumerate(pieces):
            load_flat(meta, piece, sources[which], weights.at[which], sems.at[which])
        for rows in tiles:
            input_grad[rows, :] = resid_grad[rows, :]

    await_stored(weights.at[step], sems.at[step])
    for rows in tiles:
        input_grad[rows, :] += dot_nt(grads[0, rows, :], weights[step])

    if len(outputs) > 1:

        @pl.when(step == 2)
        def _():
            outputs[1][...] = input_grad[...].astype(jnp.bfloat16)


def fixed(shape):
    return pl.BlockSpec(
        shape, lambda *_: (0,) * len(shape), pipeline_mode=pl.Buffered(1)
    )


def fixed_out(shape):
    return pl.BlockSpec(shape, lambda *_: (0,) * len(shape))


ANYWHERE = pl.BlockSpec(memory_space=pl.ANY)


def run_kernel(kernel, meta, grid, ins, outs, scratch, flops, moved, name, after=()):
    used = len(ins)
    ins = list(ins) + [(ANYWHERE, member) for member in after]
    in_specs, operands = zip(*ins)
    out_specs, out_shapes = zip(*outs)

    def body(meta_ref, *refs):
        kernel(meta_ref, *refs[:used], *refs[len(ins) :])

    return pl.pallas_call(
        body,
        grid_spec=pltpu.PrefetchScalarGridSpec(
            num_scalar_prefetch=1,
            grid=grid,
            in_specs=list(in_specs),
            out_specs=list(out_specs),
            scratch_shapes=scratch,
        ),
        out_shape=list(out_shapes),
        compiler_params=pltpu.CompilerParams(vmem_limit_bytes=VMEM_LIMIT),
        cost_estimate=pl.CostEstimate(flops=(BACK_WEIGHT if "forward" not in name else COST_WEIGHT) * flops, bytes_accessed=moved, transcendentals=0),
        name=name,
    )(meta, *operands)


def low_shape(*shape):
    return jax.ShapeDtypeStruct(shape, jnp.bfloat16)


def full_shape(*shape):
    return jax.ShapeDtypeStruct(shape, jnp.float32)


def pair_sems():
    return pltpu.SemaphoreType.DMA((2,))


def half_of(step, meta, count):
    return meta[1] ^ (step // count)


def sources_of(pieces):
    return [(ANYWHERE, member) for piece in pieces for member in piece.arrays]


def targets_of(routed, split, width, block_rows, columns):
    if routed:
        shape = low_shape(split * width // (2 * block_rows), block_rows, columns)
        return [(ANYWHERE, shape), (ANYWHERE, shape)]
    return [(ANYWHERE, low_shape(split, width, columns))]


def three_sems():
    return pltpu.SemaphoreType.DMA((3,))


def qkv_forward(meta, inputs, bias, pieces, after=()):
    rows, width = inputs.shape
    (qkv,) = run_kernel(
        functools.partial(qkv_forward_kernel, pieces),
        meta,
        (3,),
        [
            (fixed((rows, width)), inputs),
            (pl.BlockSpec((1, 1, width), lambda i, m: (i, 0, 0)), bias),
        ]
        + sources_of(pieces),
        [(pl.BlockSpec((1, rows, width), lambda i, m: (i, 0, 0)), low_shape(3, rows, width))],
        [pltpu.VMEM((3, width, width), jnp.bfloat16), three_sems()],
        6 * rows * width * width,
        8 * rows * width + 6 * width * width,
        "qkv_forward",
        after,
    )
    return qkv


def attention_forward(meta, qkv, slab_count, after=()):
    _, rows, width = qkv.shape
    slab_rows = rows // slab_count
    pairs = width // PAIR
    return run_kernel(
        attention_forward_kernel,
        meta,
        (pairs, slab_count),
        [(pl.BlockSpec((3, slab_rows, PAIR), lambda p, s, m: (0, s, p)), qkv)],
        [
            (pl.BlockSpec((slab_rows, PAIR), lambda p, s, m: (s, p)), low_shape(rows, width)),
            (
                pl.BlockSpec((1, 1, 8, slab_rows), lambda p, s, m: (s, p, 0, 0)),
                full_shape(slab_count, pairs, 8, slab_rows),
            ),
        ],
        [pltpu.VMEM((slab_count, slab_rows, PAIR), jnp.bfloat16)] * 2,
        16 * rows * slab_rows * width,
        8 * rows * width,
        "attention_forward",
        after,
    )


def ffn_forward(meta, mixed, inputs, vectors, ffn_bias, pieces, after=()):
    rows, width = inputs.shape
    half_width = pieces[1].count
    part = half_width // FFN_PARTS

    def part_at(i, m):
        return half_of(i, m, FFN_PARTS) * FFN_PARTS + i % FFN_PARTS

    whole_rows = (fixed_out((rows, width)), low_shape(rows, width))
    spread = (fixed_out((rows, 128)), full_shape(rows, 128))
    inner = (
        pl.BlockSpec((rows, part), lambda i, m: (0, part_at(i, m))),
        low_shape(rows, 2 * half_width),
    )
    return run_kernel(
        functools.partial(ffn_forward_kernel, pieces),
        meta,
        (2 * FFN_PARTS,),
        [
            (fixed((rows, width)), mixed),
            (fixed((rows, width)), inputs),
            (fixed((8, width)), vectors),
            (pl.BlockSpec((1, 1, part), lambda i, m: (part_at(i, m), 0, 0)), ffn_bias),
        ]
        + sources_of(pieces),
        [whole_rows, whole_rows, spread, inner, inner, whole_rows, whole_rows, spread],
        [
            pltpu.VMEM((2, width, width // 2), jnp.bfloat16),
            pltpu.VMEM((2, width, half_width), jnp.bfloat16),
            pltpu.VMEM((2, width, half_width), jnp.bfloat16),
            pltpu.VMEM((rows, width), jnp.float32),
            pair_sems(),
            pair_sems(),
            pair_sems(),
        ],
        8 * rows * width * half_width,
        24 * rows * width + 8 * width * half_width,
        "ffn_forward",
        after,
    )


def ffn_backward(meta, gradient, kept, vectors, pieces, orders, targets, after=()):
    hidden, normed_one, spread_one, activated, slope, normed_two, spread_two = kept
    rows, width = hidden.shape
    half_width = pieces[0].count
    part = half_width // FFN_PARTS

    def part_at(i, m):
        return half_of(i, m, FFN_PARTS) * FFN_PARTS + i % FFN_PARTS

    low_rows = fixed((rows, width))
    spread = fixed((rows, 128))
    inner = pl.BlockSpec((rows, part), lambda i, m: (0, part_at(i, m)))
    return run_kernel(
        functools.partial(ffn_backward_kernel, pieces, orders, len(targets)),
        meta,
        (2 * FFN_PARTS,),
        [
            (low_rows, gradient),
            (low_rows, normed_two),
            (spread, spread_two),
            (low_rows, hidden),
            (low_rows, normed_one),
            (spread, spread_one),
            (inner, activated),
            (inner, slope),
            (fixed((8, width)), vectors),
        ]
        + sources_of(pieces),
        [
            (fixed_out((rows, width)), low_shape(rows, width)),
            (fixed_out((rows, width)), full_shape(rows, width)),
            (fixed_out((8, width)), full_shape(8, width)),
            (
                pl.BlockSpec((1, 1, part), lambda i, m: (part_at(i, m), 0, 0)),
                full_shape(2 * FFN_PARTS, 1, part),
            ),
        ]
        + targets,
        [
            pltpu.VMEM((2, width, half_width), jnp.bfloat16),
            pltpu.VMEM((2, width, half_width), jnp.bfloat16),
            pltpu.VMEM((rows, width), jnp.float32),
            pltpu.VMEM((rows, width), jnp.bfloat16),
            pltpu.VMEM((width, rows), jnp.bfloat16),
            pltpu.VMEM((width, rows), jnp.bfloat16),
            pltpu.VMEM((rows, part), jnp.bfloat16),
            pltpu.VMEM((2, 2, width, part), jnp.bfloat16),
            pair_sems(),
            pair_sems(),
            pltpu.SemaphoreType.DMA((2, 2)),
        ],
        16 * rows * width * half_width,
        40 * rows * width + 16 * width * half_width,
        "ffn_backward",
        after,
    )


def out_backward(meta, attention_grad, mixed, piece, order, targets, after=()):
    rows, width = mixed.shape
    return run_kernel(
        functools.partial(out_backward_kernel, [piece], order, len(targets)),
        meta,
        (1,),
        [(fixed((rows, width)), attention_grad), (fixed((rows, width)), mixed)]
        + sources_of([piece]),
        [(fixed_out((rows, width)), low_shape(rows, width))] + targets,
        [
            pltpu.VMEM((width, width), jnp.bfloat16),
            pltpu.VMEM((width, rows), jnp.bfloat16),
            pltpu.VMEM((width, width), jnp.bfloat16),
            pltpu.SemaphoreType.DMA,
            pltpu.SemaphoreType.DMA,
        ],
        4 * rows * width * width,
        6 * rows * width + 4 * width * width,
        "out_backward",
        after,
    )


def attention_backward(meta, qkv, mixed, mixed_grad, logsum, slab_count, after=()):
    _, rows, width = qkv.shape
    slab_rows = rows // slab_count
    pairs = width // PAIR
    three = pl.BlockSpec((3, slab_rows, PAIR), lambda p, s, m: (0, s, p))
    one = pl.BlockSpec((slab_rows, PAIR), lambda p, s, m: (s, p))
    return run_kernel(
        attention_backward_kernel,
        meta,
        (pairs, slab_count),
        [
            (three, qkv),
            (one, mixed),
            (one, mixed_grad),
            (pl.BlockSpec((1, 1, 8, slab_rows), lambda p, s, m: (s, p, 0, 0)), logsum),
        ],
        [
            (three, low_shape(3, rows, width)),
            (pl.BlockSpec((8, PAIR), lambda p, s, m: (0, p)), full_shape(8, width)),
        ],
        [pltpu.VMEM((slab_count, slab_rows, PAIR), jnp.bfloat16)] * 2,
        40 * rows * slab_rows * width,
        16 * rows * width,
        "attention_backward",
        after,
    )


def qkv_grad(meta, inputs, grads, orders, targets, after=()):
    rows, width = inputs.shape
    return run_kernel(
        functools.partial(qkv_grad_kernel, orders, len(targets)),
        meta,
        (3,),
        [
            (fixed((rows, width)), inputs),
            (pl.BlockSpec((1, rows, width), lambda i, m: (i, 0, 0)), grads),
        ],
        targets,
        [
            pltpu.VMEM((width, rows), jnp.bfloat16),
            pltpu.VMEM((3, width, width), jnp.bfloat16),
            three_sems(),
        ],
        6 * rows * width * width,
        8 * rows * width + 6 * width * width,
        "qkv_grad",
        after,
    )


def input_gradient(meta, grads, resid_grad, pieces, after=(), low=False):
    rows, width = resid_grad.shape
    outs = [(fixed_out((rows, width)), full_shape(rows, width))]
    if low:
        outs.append((fixed_out((rows, width)), low_shape(rows, width)))
    return run_kernel(
        functools.partial(input_grad_kernel, pieces),
        meta,
        (3,),
        [
            (pl.BlockSpec((1, rows, width), lambda i, m: (i, 0, 0)), grads),
            (fixed((rows, width)), resid_grad),
        ]
        + sources_of(pieces),
        outs,
        [pltpu.VMEM((3, width, width), jnp.bfloat16), three_sems()],
        6 * rows * width * width,
        14 * rows * width + 6 * width * width,
        "input_gradient",
        after,
    )


def both_halves(mine, theirs, place):
    first = jnp.concatenate([mine, theirs], axis=0)
    second = jnp.concatenate([theirs, mine], axis=0)
    return jnp.where(place == 0, first, second)


def on_device(
    tokens,
    cotangent,
    buckets,
    lengths,
    qkv_weight,
    qv_bias,
    out_weight,
    ffn_in_weight,
    ffn_in_bias,
    ffn_out_weight,
    out_bias,
    norm_gain,
    norm_bias,
):
    split = lax.axis_size("tensor")
    dp_size = lax.axis_size("dp")
    place = lax.axis_index("tensor")
    width = tokens.shape[1]
    rows = tokens.shape[0] // split
    slabs = buckets.shape[0] // split
    layer_count = qkv_weight.shape[0]
    block_rows = width // dp_size
    routed = block_rows % TILE_ROWS == 0 and dp_size & (dp_size - 1) == 0
    orders = hop_orders(dp_size if routed else PLANNED_BLOCKS)

    own_tokens = lax.dynamic_slice_in_dim(tokens, place * rows, rows)
    own_cotangent = lax.dynamic_slice_in_dim(cotangent, place * rows, rows)
    own_buckets = lax.dynamic_slice_in_dim(buckets, place * slabs, slabs)
    own_lengths = lax.dynamic_slice_in_dim(lengths, place * slabs, slabs)
    if routed:
        position = jnp.stack([lax.axis_index("dp"), place]).astype(jnp.int32)
    else:
        position = jnp.zeros((2,), jnp.int32)
    meta = jnp.concatenate([position, own_buckets, own_lengths.reshape(-1)])

    bias_flat = jnp.concatenate([qv_bias.reshape(layer_count, -1), ffn_in_bias], axis=1)
    bias_other = hop(bias_flat, ("tensor", 1))
    bias_halves = jnp.where(
        place == 0, jnp.stack([bias_flat, bias_other]), jnp.stack([bias_other, bias_flat])
    )
    qv_columns = qv_bias.shape[2]
    ffn_columns = ffn_in_bias.shape[1]

    def small_inputs(index):
        halves = bias_halves[:, index]
        value = halves[:, : 2 * qv_columns].reshape(2, 2, qv_columns)
        zero = jnp.zeros((2, qv_columns), jnp.float32)
        bias = jnp.stack([value[:, 0], zero, value[:, 1]]).reshape(3, 1, -1)
        vectors = jnp.concatenate(
            [out_bias[index], norm_gain[index], norm_bias[index], jnp.zeros((2, width), jnp.float32)]
        )
        return bias, vectors, halves[:, 2 * qv_columns :].reshape(2 * FFN_PARTS, 1, -1)

    def gathering(flag, *members):
        shard = jnp.concatenate(members, axis=1)
        return (Gathering if flag else WholeGathering)(shard, orders)

    def attention_split(pieces):
        half = width // 2
        query_key, value_out = pieces
        qkv = [query_key.narrow(0, half), query_key.narrow(half, half), value_out.narrow(0, half)]
        return qkv, value_out.narrow(half, half)

    hops_back = [[routed and flag for flag in flags] for flags in HOPS_BACK]

    def waits(flag, members):
        return list(members) if flag else []

    first = gathering(routed, *qkv_weight[0], out_weight[0])
    first_ffn = gathering(False, ffn_in_weight[0], ffn_out_weight[0])
    second = gathering(routed, *qkv_weight[1], out_weight[1])
    if SPLIT_DOWN:
        second_in = gathering(False, ffn_in_weight[1])
        second_down = gathering(routed, ffn_out_weight[1])
    else:
        second_in = gathering(False, ffn_in_weight[1], ffn_out_weight[1])
        second_down = second_in
    first.send_far()
    first.land_far()
    first.send_middle()
    first.land_middle()
    last = first.send_last()
    first.send_core()
    second.send_far(*waits(routed, last))
    bias, vectors, ffn_bias = small_inputs(0)
    qkv_pieces, out_piece = attention_split(first.pieces())
    qkv = qkv_forward(meta, own_tokens, bias, qkv_pieces)
    second.land_far(qkv)
    second.send_middle(qkv)
    mixed, logsum = attention_forward(meta, qkv, slabs)
    second.land_middle(mixed)
    second_last = second.send_last(mixed)
    if SPLIT_DOWN:
        second_down.send_far(mixed)
    first_pieces = (qkv_pieces, out_piece, first_ffn.pieces())
    out = ffn_forward(
        meta, mixed, own_tokens, vectors, ffn_bias, [out_piece] + first_pieces[2]
    )
    kept_layers = [(own_tokens, qkv, mixed, logsum, vectors, out)]
    layer_one = out[5]
    second.send_core(layer_one)
    if SPLIT_DOWN:
        second_down.land_far(layer_one)
        second_down.send_middle(layer_one)
    bias, vectors, ffn_bias = small_inputs(1)
    qkv_pieces, out_piece = attention_split(second.pieces())
    qkv = qkv_forward(meta, layer_one, bias, qkv_pieces, waits(routed, second_last))
    if SPLIT_DOWN:
        second_down.land_middle(qkv)
        second_down.send_last(qkv)
    mixed, logsum = attention_forward(meta, qkv, slabs)
    if SPLIT_DOWN:
        second_down.send_core(mixed)
        ffn_pieces = [Joined(second_in.pieces()), Joined(second_down.pieces())]
    else:
        ffn_pieces = second_in.pieces()
    one_other = hop(tied(layer_one, [mixed]), ("tensor", 1))
    second_pieces = (qkv_pieces, out_piece, ffn_pieces)
    out = ffn_forward(
        meta, mixed, layer_one, vectors, ffn_bias, [out_piece] + second_pieces[2]
    )
    kept_layers.append((layer_one, qkv, mixed, logsum, vectors, out))
    layer_two = out[5]
    two_other = hop(layer_two, ("tensor", 1))
    layer_one_whole = both_halves(layer_one, tied(one_other, [layer_two]), place)

    def targets(flag, columns):
        return targets_of(flag, split, width, block_rows, columns)

    def scattering(flag, members, sides):
        kind = Scattering if flag else WholeScattering
        return kind(members, orders, sides)

    half_ffn = ffn_in_weight.shape[2]

    def ffn_back(index, gradient, pieces, after=()):
        inputs, qkv, mixed, logsum, vectors, out = kept_layers[index]
        hidden, normed_one, spread_one, activated, slope, _, normed_two, spread_two = out
        kept = (hidden, normed_one, spread_one, activated, slope, normed_two, spread_two)
        attention_grad, resid_grad, sums, ffn_sums, *members = ffn_backward(
            meta, gradient, kept, vectors, pieces[2], orders, targets(hops_back[index][1], 2 * half_ffn), after
        )
        scatter = scattering(
            hops_back[index][1], [members], [[(0, 0, half_ffn)], [(0, half_ffn, 2 * half_ffn)]]
        )
        return attention_grad, resid_grad, (sums, ffn_sums), scatter

    def out_back(index, attention_grad, pieces, after=()):
        mixed = kept_layers[index][2]
        return out_backward(
            meta, attention_grad, mixed, pieces[1], orders[0], targets(hops_back[index][0], width // 2), after
        )

    def attention_back(index, mixed_grad, after=()):
        _, qkv, mixed, logsum, _, _ = kept_layers[index]
        return attention_backward(meta, qkv, mixed, mixed_grad, logsum, slabs, after)

    def qkv_grads(index, grads, out_members, after=()):
        members = qkv_grad(
            meta, kept_layers[index][0], grads, orders,
            targets(hops_back[index][0], 3 * width // 2), after,
        )
        columns = width // 2
        return scattering(
            hops_back[index][0],
            [out_members, members],
            [[(0, 0, columns), (1, 0, columns)], [(1, columns, 3 * columns)]],
        )

    def flat_smalls(sums, ffn_sums, qkv_sums):
        return jnp.concatenate(
            [sums[:6].reshape(-1), qkv_sums[:2].reshape(-1), ffn_sums.reshape(-1)]
        )

    attention_grad, resid_grad, sums, ffn_one = ffn_back(1, own_cotangent, second_pieces, [one_other])
    layer_two_whole = both_halves(layer_two, tied(two_other, [attention_grad]), place)
    ffn_one.send_core()
    mixed_grad, *out_members = out_back(1, attention_grad, second_pieces, [two_other])
    ffn_one.land_core(mixed_grad)
    ffn_one.send_last(mixed_grad)
    grads, qkv_sums = attention_back(1, mixed_grad)
    ffn_one.land(grads)
    smalls_one = flat_smalls(*sums, qkv_sums)
    attention_one = qkv_grads(1, grads, out_members)
    begun = attention_one.begun
    one_core = attention_one.send_core()
    ffn_one.send_middle(*begun)
    (gradient,) = input_gradient(meta, grads, resid_grad, second_pieces[0], begun)
    attention_one.land_core(gradient)
    ffn_one.land(gradient)
    one_last = attention_one.send_last(gradient)
    ffn_one.send_far(gradient)
    attention_grad, resid_grad, sums, ffn_zero = ffn_back(
        0, gradient, first_pieces, waits(hops_back[1][0], one_core)
    )
    attention_one.land(attention_grad)
    ffn_one.land_far(attention_grad)
    one_middle = attention_one.send_middle(attention_grad)
    zero_core = ffn_zero.send_core(attention_grad)
    mixed_grad, *out_members = out_back(
        0, attention_grad, first_pieces, waits(hops_back[1][0], one_last)
    )
    ffn_zero.land_core(mixed_grad)
    attention_one.land(mixed_grad)
    ffn_last = ffn_zero.send_last(mixed_grad)
    one_far = attention_one.send_far(mixed_grad)
    grads, qkv_sums = attention_back(0, mixed_grad, waits(routed, one_middle + zero_core))
    ffn_zero.land(grads)
    attention_one.land_far(grads)
    smalls_zero = flat_smalls(*sums, qkv_sums)
    totals = Totals(jnp.stack([smalls_zero, smalls_one]), routed)
    totals.send("dp", 1, 4, grads)
    zero_middle = ffn_zero.send_middle(grads)
    attention_zero = qkv_grads(0, grads, out_members, waits(routed, one_far))
    begun = attention_zero.begun
    totals.land(*begun)
    totals.send("dp", 4, dp_size // 4, *begun)
    attention_zero.send_core(*begun)
    gradient, token_low = input_gradient(
        meta, grads, resid_grad, first_pieces[0], begun, True
    )
    totals.land(gradient)
    attention_zero.land_core(gradient)
    zero_last = attention_zero.send_last(gradient)
    ffn_zero.land(gradient)
    ffn_zero.send_far(gradient)
    if HOLD_TOKENS:
        token_low = tied(token_low, waits(routed, zero_last))
    token_other = hop(token_low, ("tensor", 1))
    totals.send("tensor", 1, 2, gradient, *waits(routed, zero_last))
    attention_zero.land(gradient)
    zero_middle = attention_zero.send_middle(gradient)
    totals.land(gradient, *waits(routed, zero_middle))
    smalls = totals.total
    ffn_zero.land_far(gradient, *waits(routed, zero_middle))
    attention_zero.land(gradient)
    attention_zero.send_far(gradient)
    attention_zero.land_far(gradient)
    token_grad = both_halves(gradient, token_other.astype(jnp.float32), place)
    matrix_grads = []
    for attention, ffn in ((attention_zero, ffn_zero), (attention_one, ffn_one)):
        out_part, *qkv_parts = jnp.split(attention.result, 4, axis=1)
        matrix_grads.append((jnp.stack(qkv_parts), out_part, *jnp.split(ffn.result, 2, axis=1)))
    eight = smalls[:, : 8 * width].reshape(layer_count, 4, 2, width)
    ffn_total = smalls[:, 8 * width :]
    return (
        layer_one_whole,
        layer_two_whole,
        token_grad,
        jnp.stack([member[0] for member in matrix_grads]),
        lax.dynamic_slice_in_dim(eight[:, 3], place * qv_columns, qv_columns, axis=2),
        jnp.stack([member[1] for member in matrix_grads]),
        jnp.stack([member[2] for member in matrix_grads]),
        lax.dynamic_slice_in_dim(ffn_total, place * ffn_columns, ffn_columns, axis=1),
        jnp.stack([member[3] for member in matrix_grads]),
        eight[:, 0],
        eight[:, 1],
        eight[:, 2],
    )


def solution(mesh):
    placed = (
        P("dp", None),
        P("dp", None),
        P("dp"),
        P("dp", None),
        P(None, None, "dp", "tensor"),
        P(None, None, "tensor"),
        P(None, "dp", "tensor"),
        P(None, "dp", "tensor"),
        P(None, "tensor"),
        P(None, "dp", "tensor"),
        P(),
        P(),
        P(),
    )
    return jax.shard_map(
        on_device,
        mesh=mesh,
        in_specs=placed,
        out_specs=(
            P("dp", None),
            P("dp", None),
            P("dp", None),
            P(None, None, "dp", "tensor"),
            P(None, None, "tensor"),
            P(None, "dp", "tensor"),
            P(None, "dp", "tensor"),
            P(None, "tensor"),
            P(None, "dp", "tensor"),
            P(),
            P(),
            P(),
        ),
        check_vma=False,
    )
```
